32 devices in a mesh: grp: 4 (over y, x), dev: 8 (over z, core).
Axes of the slice: x: 2, y: 2, z: 4, core: 2. Of those that a mesh axis runs over, the one named last changes fastest.
Arguments:
- counts: bfloat16 [768, 64, 4096], P(('grp', 'dev')), may hold values from 0.099609375 to 10
- src_factor: bfloat16 [8192, 256], P(('grp', 'dev')), may hold values from -0.5 to 0.5
- dst_factor: bfloat16 [2048, 256], P('dev'), may hold values from -0.5 to 0.5
- hour_factor: bfloat16 [4096, 256], replicated, may hold values from -0.5 to 0.5
- src_owner: int32 [768, 1], P(('grp', 'dev')), may hold values from 0 to 7; in each aligned block of 24 rows (0 to 23, 24 to 47, ...) at most 4 rows name the same one
- src_slot: int32 [768], P(('grp', 'dev')), may hold values from 0 to 3
- dst_owner: int32 [768, 1], P(('grp', 'dev')), may hold values from 0 to 7; in each aligned block of 24 rows (0 to 23, 24 to 47, ...) at most 4 rows name the same one
- dst_slot: int32 [768], P(('grp', 'dev')), may hold values from 0 to 3
- hour_block: int32 [768], P(('grp', 'dev')), may hold values from 0 to 63
Outputs:
- grad_src: float32 [8192, 256], P(('grp', 'dev'))
- grad_dst: float32 [2048, 256], P('dev')
- grad_hour: float32 [4096, 256], replicated
The draws below stay inside these ranges and needn't reach their ends.
Inputs may be any that keep to these rules, and one draw needn't show every extreme that they name: `src_owner`: among the 24 rows of one device no owner is named more than 4 times; in every draw some device names some owner exactly 4 times. `dst_owner`: among the 24 rows of one device no owner is named more than 4 times; in every draw some device names some owner exactly 4 times.
All inputs are finite; a program needn't handle non-finite values.
Results may differ from the reference program's by a relative error of at most 0.003.
Values may be sent and summed in bfloat16 or wider, within the bound.
No kernel may reach another device: no remote copies, remote signals or barrier semaphores. Data moves between devices by JAX's collectives and lax.ppermute only.
A program may use at most 128 MiB of HBM per device.

```python
import math
import jax
import jax.numpy as jnp
import numpy as np
from jax import lax

BS = 64
R = 256
NB = 24
SRC_DEV = 4
DST_DEV = 4
HB = 64
CAP = 4
TOT_BLK = 768
SRC_ROWS = 8192
DST_ROWS = 2048
HOURS = 4096
N_DEV = 8


def place_ends(entries, own_key, smallest, largest):
    place = [jax.random.randint(jax.random.fold_in(own_key, axis), (), 0, length) for axis, length in enumerate(entries.shape)]
    widest = entries.shape.index(max(entries.shape))
    neighbour = place[:widest] + [(place[widest] + 1) % entries.shape[widest]] + place[widest + 1:]
    return entries.at[tuple(place)].set(smallest).at[tuple(neighbour)].set(largest)


def levels(own_key, shape, shards, smallest, top_value):
    level, own = 1.0, jax.random.fold_in(own_key, 6)
    for dim, shards_of in shards:
        steps = jnp.exp(jax.random.uniform(jax.random.fold_in(own, dim), (shards_of,), jnp.float32, smallest / len(shards), top_value / len(shards)))
        level = level * jnp.repeat(steps, shape[dim] // shards_of).reshape([-1 if axis == dim else 1 for axis in range(len(shape))])
    return level


def shared_out(key, own, number, rows, amount, top, most, skew):
    sequence = jax.random.permutation(key, amount)
    crowded, usual = load_shares(amount, rows * top, most, skew, True), load_shares(amount, rows * top, most, skew, False)
    places = jnp.arange(amount)

    def named(tallies, offset_by):
        used = int((tallies > 0).sum())
        fixed = max(1, used // 4)
        moved = fixed + (places - fixed + offset_by * (used - fixed)) % max(1, amount - fixed)
        return jnp.zeros((amount,), jnp.int32).at[sequence[jnp.where(places < fixed, places, moved)]].set(jnp.asarray(tallies, jnp.int32))

    tallies = jnp.where(number % 4 == 0, named(crowded, number // 4), named(usual, number - number // 4 - 1))
    mixed = jax.random.permutation(jax.random.fold_in(own, 3), amount)
    giver, taker = mixed[0:amount // 2 * 2:2], mixed[1:amount // 2 * 2:2]
    slack = jnp.minimum(tallies[giver] - 1, most - tallies[taker]) // 2
    slack = jnp.where((giver == sequence[0]) | (taker == sequence[0]) | (tallies[taker] == 0), 0, jnp.maximum(slack, 0))
    moved = jax.random.randint(jax.random.fold_in(own, 4), (amount // 2,), 0, 1 << 20) % (slack + 1)
    tallies = tallies.at[giver].add(-moved).at[taker].add(moved)
    items = jnp.searchsorted(jnp.cumsum(tallies), jnp.arange(rows * top), side="right").astype(jnp.int32)
    listing = items.reshape(top, rows).T
    listing = listing[jax.random.permutation(jax.random.fold_in(own, 1), rows)]
    offset_by = jax.random.randint(jax.random.fold_in(own, 2), (rows, 1), 0, top)
    return jnp.take_along_axis(listing, (jnp.arange(top)[None, :] + offset_by) % top, axis=1)


def load_shares(count, total, reach, slope, full):
    weights = [(1 << 20) // math.isqrt(rank ** slope) + 1 for rank in range(1, count + 1)]
    largest = reach if full else min(reach, max(-(-total // count), total * weights[0] // sum(weights)))
    least = 1 if total - largest >= count - 1 else 0
    given, rest = [largest] + [least] * (count - 1), total - largest - least * (count - 1)
    while rest > 0:
        movable = [i for i in range(1, count) if given[i] < largest] or [i for i in range(1, count) if given[i] < reach]
        mass, remaining = sum([weights[i] for i in movable]), rest
        for i in movable:
            addition = min(reach - given[i], max(1, remaining * weights[i] // mass), rest)
            given[i] = given[i] + addition
            rest = rest - addition
    return np.array(given)


def setup_inputs(seed: int = 0) -> dict:
    arg_keys = jax.random.split(jax.random.key(seed), 10)
    counts = jnp.clip(jnp.exp(math.log(10.0) - 4.609084 * jax.random.uniform(arg_keys[0], (TOT_BLK, BS, BS * BS), jnp.float32) ** levels(arg_keys[0], (TOT_BLK, BS, BS * BS), ((0, 32),), -0.2, 0.2)), 0.099609375, 10.0).astype(jnp.bfloat16)
    src_factor = jnp.clip(jax.random.uniform(arg_keys[1], (SRC_ROWS, R), jnp.float32, -0.5, 0.5) * levels(arg_keys[1], (SRC_ROWS, R), ((0, 32),), -0.4, 0.0), -0.5, 0.5).astype(jnp.bfloat16)
    dst_factor = jnp.clip(jax.random.uniform(arg_keys[2], (DST_ROWS, R), jnp.float32, -0.5, 0.5) * levels(arg_keys[2], (DST_ROWS, R), ((0, 8),), -0.4, 0.0), -0.5, 0.5).astype(jnp.bfloat16)
    hour_factor = jnp.clip(jax.random.uniform(arg_keys[3], (HOURS, R), jnp.float32, -0.5, 0.5), -0.5, 0.5).astype(jnp.bfloat16)
    src_owner_keys = jax.random.split(jax.random.fold_in(arg_keys[4], 1), TOT_BLK // NB)
    src_owner_turns = jax.random.permutation(jax.random.fold_in(arg_keys[4], 3), TOT_BLK // NB)
    src_owner = jax.vmap(lambda own, number: shared_out(jax.random.fold_in(arg_keys[4], 2), own, number, NB, N_DEV, 1, CAP, 2))(src_owner_keys, src_owner_turns).reshape((TOT_BLK, 1))
    src_slot = place_ends(jax.random.randint(arg_keys[5], (TOT_BLK,), 0, SRC_DEV), jax.random.fold_in(arg_keys[5], 1), 0, SRC_DEV - 1).astype(jnp.int32)
    dst_owner_keys = jax.random.split(jax.random.fold_in(arg_keys[6], 1), TOT_BLK // NB)
    dst_owner_turns = jax.random.permutation(jax.random.fold_in(arg_keys[6], 3), TOT_BLK // NB)
    dst_owner = jax.vmap(lambda own, number: shared_out(jax.random.fold_in(arg_keys[6], 2), own, number, NB, N_DEV, 1, CAP, 2))(dst_owner_keys, dst_owner_turns).reshape((TOT_BLK, 1))
    dst_slot = place_ends(jax.random.randint(arg_keys[7], (TOT_BLK,), 0, DST_DEV), jax.random.fold_in(arg_keys[7], 1), 0, DST_DEV - 1).astype(jnp.int32)
    hour_block = place_ends(jax.random.randint(arg_keys[8], (TOT_BLK,), 0, HB), jax.random.fold_in(arg_keys[8], 1), 0, HB - 1).astype(jnp.int32)
    return {"counts": counts, "src_factor": src_factor, "dst_factor": dst_factor, "hour_factor": hour_factor, "src_owner": src_owner, "src_slot": src_slot, "dst_owner": dst_owner, "dst_slot": dst_slot, "hour_block": hour_block}


def block_terms(block, src_rows, dst_rows, hour_rows):
    block_side = block.shape[0]
    factor_rank = src_rows.shape[1]
    scale = 1.0 / block_side
    wide_a = src_rows.astype(jnp.float32)
    wide_b = dst_rows.astype(jnp.float32)
    wide_c = hour_rows.astype(jnp.float32)
    pair_bc = (wide_b[:, None, :] * wide_c[None, :, :]).astype(jnp.bfloat16)
    pair_ac = (wide_a[:, None, :] * wide_c[None, :, :]).astype(jnp.bfloat16)
    pair_ab = (wide_a[:, None, :] * wide_b[None, :, :]).astype(jnp.bfloat16)
    flat_bc = pair_bc.reshape(block_side * block_side, factor_rank)
    theta = jnp.dot(src_rows, flat_bc.T, preferred_element_type=jnp.float32)
    resid = (jnp.exp(theta) - block.reshape(block_side, block_side * block_side).astype(jnp.float32)).astype(jnp.bfloat16)
    grad_a = jnp.dot(resid, flat_bc, preferred_element_type=jnp.float32) * scale
    cube = resid.reshape(block_side, block_side, block_side).astype(jnp.float32)
    grad_b = jnp.einsum("ijk,ikr->jr", cube, pair_ac.astype(jnp.float32), preferred_element_type=jnp.float32) * scale
    grad_c = jnp.einsum("ijk,ijr->kr", cube, pair_ab.astype(jnp.float32), preferred_element_type=jnp.float32) * scale
    return grad_a, grad_b, grad_c


def reference(counts, src_factor, dst_factor, hour_factor, src_owner, src_slot, dst_owner, dst_slot, hour_block):
    total = counts.shape[0]
    src_table = src_factor.reshape(-1, BS, R)
    dst_table = dst_factor.reshape(-1, BS, R)
    group_of = jnp.arange(total, dtype=jnp.int32) // (N_DEV * NB)
    src_index = (group_of * (N_DEV * SRC_DEV) + src_owner[:, 0] * SRC_DEV + src_slot).astype(jnp.int32)
    dst_index = (dst_owner[:, 0] * DST_DEV + dst_slot).astype(jnp.int32)

    def visit(carry, inputs):
        acc_src, acc_dst, acc_hour = carry
        block, src_pick, dst_pick, hour_pick = inputs
        a_rows = lax.dynamic_index_in_dim(src_table, src_pick, 0, keepdims=False)
        b_rows = lax.dynamic_index_in_dim(dst_table, dst_pick, 0, keepdims=False)
        start = (hour_pick * BS).astype(jnp.int32)
        c_rows = lax.dynamic_slice_in_dim(hour_factor, start, BS, 0)
        grad_a, grad_b, grad_c = block_terms(block, a_rows, b_rows, c_rows)
        acc_src = acc_src.at[src_pick].add(grad_a)
        acc_dst = acc_dst.at[dst_pick].add(grad_b)
        current = lax.dynamic_slice_in_dim(acc_hour, start, BS, 0)
        acc_hour = lax.dynamic_update_slice_in_dim(acc_hour, current + grad_c, start, 0)
        return (acc_src, acc_dst, acc_hour), None

    start_state = (jnp.zeros(src_table.shape, jnp.float32), jnp.zeros(dst_table.shape, jnp.float32), jnp.zeros(hour_factor.shape, jnp.float32))
    final, unused = lax.scan(visit, start_state, (counts, src_index, dst_index, hour_block.astype(jnp.int32)))
    acc_src, acc_dst, acc_hour = final
    return acc_src.reshape(-1, R), acc_dst.reshape(-1, R), acc_hour
```

```python
import functools

import jax
import jax.numpy as jnp
from jax import lax
from jax.experimental import pallas as pl
from jax.experimental.pallas import tpu as pltpu
from jax.sharding import PartitionSpec as P

F32 = jnp.float32
BF16 = jnp.bfloat16
SIDE = 64
RING = 6
PITCH = 72

VMEM = pl.BlockSpec(memory_space=pltpu.VMEM)
SMEM = pl.BlockSpec(memory_space=pltpu.SMEM)
ANY = pl.BlockSpec(memory_space=pl.ANY)


def mesh_sizes(mesh):
    return mesh.shape["grp"], mesh.shape["dev"]


def swap(x, axis, size, mask):
    return lax.ppermute(x, axis, [(i, i ^ mask) for i in range(size)])


def block_terms(count, a, b, c, cube, even, odd):
    rank = a.shape[1]
    resids, pairs_bc, turned, pairs_ab = [], [], [], []
    for g in range(SIDE // 4):
        b4 = b[g * 4 : g * 4 + 4]
        bc = (b4[:, None, :] * c[None, :, :]).reshape(4 * SIDE, rank)
        ab = (b4[:, None, :] * a[None, :, :]).reshape(4 * SIDE, rank)
        theta = lax.dot_general(a, bc, (((1,), (1,)), ((), ())), preferred_element_type=F32)
        wide = jnp.exp(theta) - count[:, g * 256 : (g + 1) * 256].astype(F32)
        for p in range(2):
            cube[pl.ds((g * 2 + p) * PITCH, SIDE), :] = wide[:, p * 128 : (p + 1) * 128]
        resid = wide.astype(BF16)
        flip = resid.T
        turned += [flip[q * SIDE : (q + 1) * SIDE] for q in range(4)]
        resids.append(resid)
        pairs_bc.append(bc)
        pairs_ab.append(ab)
    term_a = jnp.dot(
        jnp.concatenate(resids, axis=1),
        jnp.concatenate(pairs_bc, axis=0),
        preferred_element_type=F32,
    )
    term_c = jnp.dot(
        jnp.concatenate(turned, axis=1),
        jnp.concatenate(pairs_ab, axis=0),
        preferred_element_type=F32,
    )
    low = lax.broadcasted_iota(jnp.int32, (SIDE // 2, 128), 1) < SIDE
    rows, pairs_ac = [], []
    for g in range(SIDE // 4):
        x = [cube[pl.ds(g * 4 + q, SIDE // 2, stride=PITCH), :] for q in range(4)]
        y = [pltpu.roll(v, SIDE, 1) for v in x]
        evens = [jnp.where(low, x[0], y[1]), jnp.where(low, x[2], y[3])]
        odds = [jnp.where(low, y[0], x[1]), jnp.where(low, y[2], x[3])]
        both = [jnp.concatenate(evens, axis=1), jnp.concatenate(odds, axis=1)]
        rows.append(jnp.concatenate(both, axis=0).astype(BF16))
        pairs_ac.append((a[g * 4 : g * 4 + 4][:, None, :] * c[None, :, :]).reshape(4 * SIDE, rank))
    mixed = jnp.dot(
        jnp.concatenate(rows, axis=1),
        jnp.concatenate(pairs_ac, axis=0),
        preferred_element_type=F32,
    )
    half = SIDE // 2
    for u in range(2):
        even[pl.ds(u, half, stride=2), :] = mixed[u * half : (u + 1) * half, :128]
        odd[pl.ds(u, half, stride=2), :] = mixed[u * half : (u + 1) * half, 128:]
    term_b = jnp.concatenate([even[...], odd[...]], axis=1)
    return term_a, term_b, term_c


def main_kernel(shape, ids, counts, hours, *refs):
    grps, devs, local, hour_rows = shape
    depth = devs // 2
    pieces = refs[:devs]
    hd_keep, s_keep, hd_send, s_send = refs[devs : devs + 4]
    (ring, table, hd_acc, s_acc, hd_out, s_out, cube, even, odd, ring_sem, in_sem, out_sem) = refs[
        devs + 4 :
    ]
    blocks = counts.shape[0]
    hour_part = hour_rows // (2 * grps)
    dst_part = local // grps
    part = hour_part + depth * dst_part
    hour_blocks = hour_part // SIDE

    def fetch(t):
        slot = lax.rem(t, RING)
        return pltpu.make_async_copy(counts.at[t], ring.at[slot], ring_sem.at[slot])

    for t in range(min(RING, blocks)):
        fetch(t).start()
    loads = [
        pltpu.make_async_copy(pieces[m], table.at[pl.ds(m * 2 * local, 2 * local)], in_sem.at[m])
        for m in range(devs)
    ]
    for load in loads:
        load.start()
    hd_acc[...] = jnp.zeros_like(hd_acc)
    s_acc[...] = jnp.zeros_like(s_acc)
    for load in loads:
        load.wait()
    me, grp = ids[0], ids[1]
    core = me & 1
    base = 8

    def visit(t, carry):
        src_from = ids[base + t] ^ me
        src_slot = ids[base + blocks + t]
        dst_from = ids[base + 2 * blocks + t] ^ me
        dst_slot = ids[base + 3 * blocks + t]
        hour = ids[base + 4 * blocks + t]
        fetch(t).wait()
        a_at = pl.multiple_of(src_from * (2 * local) + src_slot * SIDE, SIDE)
        b_at = pl.multiple_of(dst_from * (2 * local) + local + dst_slot * SIDE, SIDE)
        c_at = pl.multiple_of(hour * SIDE, SIDE)
        term_a, term_b, term_c = block_terms(
            ring.at[lax.rem(t, RING)],
            table[pl.ds(a_at, SIDE), :],
            table[pl.ds(b_at, SIDE), :],
            hours[pl.ds(c_at, SIDE), :],
            cube,
            even,
            odd,
        )
        s_at = (src_from & 1) * (depth * local) + (src_from >> 1) * local + src_slot * SIDE
        row = dst_slot * SIDE
        d_at = ((dst_from & 1) * grps + ((row // dst_part) ^ grp)) * part + hour_part
        d_at = d_at + (dst_from >> 1) * dst_part + row % dst_part
        home = hour // hour_blocks
        h_at = (((home // grps) ^ core) * grps + ((home % grps) ^ grp)) * part
        h_at = h_at + (hour % hour_blocks) * SIDE
        s_acc[pl.ds(pl.multiple_of(s_at, SIDE), SIDE), :] += term_a
        hd_acc[pl.ds(pl.multiple_of(d_at, SIDE), SIDE), :] += term_b
        hd_acc[pl.ds(pl.multiple_of(h_at, SIDE), SIDE), :] += term_c

        @pl.when(t + RING < blocks)
        def _():
            fetch(t + RING).start()

        return carry

    lax.fori_loop(0, blocks, visit, 0)
    hd_half, s_half = grps * part, depth * local
    stores = [
        pltpu.make_async_copy(hd_acc.at[pl.ds(0, hd_half)], hd_keep, out_sem.at[0]),
        pltpu.make_async_copy(s_acc.at[pl.ds(0, s_half)], s_keep, out_sem.at[1]),
        pltpu.make_async_copy(hd_out, hd_send, out_sem.at[2]),
        pltpu.make_async_copy(s_out, s_send, out_sem.at[3]),
    ]
    hd_out[...] = hd_acc[pl.ds(hd_half, hd_half), :].astype(BF16)
    stores[2].start()
    stores[0].start()
    s_out[...] = s_acc[pl.ds(s_half, s_half), :].astype(BF16)
    stores[3].start()
    stores[1].start()
    for store in stores:
        store.wait()


def run_main(shape, ids, counts, hours, pieces):
    grps, devs, local, hour_rows = shape
    depth = devs // 2
    rank = hours.shape[1]
    part = hour_rows // (2 * grps) + depth * (local // grps)
    hd_half, s_half = grps * part, depth * local
    scratch = [
        ((RING,) + counts.shape[1:], BF16),
        ((devs * 2 * local, rank), BF16),
        ((2 * hd_half, rank), F32),
        ((2 * s_half, rank), F32),
        ((hd_half, rank), BF16),
        ((s_half, rank), BF16),
        ((SIDE // 2 * PITCH, 128), F32),
        ((SIDE, 128), F32),
        ((SIDE, 128), F32),
    ]
    need = sum(jnp.dtype(t).itemsize * functools.reduce(lambda x, y: x * y, s) for s, t in scratch)
    need += hours.size * 2 + (10 << 20)
    blocks = counts.shape[0]
    flops = 8 * blocks * SIDE**3 * rank
    return pl.pallas_call(
        functools.partial(main_kernel, shape),
        in_specs=[SMEM, ANY, VMEM] + [ANY] * devs,
        out_specs=[ANY] * 4,
        out_shape=[
            jax.ShapeDtypeStruct((hd_half, rank), F32),
            jax.ShapeDtypeStruct((s_half, rank), F32),
            jax.ShapeDtypeStruct((hd_half, rank), BF16),
            jax.ShapeDtypeStruct((s_half, rank), BF16),
        ],
        scratch_shapes=[pltpu.VMEM(s, t) for s, t in scratch]
        + [
            pltpu.SemaphoreType.DMA((RING,)),
            pltpu.SemaphoreType.DMA((devs,)),
            pltpu.SemaphoreType.DMA((4,)),
        ],
        compiler_params=pltpu.CompilerParams(vmem_limit_bytes=need),
        cost_estimate=pl.CostEstimate(
            flops=flops, bytes_accessed=counts.size * 2, transcendentals=counts.size
        ),
        name="terms",
    )(ids, counts, hours, *pieces)


def split_kernel(ways, keep, got, mine, *sends):
    rows = mine.shape[0]
    mine[...] = keep[pl.ds(0, rows), :] + got[pl.ds(0, rows), :].astype(F32)
    for m in range(1, ways):
        at = pl.ds(m * rows, rows)
        sends[m - 1][...] = (keep[at, :] + got[at, :].astype(F32)).astype(BF16)


def run_split(ways, keep, got, name):
    rows, rank = keep.shape[0] // ways, keep.shape[1]
    return pl.pallas_call(
        functools.partial(split_kernel, ways),
        in_specs=[VMEM, VMEM],
        out_specs=[VMEM] * ways,
        out_shape=[jax.ShapeDtypeStruct((rows, rank), F32)]
        + [jax.ShapeDtypeStruct((rows, rank), BF16)] * (ways - 1),
        compiler_params=pltpu.CompilerParams(vmem_limit_bytes=40 << 20),
        name=name,
    )(keep, got)


def run_grp_sum(hour_part, depth, ids, parts):
    rows, rank = parts[0].shape
    hour_rows = hour_part // depth
    dst_rows = (rows - hour_part) // depth
    ways = len(parts)

    def kernel(ids, *refs):
        ins, outs, total = refs[:ways], refs[ways:-1], refs[-1]
        z = ids[0] >> 1
        acc = ins[0][...]
        for r in ins[1:]:
            acc = acc + r[...].astype(F32)
        total[...] = acc
        for m in range(depth):
            at = pl.multiple_of((z ^ m) * hour_rows, hour_rows)
            kind = F32 if m == 0 else BF16
            outs[m][pl.ds(0, hour_rows), :] = total[pl.ds(at, hour_rows), :].astype(kind)
            low = hour_part + m * dst_rows
            outs[m][pl.ds(hour_rows, dst_rows), :] = total[pl.ds(low, dst_rows), :].astype(kind)

    each = hour_rows + dst_rows
    return pl.pallas_call(
        kernel,
        in_specs=[SMEM] + [VMEM] * ways,
        out_specs=[VMEM] * depth,
        out_shape=[jax.ShapeDtypeStruct((each, rank), F32)]
        + [jax.ShapeDtypeStruct((each, rank), BF16)] * (depth - 1),
        scratch_shapes=[pltpu.VMEM((rows, rank), F32)],
        compiler_params=pltpu.CompilerParams(vmem_limit_bytes=32 << 20),
        name="grp_sum",
    )(ids, *parts)


def run_z_sum(hour_rows, hd_parts, s_parts):
    rank = hd_parts[0].shape[1]
    dst_rows = hd_parts[0].shape[0] - hour_rows
    src_rows = s_parts[0].shape[0]
    n = len(hd_parts)

    def kernel(*refs):
        hd, s, (h_out, d_out, s_out) = refs[:n], refs[n : 2 * n], refs[2 * n :]
        acc = hd[0][...]
        for r in hd[1:]:
            acc = acc + r[...].astype(F32)
        acc = acc * (1.0 / SIDE)
        h_out[...] = acc[:hour_rows].astype(BF16)
        d_out[...] = acc[hour_rows:]
        acc = s[0][...]
        for r in s[1:]:
            acc = acc + r[...].astype(F32)
        s_out[...] = acc * (1.0 / SIDE)

    return pl.pallas_call(
        kernel,
        in_specs=[VMEM] * (2 * n),
        out_specs=[VMEM] * 3,
        out_shape=[
            jax.ShapeDtypeStruct((hour_rows, rank), BF16),
            jax.ShapeDtypeStruct((dst_rows, rank), F32),
            jax.ShapeDtypeStruct((src_rows, rank), F32),
        ],
        compiler_params=pltpu.CompilerParams(vmem_limit_bytes=32 << 20),
        name="z_sum",
    )(*hd_parts, *s_parts)


def run_place(grps, depth, ids, hour_parts, dst_parts):
    part, rank = hour_parts[0].shape
    rows = part // depth
    dst_rows = dst_parts[0].shape[0]
    n = len(hour_parts)

    def kernel(ids, *refs):
        hours, dsts, h_out, d_out = refs[:n], refs[n : n + grps], refs[-2], refs[-1]
        core, z, grp = ids[0] & 1, ids[0] >> 1, ids[1]
        for m in range(n):
            home = ((core ^ (m // grps)) * grps + (grp ^ (m % grps))) * part
            for k in range(depth):
                at = pl.multiple_of(home + (z ^ k) * rows, rows)
                h_out[pl.ds(at, rows), :] = hours[m][pl.ds(k * rows, rows), :].astype(F32)
        for m in range(grps):
            at = pl.multiple_of((grp ^ m) * dst_rows, dst_rows)
            d_out[pl.ds(at, dst_rows), :] = dsts[m][...]

    return pl.pallas_call(
        kernel,
        in_specs=[SMEM] + [VMEM] * (n + grps),
        out_specs=[VMEM] * 2,
        out_shape=[
            jax.ShapeDtypeStruct((n * part, rank), F32),
            jax.ShapeDtypeStruct((grps * dst_rows, rank), F32),
        ],
        compiler_params=pltpu.CompilerParams(vmem_limit_bytes=32 << 20),
        name="place",
    )(ids, *hour_parts, *dst_parts)


def per_device(
    sizes,
    counts,
    src_factor,
    dst_factor,
    hour_factor,
    src_owner,
    src_slot,
    dst_owner,
    dst_slot,
    hour_block,
):
    grps, devs = sizes
    depth = devs // 2
    local = src_factor.shape[0]
    hour_rows = hour_factor.shape[0]
    me = lax.axis_index("dev").astype(jnp.int32)
    grp = lax.axis_index("grp").astype(jnp.int32)
    place = jnp.stack([me, grp] + [me * 0] * 6)
    ids = jnp.concatenate(
        [place, src_owner[:, 0], src_slot, dst_owner[:, 0], dst_slot, hour_block]
    )
    own = jnp.concatenate([src_factor, dst_factor], axis=0)
    along = [own] + [swap(own, "dev", devs, 2 * m) for m in range(1, depth)]
    across = [swap(x, "dev", devs, 1) for x in along]
    pieces = [x for pair in zip(along, across) for x in pair]
    shape = (grps, devs, local, hour_rows)
    hd_keep, s_keep, hd_send, s_send = run_main(shape, ids, counts, hour_factor, pieces)
    hd_got = swap(hd_send, "dev", devs, 1)
    s_got = swap(s_send, "dev", devs, 1)
    hd = run_split(grps, hd_keep, hd_got, "core_hd")
    s = run_split(depth, s_keep, s_got, "core_s")
    hd = [hd[0]] + [swap(x, "grp", grps, m) for m, x in enumerate(hd) if m]
    s = [s[0]] + [swap(x, "dev", devs, 2 * m) for m, x in enumerate(s) if m]
    hour_part = hour_rows // (2 * grps)
    hd = run_grp_sum(hour_part, depth, ids, hd)
    hd = [hd[0]] + [swap(x, "dev", devs, 2 * m) for m, x in enumerate(hd) if m]
    hour, dst, grad_src = run_z_sum(hour_part // depth, hd, s)
    dsts = [dst] + [swap(dst, "grp", grps, m) for m in range(1, grps)]
    hour = jnp.concatenate(
        [hour] + [swap(hour, "dev", devs, 2 * m) for m in range(1, depth)], axis=0
    )
    hours = [hour] + [swap(hour, "grp", grps, m) for m in range(1, grps)]
    hours = hours + [swap(x, "dev", devs, 1) for x in hours]
    grad_hour, grad_dst = run_place(grps, depth, ids, hours, dsts)
    return grad_src, grad_dst, grad_hour


def solution(mesh):
    in_specs = (
        P(("grp", "dev"), None, None),
        P(("grp", "dev"), None),
        P("dev", None),
        P(),
        P(("grp", "dev"), None),
        P(("grp", "dev")),
        P(("grp", "dev"), None),
        P(("grp", "dev")),
        P(("grp", "dev")),
    )
    out_specs = (P(("grp", "dev"), None), P("dev", None), P())
    return jax.shard_map(
        functools.partial(per_device, mesh_sizes(mesh)),
        mesh=mesh,
        in_specs=in_specs,
        out_specs=out_specs,
        check_vma=False,
    )
```

```python
import functools

import jax
import jax.numpy as jnp
from jax import lax
from jax.experimental import pallas as pl
from jax.experimental.pallas import tpu as pltpu
from jax.sharding import PartitionSpec as P

F32 = jnp.float32
BF16 = jnp.bfloat16
SIDE = 64
RING = 8
PITCH = 72
GRANT = 36 << 20

VMEM = pl.BlockSpec(memory_space=pltpu.VMEM)
SMEM = pl.BlockSpec(memory_space=pltpu.SMEM)
ANY = pl.BlockSpec(memory_space=pl.ANY)
HBM = pl.BlockSpec(memory_space=pltpu.HBM)


def mesh_sizes(mesh):
    return mesh.shape["grp"], mesh.shape["dev"]


def swap(x, axis, size, mask):
    return lax.ppermute(x, axis, [(i, i ^ mask) for i in range(size)])


def block_terms(count, a, b, c, cube, even, odd):
    rank = a.shape[1]
    resids, pairs_bc, turned, pairs_ab = [], [], [], []
    for g in range(SIDE // 4):
        b4 = b[g * 4 : g * 4 + 4]
        bc = (b4[:, None, :] * c[None, :, :]).reshape(4 * SIDE, rank)
        ab = (b4[:, None, :] * a[None, :, :]).reshape(4 * SIDE, rank)
        theta = lax.dot_general(a, bc, (((1,), (1,)), ((), ())), preferred_element_type=F32)
        wide = jnp.exp(theta) - count[:, g * 256 : (g + 1) * 256].astype(F32)
        for p in range(2):
            cube[pl.ds((g * 2 + p) * PITCH, SIDE), :] = wide[:, p * 128 : (p + 1) * 128]
        resid = wide.astype(BF16)
        flip = resid.T
        turned += [flip[q * SIDE : (q + 1) * SIDE] for q in range(4)]
        resids.append(resid)
        pairs_bc.append(bc)
        pairs_ab.append(ab)
    term_a = jnp.dot(
        jnp.concatenate(resids, axis=1),
        jnp.concatenate(pairs_bc, axis=0),
        preferred_element_type=F32,
    )
    term_c = jnp.dot(
        jnp.concatenate(turned, axis=1),
        jnp.concatenate(pairs_ab, axis=0),
        preferred_element_type=F32,
    )
    low = lax.broadcasted_iota(jnp.int32, (SIDE // 2, 128), 1) < SIDE
    rows, pairs_ac = [], []
    for g in range(SIDE // 4):
        x = [cube[pl.ds(g * 4 + q, SIDE // 2, stride=PITCH), :] for q in range(4)]
        y = [pltpu.roll(v, SIDE, 1) for v in x]
        evens = [jnp.where(low, x[0], y[1]), jnp.where(low, x[2], y[3])]
        odds = [jnp.where(low, y[0], x[1]), jnp.where(low, y[2], x[3])]
        both = [jnp.concatenate(evens, axis=1), jnp.concatenate(odds, axis=1)]
        rows.append(jnp.concatenate(both, axis=0).astype(BF16))
        pairs_ac.append((a[g * 4 : g * 4 + 4][:, None, :] * c[None, :, :]).reshape(4 * SIDE, rank))
    mixed = jnp.dot(
        jnp.concatenate(rows, axis=1),
        jnp.concatenate(pairs_ac, axis=0),
        preferred_element_type=F32,
    )
    half = SIDE // 2
    for u in range(2):
        even[pl.ds(u, half, stride=2), :] = mixed[u * half : (u + 1) * half, :128]
        odd[pl.ds(u, half, stride=2), :] = mixed[u * half : (u + 1) * half, 128:]
    term_b = jnp.concatenate([even[...], odd[...]], axis=1)
    return term_a, term_b, term_c


def run_pick(blocks, ids, hours, own):
    rank = hours.shape[1]

    def kernel(ids, hours, own, out, same, sem):
        copies = []
        for t in range(blocks):
            at = pl.multiple_of(ids[8 + 4 * blocks + t] * SIDE, SIDE)
            copies.append(
                pltpu.make_async_copy(
                    hours.at[pl.ds(at, SIDE)], out.at[pl.ds(t * SIDE, SIDE)], sem.at[t]
                )
            )
            copies[-1].start()
        same[...] = own[...]
        for copy in copies:
            copy.wait()

    return pl.pallas_call(
        kernel,
        in_specs=[SMEM, HBM, VMEM],
        out_specs=[VMEM, VMEM],
        out_shape=[
            jax.ShapeDtypeStruct((blocks * SIDE, rank), BF16),
            jax.ShapeDtypeStruct(own.shape, BF16),
        ],
        scratch_shapes=[pltpu.SemaphoreType.DMA((blocks,))],
        name="pick_hours",
    )(ids, hours, own)


def main_kernel(shape, ids, counts, hours, *refs):
    grps, devs, local, hour_rows = shape
    depth = devs // 2
    pieces = refs[:devs]
    h_acc, sd_acc, h_send, sd_send = refs[devs : devs + 4]
    ring, table, cube, even, odd, ring_sem, in_sem = refs[devs + 4 :]
    blocks = counts.shape[0]
    hour_part = hour_rows // (2 * grps)
    hour_blocks = hour_part // SIDE
    dst_part = local // grps
    sd_half = 2 * depth * local
    base = 8

    def fetch(t):
        slot = lax.rem(t, RING)
        return pltpu.make_async_copy(counts.at[t], ring.at[slot], ring_sem.at[slot])

    for t in range(min(RING, blocks)):
        fetch(t).start()
    loads = [
        pltpu.make_async_copy(pieces[m], table.at[pl.ds(m * 2 * local, 2 * local)], in_sem.at[m])
        for m in range(devs)
    ]
    for load in loads:
        load.start()
    h_acc[...] = jnp.zeros_like(h_acc)
    sd_acc[...] = jnp.zeros_like(sd_acc)
    for load in loads:
        load.wait()
    me, grp = ids[0], ids[1]
    core = me & 1

    def visit(t, carry):
        src_from = ids[base + t] ^ me
        src_slot = ids[base + blocks + t]
        dst_from = ids[base + 2 * blocks + t] ^ me
        dst_slot = ids[base + 3 * blocks + t]
        hour = ids[base + 4 * blocks + t]
        fetch(t).wait()
        slot = lax.rem(t, RING)
        a_at = pl.multiple_of(src_from * (2 * local) + src_slot * SIDE, SIDE)
        b_at = pl.multiple_of(dst_from * (2 * local) + local + dst_slot * SIDE, SIDE)
        term_a, term_b, term_c = block_terms(
            ring.at[slot],
            table[pl.ds(a_at, SIDE), :],
            table[pl.ds(b_at, SIDE), :],
            hours[pl.ds(pl.multiple_of(t * SIDE, SIDE), SIDE), :],
            cube,
            even,
            odd,
        )
        s_at = (src_from & 1) * sd_half + depth * local
        s_at = s_at + (src_from >> 1) * local + src_slot * SIDE
        row = dst_slot * SIDE
        d_at = (dst_from & 1) * sd_half + ((row // dst_part) ^ grp) * (depth * dst_part)
        d_at = d_at + (dst_from >> 1) * dst_part + row % dst_part
        home = hour // hour_blocks
        h_at = (((home // grps) ^ core) * grps + ((home % grps) ^ grp)) * hour_part
        h_at = h_at + (hour % hour_blocks) * SIDE
        sd_acc[pl.ds(pl.multiple_of(s_at, SIDE), SIDE), :] += term_a
        sd_acc[pl.ds(pl.multiple_of(d_at, SIDE), SIDE), :] += term_b
        h_acc[pl.ds(pl.multiple_of(h_at, SIDE), SIDE), :] += term_c

        @pl.when(t + RING < blocks)
        def _():
            fetch(t + RING).start()

        return carry

    lax.fori_loop(0, blocks, visit, 0)
    h_send[...] = h_acc[pl.ds(hour_rows // 2, hour_rows // 2), :].astype(BF16)
    sd_send[...] = sd_acc[pl.ds(sd_half, sd_half), :].astype(BF16)


def size_of(shapes):
    return sum(jnp.dtype(t).itemsize * functools.reduce(lambda x, y: x * y, s) for s, t in shapes)


def run_main(shape, ids, counts, hours, pieces):
    grps, devs, local, hour_rows = shape
    rank = hours.shape[1]
    outs = [
        ((hour_rows, rank), F32),
        ((2 * devs * local, rank), F32),
        ((hour_rows // 2, rank), BF16),
        ((devs * local, rank), BF16),
    ]
    scratch = [
        ((RING,) + counts.shape[1:], BF16),
        ((devs * 2 * local, rank), BF16),
        ((SIDE // 2 * PITCH, 128), F32),
        ((SIDE, 128), F32),
        ((SIDE, 128), F32),
    ]
    need = max(size_of(outs) + size_of(scratch) + (8 << 20), GRANT)
    return pl.pallas_call(
        functools.partial(main_kernel, shape),
        in_specs=[SMEM, HBM, VMEM] + [ANY] * devs,
        out_specs=[VMEM] * 4,
        out_shape=[jax.ShapeDtypeStruct(s, t) for s, t in outs],
        scratch_shapes=[pltpu.VMEM(s, t) for s, t in scratch]
        + [
            pltpu.SemaphoreType.DMA((RING,)),
            pltpu.SemaphoreType.DMA((devs,)),
        ],
        compiler_params=pltpu.CompilerParams(vmem_limit_bytes=need),
        cost_estimate=pl.CostEstimate(
            flops=8 * counts.size * rank,
            bytes_accessed=counts.size * 2,
            transcendentals=counts.size,
        ),
        name="terms",
    )(ids, counts, hours, *pieces)


def call(kernel, name, ins, outs, specs=None, scratch=()):
    shapes = [(x.shape, x.dtype) for x in ins] + list(outs) + list(scratch)
    return pl.pallas_call(
        kernel,
        in_specs=specs or [VMEM] * len(ins),
        out_specs=[VMEM] * len(outs),
        out_shape=[jax.ShapeDtypeStruct(s, t) for s, t in outs],
        scratch_shapes=[pltpu.VMEM(s, t) for s, t in scratch],
        compiler_params=pltpu.CompilerParams(vmem_limit_bytes=size_of(shapes) + (4 << 20)),
        name=name,
    )(*ins)


def cut(acc, got, start, rows, ways, outs):
    for m in range(ways):
        at = pl.ds(start + m * rows, rows)
        outs[m][...] = (acc[at, :] + got[at, :].astype(F32)).astype(outs[m].dtype)


def shares(rows, rank, ways):
    return [((rows, rank), F32)] + [((rows, rank), BF16)] * (ways - 1)


def run_cut_hours(grps, acc, got):
    rows, rank = got.shape[0] // grps, got.shape[1]

    def kernel(acc, got, *outs):
        cut(acc, got, 0, rows, grps, outs)

    return call(kernel, "core_hours", (acc, got), shares(rows, rank, grps))


def run_cut_src(depth, local, acc, got):
    rank = got.shape[1]

    def kernel(acc, got, *outs):
        cut(acc, got, depth * local, local, depth, outs)

    return call(kernel, "core_src", (acc, got), shares(local, rank, depth))


def run_cut_dst(grps, depth, local, acc, got, after):
    rank = got.shape[1]
    rows = depth * local // grps

    def kernel(acc, got, after, *outs):
        cut(acc, got, 0, rows, grps, outs)

    return call(
        kernel,
        "core_dst",
        (acc, got, after),
        shares(rows, rank, grps),
        specs=[VMEM, VMEM, ANY],
    )


def total(refs):
    acc = refs[0][...]
    for r in refs[1:]:
        acc = acc + r[...].astype(F32)
    return acc


def run_grp_hours(depth, ids, parts):
    rows, rank = parts[0].shape
    ways, each = len(parts), rows // depth

    def kernel(ids, *refs):
        outs, acc = refs[ways:-1], refs[-1]
        z = ids[0] >> 1
        acc[...] = total(refs[:ways])
        for m in range(depth):
            at = pl.multiple_of((z ^ m) * each, each)
            outs[m][...] = acc[pl.ds(at, each), :].astype(outs[m].dtype)

    return call(
        kernel,
        "grp_hours",
        (ids, *parts),
        shares(each, rank, depth),
        specs=[SMEM] + [VMEM] * ways,
        scratch=[((rows, rank), F32)],
    )


def run_grp_dst(depth, parts):
    rows, rank = parts[0].shape
    ways, each = len(parts), rows // depth

    def kernel(*refs):
        acc = total(refs[:ways])
        for m in range(depth):
            out = refs[ways + m]
            out[...] = acc[m * each : (m + 1) * each].astype(out.dtype)

    return call(kernel, "grp_dst", parts, shares(each, rank, depth))


def run_z(parts, kind, name):
    def kernel(*refs):
        refs[-1][...] = (total(refs[:-1]) * (1.0 / SIDE)).astype(kind)

    return call(kernel, name, parts, [(parts[0].shape, kind)])[0]


def run_join(parts):
    rows = [p.shape[0] for p in parts]

    def kernel(*refs):
        at = 0
        for ref, n in zip(refs[:-1], rows):
            refs[-1][at : at + n, :] = ref[...]
            at += n

    return call(kernel, "join", parts, [((sum(rows), parts[0].shape[1]), BF16)])[0]


def run_place(sizes, hour_rows, dst_rows, far, ids, parts, so_far):
    grps, devs = sizes
    depth = devs // 2
    rank = parts[0].shape[1]
    part = hour_rows // (2 * grps)
    rows = part // depth

    def kernel(ids, *refs):
        ins = refs[:grps]
        if far:
            h_out, stage, sem = refs[grps + 1 :]
        else:
            h_out, d_out, stage, sem = refs[grps:]
        core, z, grp = (ids[0] & 1) ^ far, ids[0] >> 1, ids[1]
        copies = []
        for m in range(grps):
            for k in range(depth):
                at = pl.multiple_of((z ^ k) * rows, rows)
                stage[m, pl.ds(at, rows), :] = ins[m][pl.ds(k * rows, rows), :].astype(F32)
            home = pl.multiple_of((core * grps + (grp ^ m)) * part, part)
            copies.append(
                pltpu.make_async_copy(stage.at[m], h_out.at[pl.ds(home, part)], sem.at[m])
            )
            copies[-1].start()
        if not far:
            for m in range(grps):
                at = pl.multiple_of((grp ^ m) * dst_rows, dst_rows)
                d_out[pl.ds(at, dst_rows), :] = ins[m][pl.ds(part, dst_rows), :].astype(F32)
        for copy in copies:
            copy.wait()

    hours = jax.ShapeDtypeStruct((hour_rows, rank), F32)
    dst = jax.ShapeDtypeStruct((grps * dst_rows, rank), F32)
    scratch = [((grps, part, rank), F32)]
    need = size_of([(p.shape, p.dtype) for p in parts] + scratch) + (4 << 20)
    return pl.pallas_call(
        kernel,
        in_specs=[SMEM] + [VMEM] * grps + ([HBM] if far else []),
        out_specs=[HBM] if far else [HBM, VMEM],
        out_shape=[hours] if far else [hours, dst],
        scratch_shapes=[pltpu.VMEM(s, t) for s, t in scratch]
        + [pltpu.SemaphoreType.DMA((grps,))],
        input_output_aliases={grps + 1: 0} if far else {},
        compiler_params=pltpu.CompilerParams(vmem_limit_bytes=need),
        name="place_far" if far else "place_near",
    )(ids, *parts, *([so_far] if far else []))


def per_device(
    sizes,
    counts,
    src_factor,
    dst_factor,
    hour_factor,
    src_owner,
    src_slot,
    dst_owner,
    dst_slot,
    hour_block,
):
    grps, devs = sizes
    depth = devs // 2
    local = src_factor.shape[0]
    hour_rows = hour_factor.shape[0]
    me = lax.axis_index("dev").astype(jnp.int32)
    grp = lax.axis_index("grp").astype(jnp.int32)
    place = jnp.stack([me, grp] + [me * 0] * 6)
    ids = jnp.concatenate(
        [place, src_owner[:, 0], src_slot, dst_owner[:, 0], dst_slot, hour_block]
    )
    own = run_join([src_factor, dst_factor])
    along = [own] + [swap(own, "dev", devs, 2 * m) for m in range(1, depth)]
    picked, same = run_pick(counts.shape[0], ids, hour_factor, own)
    across = [swap(x, "dev", devs, 1) for x in [same] + along[1:]]
    pieces = [x for pair in zip(along, across) for x in pair]
    shape = (grps, devs, local, hour_rows)
    h_acc, sd_acc, h_send, sd_send = run_main(shape, ids, counts, picked, pieces)

    def exchange(parts, axis, size, step):
        return [parts[0]] + [swap(x, axis, size, step * m) for m, x in enumerate(parts) if m]

    h_got = swap(h_send, "dev", devs, 1)
    sd_got = swap(sd_send, "dev", devs, 1)
    hours = run_cut_hours(grps, h_acc, h_got)
    srcs = run_cut_src(depth, local, sd_acc, sd_got)
    hours = run_grp_hours(depth, ids, exchange(hours, "grp", grps, 1))
    grad_src = run_z(exchange(srcs, "dev", devs, 2), F32, "z_src")
    dsts = run_cut_dst(grps, depth, local, sd_acc, sd_got, grad_src)
    dsts = run_grp_dst(depth, exchange(dsts, "grp", grps, 1))
    hour = run_z(exchange(hours, "dev", devs, 2), BF16, "z_hours")
    dst = run_z(exchange(dsts, "dev", devs, 2), BF16, "z_dst")
    back = [hour] + [swap(hour, "dev", devs, 2 * m) for m in range(1, depth)]
    joined = run_join(back + [dst])
    near = [joined] + [swap(joined, "grp", grps, m) for m in range(1, grps)]
    far = [swap(x, "dev", devs, 1) for x in near]
    dst_rows = dst.shape[0]
    part_done, grad_dst = run_place(sizes, hour_rows, dst_rows, 0, ids, near, None)
    grad_hour = run_place(sizes, hour_rows, dst_rows, 1, ids, far, part_done)[0]
    return grad_src, grad_dst, grad_hour


def solution(mesh):
    in_specs = (
        P(("grp", "dev"), None, None),
        P(("grp", "dev"), None),
        P("dev", None),
        P(),
        P(("grp", "dev"), None),
        P(("grp", "dev")),
        P(("grp", "dev"), None),
        P(("grp", "dev")),
        P(("grp", "dev")),
    )
    out_specs = (P(("grp", "dev"), None), P("dev", None), P())
    return jax.shard_map(
        functools.partial(per_device, mesh_sizes(mesh)),
        mesh=mesh,
        in_specs=in_specs,
        out_specs=out_specs,
        check_vma=False,
    )
```

```python
import functools

import jax
import jax.numpy as jnp
from jax import lax
from jax.experimental import pallas as pl
from jax.experimental.pallas import tpu as pltpu
from jax.sharding import PartitionSpec as P

F32 = jnp.float32
BF16 = jnp.bfloat16
SIDE = 64
RING = 8
PITCH = 72
GRANT = 36 << 20

VMEM = pl.BlockSpec(memory_space=pltpu.VMEM)
SMEM = pl.BlockSpec(memory_space=pltpu.SMEM)
ANY = pl.BlockSpec(memory_space=pl.ANY)
HBM = pl.BlockSpec(memory_space=pltpu.HBM)


def mesh_sizes(mesh):
    return mesh.shape["grp"], mesh.shape["dev"]


def swap(x, axis, size, mask):
    return lax.ppermute(x, axis, [(i, i ^ mask) for i in range(size)])


def block_terms(count, a, b, c, cube, even, odd):
    rank = a.shape[1]
    resids, pairs_bc, turned, pairs_ab = [], [], [], []
    for g in range(SIDE // 4):
        b4 = b[g * 4 : g * 4 + 4]
        bc = (b4[:, None, :] * c[None, :, :]).reshape(4 * SIDE, rank)
        ab = (b4[:, None, :] * a[None, :, :]).reshape(4 * SIDE, rank)
        theta = lax.dot_general(a, bc, (((1,), (1,)), ((), ())), preferred_element_type=F32)
        wide = jnp.exp(theta) - count[:, g * 256 : (g + 1) * 256].astype(F32)
        for p in range(2):
            cube[pl.ds((g * 2 + p) * PITCH, SIDE), :] = wide[:, p * 128 : (p + 1) * 128]
        resid = wide.astype(BF16)
        flip = resid.T
        turned += [flip[q * SIDE : (q + 1) * SIDE] for q in range(4)]
        resids.append(resid)
        pairs_bc.append(bc)
        pairs_ab.append(ab)
    term_a = jnp.dot(
        jnp.concatenate(resids, axis=1),
        jnp.concatenate(pairs_bc, axis=0),
        preferred_element_type=F32,
    )
    term_c = jnp.dot(
        jnp.concatenate(turned, axis=1),
        jnp.concatenate(pairs_ab, axis=0),
        preferred_element_type=F32,
    )
    low = lax.broadcasted_iota(jnp.int32, (SIDE // 2, 128), 1) < SIDE
    rows, pairs_ac = [], []
    for g in range(SIDE // 4):
        x = [cube[pl.ds(g * 4 + q, SIDE // 2, stride=PITCH), :] for q in range(4)]
        y = [pltpu.roll(v, SIDE, 1) for v in x]
        evens = [jnp.where(low, x[0], y[1]), jnp.where(low, x[2], y[3])]
        odds = [jnp.where(low, y[0], x[1]), jnp.where(low, y[2], x[3])]
        both = [jnp.concatenate(evens, axis=1), jnp.concatenate(odds, axis=1)]
        rows.append(jnp.concatenate(both, axis=0).astype(BF16))
        pairs_ac.append((a[g * 4 : g * 4 + 4][:, None, :] * c[None, :, :]).reshape(4 * SIDE, rank))
    mixed = jnp.dot(
        jnp.concatenate(rows, axis=1),
        jnp.concatenate(pairs_ac, axis=0),
        preferred_element_type=F32,
    )
    half = SIDE // 2
    for u in range(2):
        even[pl.ds(u, half, stride=2), :] = mixed[u * half : (u + 1) * half, :128]
        odd[pl.ds(u, half, stride=2), :] = mixed[u * half : (u + 1) * half, 128:]
    term_b = jnp.concatenate([even[...], odd[...]], axis=1)
    return term_a, term_b, term_c


def run_pick(blocks, ids, hours, own):
    grant = 4 * blocks * SIDE * hours.shape[1] + 4 * own.size + (2 << 20)
    rank = hours.shape[1]

    def kernel(ids, hours, own, out, same, sem):
        copies = []
        for t in range(blocks):
            at = pl.multiple_of(ids[8 + 4 * blocks + t] * SIDE, SIDE)
            copies.append(
                pltpu.make_async_copy(
                    hours.at[pl.ds(at, SIDE)], out.at[pl.ds(t * SIDE, SIDE)], sem.at[t]
                )
            )
            copies[-1].start()
        same[...] = own[...]
        for copy in copies:
            copy.wait()

    return pl.pallas_call(
        kernel,
        in_specs=[SMEM, HBM, VMEM],
        out_specs=[VMEM, VMEM],
        out_shape=[
            jax.ShapeDtypeStruct((blocks * SIDE, rank), BF16),
            jax.ShapeDtypeStruct(own.shape, BF16),
        ],
        scratch_shapes=[pltpu.SemaphoreType.DMA((blocks,))],
        compiler_params=pltpu.CompilerParams(vmem_limit_bytes=grant),
        name="pick_hours",
    )(ids, hours, own)


def main_kernel(shape, ids, counts, hours, *refs):
    grps, devs, local, hour_rows = shape
    depth = devs // 2
    pieces, refs = refs[:-11], refs[-11:]
    hd_acc, s_acc, hd_send, s_send, ring, table, cube, even, odd, ring_sem, in_sem = refs
    blocks = counts.shape[0]
    hour_part = hour_rows // (2 * grps)
    hour_blocks = hour_part // SIDE
    dst_part = local // grps
    part = hour_part + depth * dst_part
    base = 8

    def fetch(t):
        slot = lax.rem(t, RING)
        return pltpu.make_async_copy(counts.at[t], ring.at[slot], ring_sem.at[slot])

    for t in range(min(RING, blocks)):
        fetch(t).start()
    loads, at = [], 0
    for m, piece in enumerate(pieces):
        rows = piece.shape[0]
        loads.append(pltpu.make_async_copy(piece, table.at[pl.ds(at, rows)], in_sem.at[m]))
        loads[-1].start()
        at += rows
    hd_acc[...] = jnp.zeros_like(hd_acc)
    s_acc[...] = jnp.zeros_like(s_acc)
    for load in loads:
        load.wait()
    me, grp = ids[0], ids[1]
    core = me & 1

    def visit(t, carry):
        src_from = ids[base + t] ^ me
        src_slot = ids[base + blocks + t]
        dst_from = ids[base + 2 * blocks + t] ^ me
        dst_slot = ids[base + 3 * blocks + t]
        hour = ids[base + 4 * blocks + t]
        fetch(t).wait()
        slot = lax.rem(t, RING)
        row = dst_slot * SIDE
        turn = (row // dst_part) ^ grp
        inner = (dst_from >> 1) * dst_part + row % dst_part
        outer = (src_from >> 1) * local + src_slot * SIDE
        half = depth * local
        a_at = pl.multiple_of((src_from & 1) * (2 * half) + outer, SIDE)
        b_at = (dst_from & 1) * (2 * half) + half + turn * (depth * dst_part) + inner
        b_at = pl.multiple_of(b_at, SIDE)
        term_a, term_b, term_c = block_terms(
            ring.at[slot],
            table[pl.ds(a_at, SIDE), :],
            table[pl.ds(b_at, SIDE), :],
            hours[pl.ds(pl.multiple_of(t * SIDE, SIDE), SIDE), :],
            cube,
            even,
            odd,
        )
        s_at = pl.multiple_of((src_from & 1) * half + outer, SIDE)
        d_at = ((dst_from & 1) * grps + turn) * part + hour_part + inner
        home = hour // hour_blocks
        h_at = (((home // grps) ^ core) * grps + ((home % grps) ^ grp)) * part
        h_at = h_at + (hour % hour_blocks) * SIDE
        s_acc[pl.ds(s_at, SIDE), :] += term_a
        hd_acc[pl.ds(pl.multiple_of(d_at, SIDE), SIDE), :] += term_b
        hd_acc[pl.ds(pl.multiple_of(h_at, SIDE), SIDE), :] += term_c

        @pl.when(t + RING < blocks)
        def _():
            fetch(t + RING).start()

        return carry

    lax.fori_loop(0, blocks, visit, 0)
    hd_half, s_half = grps * part, depth * local
    hd_send[...] = hd_acc[pl.ds(hd_half, hd_half), :].astype(BF16)
    s_send[...] = s_acc[pl.ds(s_half, s_half), :].astype(BF16)


def size_of(shapes):
    return sum(jnp.dtype(t).itemsize * functools.reduce(lambda x, y: x * y, s) for s, t in shapes)


def run_main(shape, ids, counts, hours, pieces):
    grps, devs, local, hour_rows = shape
    rank = hours.shape[1]
    hd_rows = hour_rows + devs * local
    outs = [
        ((hd_rows, rank), F32),
        ((devs * local, rank), F32),
        ((hd_rows // 2, rank), BF16),
        ((devs * local // 2, rank), BF16),
    ]
    scratch = [
        ((RING,) + counts.shape[1:], BF16),
        ((devs * 2 * local, rank), BF16),
        ((SIDE // 2 * PITCH, 128), F32),
        ((SIDE, 128), F32),
        ((SIDE, 128), F32),
    ]
    need = max(size_of(outs) + size_of(scratch) + (8 << 20), GRANT)
    return pl.pallas_call(
        functools.partial(main_kernel, shape),
        in_specs=[SMEM, HBM, VMEM] + [ANY] * len(pieces),
        out_specs=[VMEM] * 4,
        out_shape=[jax.ShapeDtypeStruct(s, t) for s, t in outs],
        scratch_shapes=[pltpu.VMEM(s, t) for s, t in scratch]
        + [pltpu.SemaphoreType.DMA((RING,)), pltpu.SemaphoreType.DMA((len(pieces),))],
        compiler_params=pltpu.CompilerParams(vmem_limit_bytes=need),
        cost_estimate=pl.CostEstimate(
            flops=8 * counts.size * rank,
            bytes_accessed=counts.size * 2,
            transcendentals=counts.size,
        ),
        name="terms",
    )(ids, counts, hours, *pieces)


def call(kernel, name, ins, outs, specs=None, scratch=()):
    shapes = [(x.shape, x.dtype) for x in ins] + list(outs) + list(scratch)
    return pl.pallas_call(
        kernel,
        in_specs=specs or [VMEM] * len(ins),
        out_specs=[VMEM] * len(outs),
        out_shape=[jax.ShapeDtypeStruct(s, t) for s, t in outs],
        scratch_shapes=[pltpu.VMEM(s, t) for s, t in scratch],
        compiler_params=pltpu.CompilerParams(vmem_limit_bytes=size_of(shapes) + (4 << 20)),
        name=name,
    )(*ins)


def shares(rows, rank, ways):
    return [((rows, rank), F32)] + [((rows, rank), BF16)] * (ways - 1)


def run_cut(ways, acc, got, name):
    rows, rank = got.shape[0] // ways, got.shape[1]

    def kernel(acc, got, *outs):
        for m in range(ways):
            at = pl.ds(m * rows, rows)
            outs[m][...] = (acc[at, :] + got[at, :].astype(F32)).astype(outs[m].dtype)

    return call(kernel, name, (acc, got), shares(rows, rank, ways))


def total(refs):
    acc = refs[0][...]
    for r in refs[1:]:
        acc = acc + r[...].astype(F32)
    return acc


def run_grp(hour_part, depth, ids, parts):
    rows, rank = parts[0].shape
    ways = len(parts)
    each, dst_rows = hour_part // depth, (rows - hour_part) // depth

    def kernel(ids, *refs):
        outs, acc = refs[ways:-1], refs[-1]
        z = ids[0] >> 1
        acc[...] = total(refs[:ways])
        for m in range(depth):
            kind = outs[m].dtype
            at = pl.multiple_of((z ^ m) * each, each)
            outs[m][pl.ds(0, each), :] = acc[pl.ds(at, each), :].astype(kind)
            at = hour_part + m * dst_rows
            outs[m][pl.ds(each, dst_rows), :] = acc[pl.ds(at, dst_rows), :].astype(kind)

    return call(
        kernel,
        "grp_sum",
        (ids, *parts),
        shares(each + dst_rows, rank, depth),
        specs=[SMEM] + [VMEM] * ways,
        scratch=[((rows, rank), F32)],
    )


def run_z(hd_parts, s_parts, hour_rows):
    n = len(hd_parts)
    rows, rank = hd_parts[0].shape

    def kernel(*refs):
        hour, dst, src = refs[2 * n :]
        acc = total(refs[:n]) * (1.0 / SIDE)
        hour[...] = acc[:hour_rows].astype(BF16)
        dst[...] = acc[hour_rows:].astype(BF16)
        src[...] = total(refs[n : 2 * n]) * (1.0 / SIDE)

    outs = [((hour_rows, rank), BF16), ((rows - hour_rows, rank), BF16), (s_parts[0].shape, F32)]
    return call(kernel, "z_sum", (*hd_parts, *s_parts), outs)


def run_join(parts):
    rows = [p.shape[0] for p in parts]

    def kernel(*refs):
        at = 0
        for ref, n in zip(refs[:-1], rows):
            refs[-1][at : at + n, :] = ref[...]
            at += n

    return call(kernel, "join", parts, [((sum(rows), parts[0].shape[1]), BF16)])[0]


def run_place(sizes, hour_rows, ids, parts, so_far, dst_rows=0, passed=()):
    grps, devs = sizes
    depth = devs // 2
    arrays = [p for p, _, _ in parts]
    rank = arrays[0].shape[1]
    part = hour_rows // (2 * grps)
    rows = part // depth
    n = len(parts)
    more = [] if so_far is None else [so_far]

    def kernel(ids, *refs):
        outs = refs[n + len(more) : -2]
        for i in passed:
            outs[-1][...] = refs[i][...]
        stage, sem = refs[-2:]
        core, z, grp = ids[0] & 1, ids[0] >> 1, ids[1]
        copies = []
        for i, (_, far, m) in enumerate(parts):
            if dst_rows and not far:
                at = pl.multiple_of((grp ^ m) * dst_rows, dst_rows)
                outs[1][pl.ds(at, dst_rows), :] = refs[i][pl.ds(part, dst_rows), :].astype(F32)
            if far is None:
                continue
            for k in range(depth):
                at = pl.multiple_of((z ^ k) * rows, rows)
                stage[i, pl.ds(at, rows), :] = refs[i][pl.ds(k * rows, rows), :].astype(F32)
            home = pl.multiple_of(((core ^ far) * grps + (grp ^ m)) * part, part)
            copies.append(
                pltpu.make_async_copy(stage.at[i], outs[0].at[pl.ds(home, part)], sem.at[i])
            )
            copies[-1].start()
        for copy in copies:
            copy.wait()

    outs = [jax.ShapeDtypeStruct((hour_rows, rank), F32)]
    if dst_rows:
        outs.append(jax.ShapeDtypeStruct((grps * dst_rows, rank), F32))
    outs += [jax.ShapeDtypeStruct(arrays[i].shape, BF16) for i in passed]
    scratch = [((n, part, rank), F32)]
    need = size_of([(p.shape, p.dtype) for p in arrays + outs[1:]] + scratch) + (4 << 20)
    return pl.pallas_call(
        kernel,
        in_specs=[SMEM] + [VMEM] * n + [HBM] * len(more),
        out_specs=[HBM] + [VMEM] * (len(outs) - 1),
        out_shape=outs,
        scratch_shapes=[pltpu.VMEM(s, t) for s, t in scratch] + [pltpu.SemaphoreType.DMA((n,))],
        input_output_aliases={n + 1: 0} if more else {},
        compiler_params=pltpu.CompilerParams(vmem_limit_bytes=need),
        name="place",
    )(ids, *arrays, *more)


def per_device(
    sizes,
    counts,
    src_factor,
    dst_factor,
    hour_factor,
    src_owner,
    src_slot,
    dst_owner,
    dst_slot,
    hour_block,
):
    grps, devs = sizes
    depth = devs // 2
    local = src_factor.shape[0]
    hour_rows = hour_factor.shape[0]
    me = lax.axis_index("dev").astype(jnp.int32)
    grp = lax.axis_index("grp").astype(jnp.int32)
    place = jnp.stack([me, grp] + [me * 0] * 6)
    ids = jnp.concatenate(
        [place, src_owner[:, 0], src_slot, dst_owner[:, 0], dst_slot, hour_block]
    )
    dst_part = local // grps
    dst_own = lax.dynamic_slice_in_dim(dst_factor, grp * dst_part, dst_part, 0)
    dst_z = [dst_own] + [swap(dst_own, "dev", devs, 2 * m) for m in range(1, depth)]
    src_z = [swap(src_factor, "dev", devs, 2 * m) for m in range(2, depth)]
    picked, src_same = run_pick(counts.shape[0], ids, hour_factor, src_factor)
    src_z = [src_factor, swap(src_same, "dev", devs, 2)] + src_z
    dst_here = run_join(dst_z)
    dsts = [dst_here] + [swap(dst_here, "grp", grps, m) for m in range(1, grps)]
    near = run_join(src_z + dsts)
    far = swap(near, "dev", devs, 1)
    shape = (grps, devs, local, hour_rows)
    hd_acc, s_acc, hd_send, s_send = run_main(shape, ids, counts, picked, [near, far])

    def exchange(parts, axis, size, step):
        return [parts[0]] + [swap(x, axis, size, step * m) for m, x in enumerate(parts) if m]

    hd_got = swap(hd_send, "dev", devs, 1)
    s_got = swap(s_send, "dev", devs, 1)
    hd = run_cut(grps, hd_acc, hd_got, "core_hours_dst")
    srcs = run_cut(depth, s_acc, s_got, "core_src")
    hour_part = hour_rows // (2 * grps)
    hd = run_grp(hour_part, depth, ids, exchange(hd, "grp", grps, 1))
    srcs = exchange(srcs, "dev", devs, 2)
    hour_each = hour_part // depth
    hour, dst, grad_src = run_z(exchange(hd, "dev", devs, 2), srcs, hour_each)
    back = [hour] + [swap(hour, "dev", devs, 2 * m) for m in range(1, depth)]
    joined = run_join(back + [dst])
    near = [joined] + [swap(joined, "grp", grps, m) for m in range(1, grps)]
    parts = [(x, 0, m) for m, x in enumerate(near)]
    parts += [(swap(x, "dev", devs, 1), 1, m) for m, x in enumerate(near)]
    grad_hour, grad_dst = run_place(sizes, hour_rows, ids, parts, None, dst_part)
    return grad_src, grad_dst, grad_hour


def solution(mesh):
    in_specs = (
        P(("grp", "dev"), None, None),
        P(("grp", "dev"), None),
        P("dev", None),
        P(),
        P(("grp", "dev"), None),
        P(("grp", "dev")),
        P(("grp", "dev"), None),
        P(("grp", "dev")),
        P(("grp", "dev")),
    )
    out_specs = (P(("grp", "dev"), None), P("dev", None), P())
    return jax.shard_map(
        functools.partial(per_device, mesh_sizes(mesh)),
        mesh=mesh,
        in_specs=in_specs,
        out_specs=out_specs,
        check_vma=False,
    )
```

```python
import functools

import jax
import jax.numpy as jnp
from jax import lax
from jax.experimental import pallas as pl
from jax.experimental.pallas import tpu as pltpu
from jax.sharding import PartitionSpec as P

F32 = jnp.float32
BF16 = jnp.bfloat16
SIDE = 64
RING = 8
OUT_RING = 4
PITCH = 72
GRANT = 36 << 20
SRC_GRANT = 44 << 20
SLOW = 10**11

VMEM = pl.BlockSpec(memory_space=pltpu.VMEM)
SMEM = pl.BlockSpec(memory_space=pltpu.SMEM)
ANY = pl.BlockSpec(memory_space=pl.ANY)
HBM = pl.BlockSpec(memory_space=pltpu.HBM)


def mesh_sizes(mesh):
    return mesh.shape["grp"], mesh.shape["dev"]


def swap(x, axis, size, mask):
    return lax.ppermute(x, axis, [(i, i ^ mask) for i in range(size)])


def block_terms(count, a, b, c, resid_out, cube, even, odd):
    rank = a.shape[1]
    turned, pairs_ab = [], []
    for g in range(SIDE // 4):
        b4 = b[g * 4 : g * 4 + 4]
        bc = (b4[:, None, :] * c[None, :, :]).reshape(4 * SIDE, rank)
        ab = (b4[:, None, :] * a[None, :, :]).reshape(4 * SIDE, rank)
        theta = lax.dot_general(a, bc, (((1,), (1,)), ((), ())), preferred_element_type=F32)
        wide = jnp.exp(theta) - count[:, g * 256 : (g + 1) * 256].astype(F32)
        for p in range(2):
            cube[pl.ds((g * 2 + p) * PITCH, SIDE), :] = wide[:, p * 128 : (p + 1) * 128]
        resid = wide.astype(BF16)
        flip = resid.T
        turned += [flip[q * SIDE : (q + 1) * SIDE] for q in range(4)]
        resid_out[:, g * 256 : (g + 1) * 256] = resid
        pairs_ab.append(ab)
    term_c = jnp.dot(
        jnp.concatenate(turned, axis=1),
        jnp.concatenate(pairs_ab, axis=0),
        preferred_element_type=F32,
    )
    low = lax.broadcasted_iota(jnp.int32, (SIDE // 2, 128), 1) < SIDE
    rows, pairs_ac = [], []
    for g in range(SIDE // 4):
        x = [cube[pl.ds(g * 4 + q, SIDE // 2, stride=PITCH), :] for q in range(4)]
        y = [pltpu.roll(v, SIDE, 1) for v in x]
        evens = [jnp.where(low, x[0], y[1]), jnp.where(low, x[2], y[3])]
        odds = [jnp.where(low, y[0], x[1]), jnp.where(low, y[2], x[3])]
        both = [jnp.concatenate(evens, axis=1), jnp.concatenate(odds, axis=1)]
        rows.append(jnp.concatenate(both, axis=0).astype(BF16))
        pairs_ac.append((a[g * 4 : g * 4 + 4][:, None, :] * c[None, :, :]).reshape(4 * SIDE, rank))
    mixed = jnp.dot(
        jnp.concatenate(rows, axis=1),
        jnp.concatenate(pairs_ac, axis=0),
        preferred_element_type=F32,
    )
    half = SIDE // 2
    for u in range(2):
        even[pl.ds(u, half, stride=2), :] = mixed[u * half : (u + 1) * half, :128]
        odd[pl.ds(u, half, stride=2), :] = mixed[u * half : (u + 1) * half, 128:]
    term_b = jnp.concatenate([even[...], odd[...]], axis=1)
    return term_b, term_c


def run_pick(blocks, ids, hours, own):
    grant = 4 * blocks * SIDE * hours.shape[1] + 4 * own.size + (2 << 20)
    rank = hours.shape[1]

    def kernel(ids, hours, own, out, same, sem):
        copies = []
        for t in range(blocks):
            at = pl.multiple_of(ids[8 + 4 * blocks + t] * SIDE, SIDE)
            copies.append(
                pltpu.make_async_copy(
                    hours.at[pl.ds(at, SIDE)], out.at[pl.ds(t * SIDE, SIDE)], sem.at[t]
                )
            )
            copies[-1].start()
        same[...] = own[...]
        for copy in copies:
            copy.wait()

    return pl.pallas_call(
        kernel,
        in_specs=[SMEM, HBM, VMEM],
        out_specs=[VMEM, VMEM],
        out_shape=[
            jax.ShapeDtypeStruct((blocks * SIDE, rank), BF16),
            jax.ShapeDtypeStruct(own.shape, BF16),
        ],
        scratch_shapes=[pltpu.SemaphoreType.DMA((blocks,))],
        compiler_params=pltpu.CompilerParams(vmem_limit_bytes=grant),
        name="pick_hours",
    )(ids, hours, own)


def main_kernel(shape, ids, counts, hours, near, far, *refs):
    grps, devs, local, hour_rows = shape
    depth = devs // 2
    hd_acc, hd_send, b_rows, resids, *refs = refs
    ring, resid_ring, table, cube, even, odd, ring_sem, resid_sem, in_sem = refs
    blocks = counts.shape[0]
    hour_part = hour_rows // (2 * grps)
    hour_blocks = hour_part // SIDE
    dst_part = local // grps
    part = hour_part + depth * dst_part
    half = depth * local
    base = 8

    def fetch(t):
        slot = lax.rem(t, RING)
        return pltpu.make_async_copy(counts.at[t], ring.at[slot], ring_sem.at[slot])

    def put(t):
        slot = lax.rem(t, OUT_RING)
        return pltpu.make_async_copy(resid_ring.at[slot], resids.at[t], resid_sem.at[slot])

    for t in range(min(RING, blocks)):
        fetch(t).start()
    loads = [
        pltpu.make_async_copy(x, table.at[pl.ds(m * 2 * half, 2 * half)], in_sem.at[m])
        for m, x in enumerate((near, far))
    ]
    for load in loads:
        load.start()
    hd_acc[...] = jnp.zeros_like(hd_acc)
    for load in loads:
        load.wait()
    me, grp = ids[0], ids[1]
    core = me & 1

    def visit(t, carry):
        src_from = ids[base + t] ^ me
        src_slot = ids[base + blocks + t]
        dst_from = ids[base + 2 * blocks + t] ^ me
        dst_slot = ids[base + 3 * blocks + t]
        hour = ids[base + 4 * blocks + t]
        row = dst_slot * SIDE
        turn = (row // dst_part) ^ grp
        inner = (dst_from >> 1) * dst_part + row % dst_part
        a_at = (src_from & 1) * (2 * half) + (src_from >> 1) * local + src_slot * SIDE
        a_at = pl.multiple_of(a_at, SIDE)
        b_at = (dst_from & 1) * (2 * half) + half + turn * (depth * dst_part) + inner
        b_at = pl.multiple_of(b_at, SIDE)
        here = pl.ds(pl.multiple_of(t * SIDE, SIDE), SIDE)
        b = table[pl.ds(b_at, SIDE), :]
        b_rows[here, :] = b
        fetch(t).wait()

        @pl.when(t >= OUT_RING)
        def _():
            put(t - OUT_RING).wait()

        term_b, term_c = block_terms(
            ring.at[lax.rem(t, RING)],
            table[pl.ds(a_at, SIDE), :],
            b,
            hours[here, :],
            resid_ring.at[lax.rem(t, OUT_RING)],
            cube,
            even,
            odd,
        )
        d_at = ((dst_from & 1) * grps + turn) * part + hour_part + inner
        home = hour // hour_blocks
        h_at = (((home // grps) ^ core) * grps + ((home % grps) ^ grp)) * part
        h_at = h_at + (hour % hour_blocks) * SIDE
        hd_acc[pl.ds(pl.multiple_of(d_at, SIDE), SIDE), :] += term_b
        hd_acc[pl.ds(pl.multiple_of(h_at, SIDE), SIDE), :] += term_c
        put(t).start()

        @pl.when(t + RING < blocks)
        def _():
            fetch(t + RING).start()

        return carry

    lax.fori_loop(0, blocks, visit, 0)
    hd_half = grps * part
    hd_send[...] = hd_acc[pl.ds(hd_half, hd_half), :].astype(BF16)
    for t in range(max(0, blocks - OUT_RING), blocks):
        put(t).wait()


def src_kernel(shape, first, last, ids, resids, b_rows, hours, after, *refs):
    devs, local = shape
    depth = devs // 2
    fresh = first == 0
    blocks = resids.shape[0]
    refs = refs if fresh else refs[1:]
    s_acc, *sends, ring, sem = refs
    me, base = ids[0], 8

    def fetch(t):
        slot = lax.rem(t - first, RING)
        return pltpu.make_async_copy(resids.at[t], ring.at[slot], sem.at[slot])

    for t in range(first, min(first + RING, last)):
        fetch(t).start()
    if fresh:
        s_acc[...] = jnp.zeros_like(s_acc)

    def visit(t, carry):
        src_from = ids[base + t] ^ me
        src_slot = ids[base + blocks + t]
        z, order, steps = src_from >> 1, 0, depth // 2
        while steps:
            order = order + (z & 1) * steps
            z, steps = z >> 1, steps // 2
        s_at = ((src_from & 1) * depth + order) * local + src_slot * SIDE
        s_at = pl.multiple_of(s_at, SIDE)
        here = pl.ds(pl.multiple_of(t * SIDE, SIDE), SIDE)
        b, c = b_rows[here, :], hours[here, :]
        fetch(t).wait()
        resid = ring[lax.rem(t - first, RING)]
        pairs = [
            (b[g * 4 : g * 4 + 4][:, None, :] * c[None, :, :]).reshape(4 * SIDE, b.shape[1])
            for g in range(SIDE // 4)
        ]
        terms = []
        for at in range(0, b.shape[1], 128):
            columns = jnp.concatenate([p[:, at : at + 128] for p in pairs], axis=0)
            terms.append(jnp.dot(resid, columns, preferred_element_type=F32))
        s_acc[pl.ds(s_at, SIDE), :] += jnp.concatenate(terms, axis=1)

        @pl.when(t + RING < last)
        def _():
            fetch(t + RING).start()

        return carry

    lax.fori_loop(first, last, visit, 0)
    for send in sends:
        send[...] = s_acc[pl.ds(depth * local, depth * local), :].astype(BF16)


def size_of(shapes):
    return sum(jnp.dtype(t).itemsize * functools.reduce(lambda x, y: x * y, s) for s, t in shapes)


def run_main(shape, ids, counts, hours, near, far):
    grps, devs, local, hour_rows = shape
    rank = hours.shape[1]
    hd_rows = hour_rows + devs * local
    outs = [
        ((hd_rows, rank), F32),
        ((hd_rows // 2, rank), BF16),
        (hours.shape, BF16),
    ]
    scratch = [
        ((RING,) + counts.shape[1:], BF16),
        ((OUT_RING,) + counts.shape[1:], BF16),
        ((devs * 2 * local, rank), BF16),
        ((SIDE // 2 * PITCH, 128), F32),
        ((SIDE, 128), F32),
        ((SIDE, 128), F32),
    ]
    need = max(size_of(outs) + size_of(scratch) + (8 << 20), GRANT)
    return pl.pallas_call(
        functools.partial(main_kernel, shape),
        in_specs=[SMEM, HBM, VMEM, ANY, ANY],
        out_specs=[VMEM] * 3 + [HBM],
        out_shape=[jax.ShapeDtypeStruct(s, t) for s, t in outs]
        + [jax.ShapeDtypeStruct(counts.shape, BF16)],
        scratch_shapes=[pltpu.VMEM(s, t) for s, t in scratch]
        + [
            pltpu.SemaphoreType.DMA((RING,)),
            pltpu.SemaphoreType.DMA((OUT_RING,)),
            pltpu.SemaphoreType.DMA((2,)),
        ],
        compiler_params=pltpu.CompilerParams(vmem_limit_bytes=need),
        cost_estimate=pl.CostEstimate(
            flops=6 * counts.size * rank,
            bytes_accessed=counts.size * 4,
            transcendentals=counts.size,
        ),
        name="hour_dst_terms",
    )(ids, counts, hours, near, far)


def run_src(shape, first, last, ids, resids, b_rows, hours, after, s_acc=None):
    devs, local = shape
    rank = hours.shape[1]
    blocks, rows, columns = resids.shape
    more = [] if s_acc is None else [s_acc]
    outs = [((devs * local, rank), F32)]
    if last == blocks:
        outs.append(((devs * local // 2, rank), BF16))
    need = size_of(outs) + size_of([((RING, rows, columns), BF16)]) + (8 << 20)
    each = rows * columns
    return pl.pallas_call(
        functools.partial(src_kernel, shape, first, last),
        in_specs=[SMEM, HBM, VMEM, VMEM, ANY] + [VMEM] * len(more),
        out_specs=[VMEM] * len(outs),
        out_shape=[jax.ShapeDtypeStruct(s, t) for s, t in outs],
        scratch_shapes=[
            pltpu.VMEM((RING, rows, columns), BF16),
            pltpu.SemaphoreType.DMA((RING,)),
        ],
        input_output_aliases={5: 0} if more else {},
        compiler_params=pltpu.CompilerParams(vmem_limit_bytes=max(need, SRC_GRANT)),
        cost_estimate=pl.CostEstimate(
            flops=8 * (last - first) * each * rank,
            bytes_accessed=(last - first) * each * 2,
            transcendentals=0,
        ),
        name="src_terms",
    )(ids, resids, b_rows, hours, after, *more)


def call(kernel, name, ins, outs, specs=None, scratch=(), weight=0):
    shapes = [(x.shape, x.dtype) for x in ins] + list(outs) + list(scratch)
    return pl.pallas_call(
        kernel,
        in_specs=specs or [VMEM] * len(ins),
        out_specs=[VMEM] * len(outs),
        out_shape=[jax.ShapeDtypeStruct(s, t) for s, t in outs],
        scratch_shapes=[pltpu.VMEM(s, t) for s, t in scratch],
        compiler_params=pltpu.CompilerParams(vmem_limit_bytes=size_of(shapes) + (4 << 20)),
        cost_estimate=pl.CostEstimate(
            flops=weight, bytes_accessed=size_of(shapes), transcendentals=0
        ),
        name=name,
    )(*ins)


def shares(rows, rank, ways):
    return [((rows, rank), F32)] + [((rows, rank), BF16)] * (ways - 1)


def run_cut(ways, acc, got, after):
    rows, rank = got.shape[0] // ways, got.shape[1]

    def kernel(acc, got, after, *outs):
        for m in range(ways):
            at = pl.ds(m * rows, rows)
            outs[m][...] = (acc[at, :] + got[at, :].astype(F32)).astype(outs[m].dtype)
        outs[ways][...] = jnp.zeros_like(outs[ways])

    outs = shares(rows, rank, ways) + [((8, 128), F32)]
    return call(kernel, "core_hours_dst", (acc, got, after), outs, specs=[VMEM, VMEM, ANY])


def halve(keep, got, stay, send):
    rows = got.shape[0]
    half = rows // 2
    stay[...] = keep[pl.ds(0, half), :] + got[pl.ds(0, half), :].astype(F32)
    at = pl.ds(half, half)
    send[...] = (keep[at, :] + got[at, :].astype(F32)).astype(BF16)


def halves(got):
    rows, rank = got.shape
    return [((rows // 2, rank), F32), ((rows // 2, rank), BF16)]


def run_halve(keep, got):
    return call(halve, "src_half", (keep, got), halves(got))


def total(refs):
    acc = refs[0][...]
    for r in refs[1:]:
        acc = acc + r[...].astype(F32)
    return acc


def run_grp(hour_part, depth, ids, parts):
    rows, rank = parts[0].shape
    ways = len(parts)
    each, dst_rows = hour_part // depth, (rows - hour_part) // depth

    def kernel(ids, *refs):
        outs, acc = refs[ways:-1], refs[-1]
        z = ids[0] >> 1
        acc[...] = total(refs[:ways])
        for m in range(depth):
            kind = outs[m].dtype
            at = pl.multiple_of((z ^ m) * each, each)
            outs[m][pl.ds(0, each), :] = acc[pl.ds(at, each), :].astype(kind)
            at = hour_part + m * dst_rows
            outs[m][pl.ds(each, dst_rows), :] = acc[pl.ds(at, dst_rows), :].astype(kind)

    return call(
        kernel,
        "grp_sum",
        (ids, *parts),
        shares(each + dst_rows, rank, depth),
        specs=[SMEM] + [VMEM] * ways,
        scratch=[((rows, rank), F32)],
        weight=SLOW,
    )


def run_z(hd_parts, hour_rows, s_acc, s_got):
    n = len(hd_parts)
    rows, rank = hd_parts[0].shape

    def kernel(*refs):
        keep, got, hour, dst, stay, send = refs[n:]
        halve(keep, got, stay, send)
        acc = total(refs[:n]) * (1.0 / SIDE)
        hour[...] = acc[:hour_rows].astype(BF16)
        dst[...] = acc[hour_rows:].astype(BF16)

    outs = [((hour_rows, rank), BF16), ((rows - hour_rows, rank), BF16)] + halves(s_got)
    return call(kernel, "z_sum", (*hd_parts, s_acc, s_got), outs)


def run_join(parts, keep=None, got=None):
    rows = [p.shape[0] for p in parts]
    n = len(parts)
    outs = [((sum(rows), parts[0].shape[1]), BF16)]
    if got is None:
        ins = tuple(parts)
    else:
        ins = (*parts, keep, got)
        outs += halves(got)

    def kernel(*refs):
        if got is not None:
            halve(refs[n], refs[n + 1], refs[-2], refs[-1])
        out, at = refs[len(ins)], 0
        for ref, n_rows in zip(refs, rows):
            out[at : at + n_rows, :] = ref[...]
            at += n_rows

    return call(kernel, "join", ins, outs)


def run_src_sum(keep, got, joined):
    def kernel(keep, got, joined, out, same):
        out[...] = (keep[...] + got[...].astype(F32)) * (1.0 / SIDE)
        same[...] = joined[...]

    outs = [(keep.shape, F32), (joined.shape, BF16)]
    return call(kernel, "src_sum", (keep, got, joined), outs)


def run_place(sizes, hour_rows, ids, parts, so_far, dst_rows=0, passed=()):
    grps, devs = sizes
    depth = devs // 2
    arrays = [p for p, _, _ in parts]
    rank = arrays[0].shape[1]
    part = hour_rows // (2 * grps)
    rows = part // depth
    n = len(parts)
    more = [] if so_far is None else [so_far]

    def kernel(ids, *refs):
        outs = refs[n + len(more) : -2]
        for i in passed:
            outs[-1][...] = refs[i][...]
        stage, sem = refs[-2:]
        core, z, grp = ids[0] & 1, ids[0] >> 1, ids[1]
        copies = []
        for i, (_, far, m) in enumerate(parts):
            if dst_rows and not far:
                at = pl.multiple_of((grp ^ m) * dst_rows, dst_rows)
                outs[1][pl.ds(at, dst_rows), :] = refs[i][pl.ds(part, dst_rows), :].astype(F32)
            if far is None:
                continue
            for k in range(depth):
                at = pl.multiple_of((z ^ k) * rows, rows)
                stage[i, pl.ds(at, rows), :] = refs[i][pl.ds(k * rows, rows), :].astype(F32)
            home = pl.multiple_of(((core ^ far) * grps + (grp ^ m)) * part, part)
            copies.append(
                pltpu.make_async_copy(stage.at[i], outs[0].at[pl.ds(home, part)], sem.at[i])
            )
            copies[-1].start()
        for copy in copies:
            copy.wait()

    outs = [jax.ShapeDtypeStruct((hour_rows, rank), F32)]
    if dst_rows:
        outs.append(jax.ShapeDtypeStruct((grps * dst_rows, rank), F32))
    outs += [jax.ShapeDtypeStruct(arrays[i].shape, BF16) for i in passed]
    scratch = [((n, part, rank), F32)]
    need = size_of([(p.shape, p.dtype) for p in arrays + outs[1:]] + scratch) + (4 << 20)
    return pl.pallas_call(
        kernel,
        in_specs=[SMEM] + [VMEM] * n + [HBM] * len(more),
        out_specs=[HBM] + [VMEM] * (len(outs) - 1),
        out_shape=outs,
        scratch_shapes=[pltpu.VMEM(s, t) for s, t in scratch] + [pltpu.SemaphoreType.DMA((n,))],
        input_output_aliases={n + 1: 0} if more else {},
        compiler_params=pltpu.CompilerParams(vmem_limit_bytes=need),
        name="place",
    )(ids, *arrays, *more)


def per_device(
    sizes,
    counts,
    src_factor,
    dst_factor,
    hour_factor,
    src_owner,
    src_slot,
    dst_owner,
    dst_slot,
    hour_block,
):
    grps, devs = sizes
    depth = devs // 2
    local = src_factor.shape[0]
    hour_rows = hour_factor.shape[0]
    me = lax.axis_index("dev").astype(jnp.int32)
    grp = lax.axis_index("grp").astype(jnp.int32)
    place = jnp.stack([me, grp] + [me * 0] * 6)
    ids = jnp.concatenate(
        [place, src_owner[:, 0], src_slot, dst_owner[:, 0], dst_slot, hour_block]
    )
    dst_part = local // grps
    dst_own = lax.dynamic_slice_in_dim(dst_factor, grp * dst_part, dst_part, 0)
    dst_z = [dst_own] + [swap(dst_own, "dev", devs, 2 * m) for m in range(1, depth)]
    src_z = [swap(src_factor, "dev", devs, 2 * m) for m in range(2, depth)]
    blocks = counts.shape[0]
    picked, src_same = run_pick(blocks, ids, hour_factor, src_factor)
    src_z = [src_factor, swap(src_same, "dev", devs, 2)] + src_z
    dst_here = run_join(dst_z)[0]
    dsts = [dst_here] + [swap(dst_here, "grp", grps, m) for m in range(1, grps)]
    near = run_join(src_z + dsts)[0]
    far = swap(near, "dev", devs, 1)
    shape = (grps, devs, local, hour_rows)
    hd_acc, hd_send, b_rows, resids = run_main(shape, ids, counts, picked, near, far)

    def exchange(parts, axis, size, step):
        return [parts[0]] + [swap(x, axis, size, step * m) for m, x in enumerate(parts) if m]

    hd_got = swap(hd_send, "dev", devs, 1)
    src = functools.partial(run_src, (devs, local))
    early = blocks // 4
    s_acc = src(0, early, ids, resids, b_rows, picked, hd_send)[0]
    *hd, cut_done = run_cut(grps, hd_acc, hd_got, s_acc)
    cut_done = swap(cut_done, "dev", devs, 1)
    s_acc, s_send = src(early, blocks, ids, resids, b_rows, picked, cut_done, s_acc)
    s_got = swap(s_send, "dev", devs, 1)
    hour_part = hour_rows // (2 * grps)
    hd = run_grp(hour_part, depth, ids, exchange(hd, "grp", grps, 1))
    hour_each = hour_part // depth
    hour, dst, s_keep, s_send = run_z(exchange(hd, "dev", devs, 2), hour_each, s_acc, s_got)
    s_got = swap(s_send, "dev", devs, 2)
    back = [hour] + [swap(hour, "dev", devs, 2 * m) for m in range(1, depth)]
    joined, s_keep, s_send = run_join(back + [dst], s_keep, s_got)
    step = 4
    s_got = swap(s_send, "dev", devs, step)
    while 2 * step < devs:
        s_keep, s_send = run_halve(s_keep, s_got)
        step *= 2
        s_got = swap(s_send, "dev", devs, step)
    grad_src, same = run_src_sum(s_keep, s_got, joined)
    near = [joined] + [swap(joined, "grp", grps, m) for m in range(1, grps)]
    parts = [(x, 0, m) for m, x in enumerate(near)]
    parts += [(swap(x, "dev", devs, 1), 1, m) for m, x in enumerate([same] + near[1:])]
    grad_hour, grad_dst = run_place(sizes, hour_rows, ids, parts, None, dst_part)
    return grad_src, grad_dst, grad_hour


def solution(mesh):
    in_specs = (
        P(("grp", "dev"), None, None),
        P(("grp", "dev"), None),
        P("dev", None),
        P(),
        P(("grp", "dev"), None),
        P(("grp", "dev")),
        P(("grp", "dev"), None),
        P(("grp", "dev")),
        P(("grp", "dev")),
    )
    out_specs = (P(("grp", "dev"), None), P("dev", None), P())
    return jax.shard_map(
        functools.partial(per_device, mesh_sizes(mesh)),
        mesh=mesh,
        in_specs=in_specs,
        out_specs=out_specs,
        check_vma=False,
    )
```

```python
import functools

import jax
import jax.numpy as jnp
from jax import lax
from jax.experimental import pallas as pl
from jax.experimental.pallas import tpu as pltpu
from jax.sharding import PartitionSpec as P

F32 = jnp.float32
BF16 = jnp.bfloat16
SIDE = 64
RING = 8
OUT_RING = 4
PITCH = 72
GRANT = 36 << 20
SRC_GRANT = 44 << 20
SLOW = 10**11

VMEM = pl.BlockSpec(memory_space=pltpu.VMEM)
SMEM = pl.BlockSpec(memory_space=pltpu.SMEM)
ANY = pl.BlockSpec(memory_space=pl.ANY)
HBM = pl.BlockSpec(memory_space=pltpu.HBM)


def mesh_sizes(mesh):
    return mesh.shape["grp"], mesh.shape["dev"]


def swap(x, axis, size, mask):
    return lax.ppermute(x, axis, [(i, i ^ mask) for i in range(size)])


def block_terms(count, a, b, c, resid_out, cube, even, odd):
    rank = a.shape[1]
    turned, pairs_ab = [], []
    for g in range(SIDE // 4):
        b4 = b[g * 4 : g * 4 + 4]
        bc = (b4[:, None, :] * c[None, :, :]).reshape(4 * SIDE, rank)
        ab = (b4[:, None, :] * a[None, :, :]).reshape(4 * SIDE, rank)
        theta = lax.dot_general(a, bc, (((1,), (1,)), ((), ())), preferred_element_type=F32)
        wide = jnp.exp(theta) - count[:, g * 256 : (g + 1) * 256].astype(F32)
        for p in range(2):
            cube[pl.ds((g * 2 + p) * PITCH, SIDE), :] = wide[:, p * 128 : (p + 1) * 128]
        resid = wide.astype(BF16)
        flip = resid.T
        turned += [flip[q * SIDE : (q + 1) * SIDE] for q in range(4)]
        resid_out[:, g * 256 : (g + 1) * 256] = resid
        pairs_ab.append(ab)
    term_c = jnp.dot(
        jnp.concatenate(turned, axis=1),
        jnp.concatenate(pairs_ab, axis=0),
        preferred_element_type=F32,
    )
    low = lax.broadcasted_iota(jnp.int32, (SIDE // 2, 128), 1) < SIDE
    rows, pairs_ac = [], []
    for g in range(SIDE // 4):
        x = [cube[pl.ds(g * 4 + q, SIDE // 2, stride=PITCH), :] for q in range(4)]
        y = [pltpu.roll(v, SIDE, 1) for v in x]
        evens = [jnp.where(low, x[0], y[1]), jnp.where(low, x[2], y[3])]
        odds = [jnp.where(low, y[0], x[1]), jnp.where(low, y[2], x[3])]
        both = [jnp.concatenate(evens, axis=1), jnp.concatenate(odds, axis=1)]
        rows.append(jnp.concatenate(both, axis=0).astype(BF16))
        pairs_ac.append((a[g * 4 : g * 4 + 4][:, None, :] * c[None, :, :]).reshape(4 * SIDE, rank))
    mixed = jnp.dot(
        jnp.concatenate(rows, axis=1),
        jnp.concatenate(pairs_ac, axis=0),
        preferred_element_type=F32,
    )
    half = SIDE // 2
    for u in range(2):
        even[pl.ds(u, half, stride=2), :] = mixed[u * half : (u + 1) * half, :128]
        odd[pl.ds(u, half, stride=2), :] = mixed[u * half : (u + 1) * half, 128:]
    term_b = jnp.concatenate([even[...], odd[...]], axis=1)
    return term_b, term_c


def run_pick(blocks, ids, hours):
    rank = hours.shape[1]

    def kernel(ids, hours, out, sem):
        copies = []
        for t in range(blocks):
            at = pl.multiple_of(ids[8 + 4 * blocks + t] * SIDE, SIDE)
            copies.append(
                pltpu.make_async_copy(
                    hours.at[pl.ds(at, SIDE)], out.at[pl.ds(t * SIDE, SIDE)], sem.at[t]
                )
            )
            copies[-1].start()
        for copy in copies:
            copy.wait()

    grant = 4 * blocks * SIDE * rank + (2 << 20)
    return pl.pallas_call(
        kernel,
        in_specs=[SMEM, HBM],
        out_specs=VMEM,
        out_shape=jax.ShapeDtypeStruct((blocks * SIDE, rank), BF16),
        scratch_shapes=[pltpu.SemaphoreType.DMA((blocks,))],
        compiler_params=pltpu.CompilerParams(vmem_limit_bytes=grant),
        cost_estimate=pl.CostEstimate(flops=SLOW // 10, bytes_accessed=0, transcendentals=0),
        name="pick_hours",
    )(ids, hours)


def main_kernel(shape, ids, counts, hours, near, far, *refs):
    grps, devs, local, hour_rows = shape
    depth = devs // 2
    hd_acc, hd_send, b_rows, resids, *refs = refs
    ring, resid_ring, table, cube, even, odd, ring_sem, resid_sem, in_sem = refs
    blocks = counts.shape[0]
    hour_part = hour_rows // (2 * grps)
    hour_blocks = hour_part // SIDE
    dst_part = local // grps
    part = hour_part + depth * dst_part
    half = depth * local
    base = 8

    def fetch(t):
        slot = lax.rem(t, RING)
        return pltpu.make_async_copy(counts.at[t], ring.at[slot], ring_sem.at[slot])

    def put(t):
        slot = lax.rem(t, OUT_RING)
        return pltpu.make_async_copy(resid_ring.at[slot], resids.at[t], resid_sem.at[slot])

    for t in range(min(RING, blocks)):
        fetch(t).start()
    loads = [
        pltpu.make_async_copy(x, table.at[pl.ds(m * 2 * half, 2 * half)], in_sem.at[m])
        for m, x in enumerate((near, far))
    ]
    for load in loads:
        load.start()
    hd_acc[...] = jnp.zeros_like(hd_acc)
    for load in loads:
        load.wait()
    me, grp = ids[0], ids[1]
    core = me & 1

    def visit(t, carry):
        src_from = ids[base + t] ^ me
        src_slot = ids[base + blocks + t]
        dst_from = ids[base + 2 * blocks + t] ^ me
        dst_slot = ids[base + 3 * blocks + t]
        hour = ids[base + 4 * blocks + t]
        row = dst_slot * SIDE
        turn = (row // dst_part) ^ grp
        inner = (dst_from >> 1) * dst_part + row % dst_part
        a_at = (src_from & 1) * (2 * half) + (src_from >> 1) * local + src_slot * SIDE
        a_at = pl.multiple_of(a_at, SIDE)
        b_at = (dst_from & 1) * (2 * half) + half + turn * (depth * dst_part) + inner
        b_at = pl.multiple_of(b_at, SIDE)
        here = pl.ds(pl.multiple_of(t * SIDE, SIDE), SIDE)
        b = table[pl.ds(b_at, SIDE), :]
        b_rows[here, :] = b
        fetch(t).wait()

        @pl.when(t >= OUT_RING)
        def _():
            put(t - OUT_RING).wait()

        term_b, term_c = block_terms(
            ring.at[lax.rem(t, RING)],
            table[pl.ds(a_at, SIDE), :],
            b,
            hours[here, :],
            resid_ring.at[lax.rem(t, OUT_RING)],
            cube,
            even,
            odd,
        )
        d_at = ((dst_from & 1) * grps + turn) * part + hour_part + inner
        home = hour // hour_blocks
        h_at = (((home // grps) ^ core) * grps + ((home % grps) ^ grp)) * part
        h_at = h_at + (hour % hour_blocks) * SIDE
        hd_acc[pl.ds(pl.multiple_of(d_at, SIDE), SIDE), :] += term_b
        hd_acc[pl.ds(pl.multiple_of(h_at, SIDE), SIDE), :] += term_c
        put(t).start()

        @pl.when(t + RING < blocks)
        def _():
            fetch(t + RING).start()

        return carry

    lax.fori_loop(0, blocks, visit, 0)
    hd_half = grps * part
    hd_send[...] = hd_acc[pl.ds(hd_half, hd_half), :].astype(BF16)
    for t in range(max(0, blocks - OUT_RING), blocks):
        put(t).wait()


def src_kernel(shape, first, last, ids, resids, b_rows, hours, after, *refs):
    devs, local = shape
    depth = devs // 2
    fresh = first == 0
    blocks = resids.shape[0]
    refs = refs if fresh else refs[1:]
    s_acc, *sends, ring, sem = refs
    me, base = ids[0], 8

    def fetch(t):
        slot = lax.rem(t - first, RING)
        return pltpu.make_async_copy(resids.at[t], ring.at[slot], sem.at[slot])

    for t in range(first, min(first + RING, last)):
        fetch(t).start()
    if fresh:
        s_acc[...] = jnp.zeros_like(s_acc)

    def visit(t, carry):
        src_from = ids[base + t] ^ me
        src_slot = ids[base + blocks + t]
        z, order, steps = src_from >> 1, 0, depth // 2
        while steps:
            order = order + (z & 1) * steps
            z, steps = z >> 1, steps // 2
        s_at = ((src_from & 1) * depth + order) * local + src_slot * SIDE
        s_at = pl.multiple_of(s_at, SIDE)
        here = pl.ds(pl.multiple_of(t * SIDE, SIDE), SIDE)
        b, c = b_rows[here, :], hours[here, :]
        fetch(t).wait()
        resid = ring[lax.rem(t - first, RING)]
        pairs = [
            (b[g * 4 : g * 4 + 4][:, None, :] * c[None, :, :]).reshape(4 * SIDE, b.shape[1])
            for g in range(SIDE // 4)
        ]
        terms = []
        for at in range(0, b.shape[1], 128):
            columns = jnp.concatenate([p[:, at : at + 128] for p in pairs], axis=0)
            terms.append(jnp.dot(resid, columns, preferred_element_type=F32))
        s_acc[pl.ds(s_at, SIDE), :] += jnp.concatenate(terms, axis=1)

        @pl.when(t + RING < last)
        def _():
            fetch(t + RING).start()

        return carry

    lax.fori_loop(first, last, visit, 0)
    for send in sends:
        send[...] = s_acc[pl.ds(depth * local, depth * local), :].astype(BF16)


def size_of(shapes):
    return sum(jnp.dtype(t).itemsize * functools.reduce(lambda x, y: x * y, s) for s, t in shapes)


def run_main(shape, ids, counts, hours, near, far):
    grps, devs, local, hour_rows = shape
    rank = hours.shape[1]
    hd_rows = hour_rows + devs * local
    outs = [
        ((hd_rows, rank), F32),
        ((hd_rows // 2, rank), BF16),
        (hours.shape, BF16),
    ]
    scratch = [
        ((RING,) + counts.shape[1:], BF16),
        ((OUT_RING,) + counts.shape[1:], BF16),
        ((devs * 2 * local, rank), BF16),
        ((SIDE // 2 * PITCH, 128), F32),
        ((SIDE, 128), F32),
        ((SIDE, 128), F32),
    ]
    need = max(size_of(outs) + size_of(scratch) + (8 << 20), GRANT)
    return pl.pallas_call(
        functools.partial(main_kernel, shape),
        in_specs=[SMEM, HBM, VMEM, ANY, ANY],
        out_specs=[VMEM] * 3 + [HBM],
        out_shape=[jax.ShapeDtypeStruct(s, t) for s, t in outs]
        + [jax.ShapeDtypeStruct(counts.shape, BF16)],
        scratch_shapes=[pltpu.VMEM(s, t) for s, t in scratch]
        + [
            pltpu.SemaphoreType.DMA((RING,)),
            pltpu.SemaphoreType.DMA((OUT_RING,)),
            pltpu.SemaphoreType.DMA((2,)),
        ],
        compiler_params=pltpu.CompilerParams(vmem_limit_bytes=need),
        cost_estimate=pl.CostEstimate(
            flops=6 * counts.size * rank,
            bytes_accessed=counts.size * 4,
            transcendentals=counts.size,
        ),
        name="hour_dst_terms",
    )(ids, counts, hours, near, far)


def run_src(shape, first, last, ids, resids, b_rows, hours, after, s_acc=None):
    devs, local = shape
    rank = hours.shape[1]
    blocks, rows, columns = resids.shape
    more = [] if s_acc is None else [s_acc]
    outs = [((devs * local, rank), F32)]
    if last == blocks:
        outs.append(((devs * local // 2, rank), BF16))
    need = size_of(outs) + size_of([((RING, rows, columns), BF16)]) + (8 << 20)
    each = rows * columns
    return pl.pallas_call(
        functools.partial(src_kernel, shape, first, last),
        in_specs=[SMEM, HBM, VMEM, VMEM, ANY] + [VMEM] * len(more),
        out_specs=[VMEM] * len(outs),
        out_shape=[jax.ShapeDtypeStruct(s, t) for s, t in outs],
        scratch_shapes=[
            pltpu.VMEM((RING, rows, columns), BF16),
            pltpu.SemaphoreType.DMA((RING,)),
        ],
        input_output_aliases={5: 0} if more else {},
        compiler_params=pltpu.CompilerParams(vmem_limit_bytes=max(need, SRC_GRANT)),
        cost_estimate=pl.CostEstimate(
            flops=8 * (last - first) * each * rank,
            bytes_accessed=(last - first) * each * 2,
            transcendentals=0,
        ),
        name="src_terms",
    )(ids, resids, b_rows, hours, after, *more)


def call(kernel, name, ins, outs, specs=None, scratch=(), weight=0):
    shapes = [(x.shape, x.dtype) for x in ins] + list(outs) + list(scratch)
    return pl.pallas_call(
        kernel,
        in_specs=specs or [VMEM] * len(ins),
        out_specs=[VMEM] * len(outs),
        out_shape=[jax.ShapeDtypeStruct(s, t) for s, t in outs],
        scratch_shapes=[pltpu.VMEM(s, t) for s, t in scratch],
        compiler_params=pltpu.CompilerParams(vmem_limit_bytes=size_of(shapes) + (4 << 20)),
        cost_estimate=pl.CostEstimate(
            flops=weight, bytes_accessed=size_of(shapes), transcendentals=0
        ),
        name=name,
    )(*ins)


def shares(rows, rank, ways):
    return [((rows, rank), F32)] + [((rows, rank), BF16)] * (ways - 1)


def run_cut(ways, acc, got, after):
    rows, rank = got.shape[0] // ways, got.shape[1]

    def kernel(acc, got, after, *outs):
        for m in range(ways):
            at = pl.ds(m * rows, rows)
            outs[m][...] = (acc[at, :] + got[at, :].astype(F32)).astype(outs[m].dtype)
        outs[ways][...] = jnp.zeros_like(outs[ways])

    outs = shares(rows, rank, ways) + [((8, 128), F32)]
    return call(kernel, "core_hours_dst", (acc, got, after), outs, specs=[VMEM, VMEM, ANY])


def halve(keep, got, stay, send):
    rows = got.shape[0]
    half = rows // 2
    stay[...] = keep[pl.ds(0, half), :] + got[pl.ds(0, half), :].astype(F32)
    at = pl.ds(half, half)
    send[...] = (keep[at, :] + got[at, :].astype(F32)).astype(BF16)


def halves(got):
    rows, rank = got.shape
    return [((rows // 2, rank), F32), ((rows // 2, rank), BF16)]


def run_halve(keep, got):
    return call(halve, "src_half", (keep, got), halves(got))


def total(refs):
    acc = refs[0][...]
    for r in refs[1:]:
        acc = acc + r[...].astype(F32)
    return acc


def run_grp(hour_part, depth, ids, parts):
    rows, rank = parts[0].shape
    ways = len(parts)
    each, dst_rows = hour_part // depth, (rows - hour_part) // depth

    def kernel(ids, *refs):
        outs, acc = refs[ways:-1], refs[-1]
        z = ids[0] >> 1
        acc[...] = total(refs[:ways])
        for m in range(depth):
            kind = outs[m].dtype
            at = pl.multiple_of((z ^ m) * each, each)
            outs[m][pl.ds(0, each), :] = acc[pl.ds(at, each), :].astype(kind)
            at = hour_part + m * dst_rows
            outs[m][pl.ds(each, dst_rows), :] = acc[pl.ds(at, dst_rows), :].astype(kind)

    return call(
        kernel,
        "grp_sum",
        (ids, *parts),
        shares(each + dst_rows, rank, depth),
        specs=[SMEM] + [VMEM] * ways,
        scratch=[((rows, rank), F32)],
        weight=SLOW,
    )


def run_z(hd_parts, hour_rows, s_acc, s_got):
    n = len(hd_parts)
    rows, rank = hd_parts[0].shape

    def kernel(*refs):
        keep, got, hour, dst, stay, send = refs[n:]
        halve(keep, got, stay, send)
        acc = total(refs[:n]) * (1.0 / SIDE)
        hour[...] = acc[:hour_rows].astype(BF16)
        dst[...] = acc[hour_rows:].astype(BF16)

    outs = [((hour_rows, rank), BF16), ((rows - hour_rows, rank), BF16)] + halves(s_got)
    return call(kernel, "z_sum", (*hd_parts, s_acc, s_got), outs)


def run_join(parts, keep=None, got=None, passed=None):
    rows = [p.shape[0] for p in parts]
    outs = [((sum(rows), parts[0].shape[1]), BF16)]
    ins = tuple(parts)
    if got is not None:
        ins += (keep, got)
        outs += halves(got)
    if passed is not None:
        ins += (passed,)
        outs += [(passed.shape, BF16)]

    def kernel(*refs):
        if got is not None:
            halve(refs[len(parts)], refs[len(parts) + 1], refs[-2], refs[-1])
        if passed is not None:
            refs[-1][...] = refs[len(parts)][...]
        out, at = refs[len(ins)], 0
        for ref, n_rows in zip(refs, rows):
            out[at : at + n_rows, :] = ref[...]
            at += n_rows

    return call(kernel, "join", ins, outs)


def run_src_sum(keep, got, joined):
    def kernel(keep, got, joined, out, same):
        out[...] = (keep[...] + got[...].astype(F32)) * (1.0 / SIDE)
        same[...] = joined[...]

    outs = [(keep.shape, F32), (joined.shape, BF16)]
    return call(kernel, "src_sum", (keep, got, joined), outs)


def run_place(sizes, hour_rows, ids, parts, so_far, dst_rows=0):
    grps, devs = sizes
    depth = devs // 2
    arrays = [p for p, _, _ in parts]
    rank = arrays[0].shape[1]
    part = hour_rows // (2 * grps)
    rows = part // depth
    n = len(parts)
    more = [] if so_far is None else [so_far]

    def kernel(ids, *refs):
        outs = refs[n + len(more) : -2]
        stage, sem = refs[-2:]
        core, z, grp = ids[0] & 1, ids[0] >> 1, ids[1]
        copies = []
        for i, (_, far, m) in enumerate(parts):
            if dst_rows and not far:
                at = pl.multiple_of((grp ^ m) * dst_rows, dst_rows)
                outs[1][pl.ds(at, dst_rows), :] = refs[i][pl.ds(part, dst_rows), :].astype(F32)
            if far is None:
                continue
            for k in range(depth):
                at = pl.multiple_of((z ^ k) * rows, rows)
                stage[i, pl.ds(at, rows), :] = refs[i][pl.ds(k * rows, rows), :].astype(F32)
            home = pl.multiple_of(((core ^ far) * grps + (grp ^ m)) * part, part)
            copies.append(
                pltpu.make_async_copy(stage.at[i], outs[0].at[pl.ds(home, part)], sem.at[i])
            )
            copies[-1].start()
        for copy in copies:
            copy.wait()

    outs = [jax.ShapeDtypeStruct((hour_rows, rank), F32)]
    if dst_rows:
        outs.append(jax.ShapeDtypeStruct((grps * dst_rows, rank), F32))
    scratch = [((n, part, rank), F32)]
    need = size_of([(p.shape, p.dtype) for p in arrays + outs[1:]] + scratch) + (4 << 20)
    return pl.pallas_call(
        kernel,
        in_specs=[SMEM] + [VMEM] * n + [HBM] * len(more),
        out_specs=[HBM] + [VMEM] * (len(outs) - 1),
        out_shape=outs,
        scratch_shapes=[pltpu.VMEM(s, t) for s, t in scratch] + [pltpu.SemaphoreType.DMA((n,))],
        input_output_aliases={n + 1: 0} if more else {},
        compiler_params=pltpu.CompilerParams(vmem_limit_bytes=need),
        cost_estimate=pl.CostEstimate(
            flops=0 if more else SLOW // 10, bytes_accessed=0, transcendentals=0
        ),
        name="place",
    )(ids, *arrays, *more)


def per_device(
    sizes,
    counts,
    src_factor,
    dst_factor,
    hour_factor,
    src_owner,
    src_slot,
    dst_owner,
    dst_slot,
    hour_block,
):
    grps, devs = sizes
    depth = devs // 2
    local = src_factor.shape[0]
    hour_rows = hour_factor.shape[0]
    me = lax.axis_index("dev").astype(jnp.int32)
    grp = lax.axis_index("grp").astype(jnp.int32)
    place = jnp.stack([me, grp] + [me * 0] * 6)
    ids = jnp.concatenate(
        [place, src_owner[:, 0], src_slot, dst_owner[:, 0], dst_slot, hour_block]
    )
    dst_part = local // grps
    dst_own = lax.dynamic_slice_in_dim(dst_factor, grp * dst_part, dst_part, 0)
    dst_z = [dst_own] + [swap(dst_own, "dev", devs, 2 * m) for m in range(1, depth)]
    src_z = [src_factor] + [swap(src_factor, "dev", devs, 2 * m) for m in range(1, depth)]
    blocks = counts.shape[0]
    picked = run_pick(blocks, ids, hour_factor)
    dst_here, src_z[1] = run_join(dst_z, passed=src_z[1])
    dsts = [dst_here] + [swap(dst_here, "grp", grps, m) for m in range(1, grps)]
    near = run_join(src_z + dsts)[0]
    far = swap(near, "dev", devs, 1)
    shape = (grps, devs, local, hour_rows)
    hd_acc, hd_send, b_rows, resids = run_main(shape, ids, counts, picked, near, far)

    def exchange(parts, axis, size, step):
        return [parts[0]] + [swap(x, axis, size, step * m) for m, x in enumerate(parts) if m]

    hd_got = swap(hd_send, "dev", devs, 1)
    src = functools.partial(run_src, (devs, local))
    early = blocks // 6
    s_acc = src(0, early, ids, resids, b_rows, picked, hd_send)[0]
    *hd, cut_done = run_cut(grps, hd_acc, hd_got, s_acc)
    cut_done = swap(cut_done, "dev", devs, 1)
    s_acc, s_send = src(early, blocks, ids, resids, b_rows, picked, cut_done, s_acc)
    s_got = swap(s_send, "dev", devs, 1)
    hour_part = hour_rows // (2 * grps)
    hd = run_grp(hour_part, depth, ids, exchange(hd, "grp", grps, 1))
    hour_each = hour_part // depth
    hour, dst, s_keep, s_send = run_z(exchange(hd, "dev", devs, 2), hour_each, s_acc, s_got)
    s_got = swap(s_send, "dev", devs, 2)
    back = [hour] + [swap(hour, "dev", devs, 2 * m) for m in range(1, depth)]
    joined, s_keep, s_send = run_join(back + [dst], s_keep, s_got)
    step = 4
    s_got = swap(s_send, "dev", devs, step)
    while 2 * step < devs:
        s_keep, s_send = run_halve(s_keep, s_got)
        step *= 2
        s_got = swap(s_send, "dev", devs, step)
    grad_src, same = run_src_sum(s_keep, s_got, joined)
    near = [joined] + [swap(joined, "grp", grps, m) for m in range(1, grps)]
    far = [swap(x, "dev", devs, 1) for x in [same] + near[1:]]
    put = functools.partial(run_place, sizes, hour_rows, ids)
    sooner = [0] + list(range(2, grps))
    grad_hour = put([(near[m], 0, m) for m in sooner], None)[0]
    parts = [(near[1], 0, 1)] + [(far[m], 1, m) for m in range(grps)]
    parts += [(near[m], None, m) for m in sooner]
    grad_hour, grad_dst = put(parts, grad_hour, dst_part)
    return grad_src, grad_dst, grad_hour


def solution(mesh):
    in_specs = (
        P(("grp", "dev"), None, None),
        P(("grp", "dev"), None),
        P("dev", None),
        P(),
        P(("grp", "dev"), None),
        P(("grp", "dev")),
        P(("grp", "dev"), None),
        P(("grp", "dev")),
        P(("grp", "dev")),
    )
    out_specs = (P(("grp", "dev"), None), P("dev", None), P())
    return jax.shard_map(
        functools.partial(per_device, mesh_sizes(mesh)),
        mesh=mesh,
        in_specs=in_specs,
        out_specs=out_specs,
        check_vma=False,
    )
```

```python
import functools

import jax
import jax.numpy as jnp
from jax import lax
from jax.experimental import pallas as pl
from jax.experimental.pallas import tpu as pltpu
from jax.sharding import PartitionSpec as P

F32 = jnp.float32
BF16 = jnp.bfloat16
SIDE = 64
RING = 8
PITCH = 72
GRANT = 36 << 20
SRC_GRANT = 44 << 20
SLOW = 10**11

VMEM = pl.BlockSpec(memory_space=pltpu.VMEM)
SMEM = pl.BlockSpec(memory_space=pltpu.SMEM)
ANY = pl.BlockSpec(memory_space=pl.ANY)
HBM = pl.BlockSpec(memory_space=pltpu.HBM)


def mesh_sizes(mesh):
    return mesh.shape["grp"], mesh.shape["dev"]


def swap(x, axis, size, mask):
    return lax.ppermute(x, axis, [(i, i ^ mask) for i in range(size)])


def block_resid(count, a, b, c, resid_out, cube):
    rank = a.shape[1]
    for g in range(SIDE // 4):
        b4 = b[g * 4 : g * 4 + 4]
        bc = (b4[:, None, :] * c[None, :, :]).reshape(4 * SIDE, rank)
        theta = lax.dot_general(a, bc, (((1,), (1,)), ((), ())), preferred_element_type=F32)
        wide = jnp.exp(theta) - count[:, g * 256 : (g + 1) * 256].astype(F32)
        for p in range(2):
            cube[pl.ds((g * 2 + p) * PITCH, SIDE), :] = wide[:, p * 128 : (p + 1) * 128]
        resid_out[:, g * 256 : (g + 1) * 256] = wide.astype(BF16)


def block_terms(resid, a, b, c, cube, even, odd):
    rank = a.shape[1]
    turned, pairs_ab = [], []
    for g in range(SIDE // 4):
        b4 = b[g * 4 : g * 4 + 4]
        pairs_ab.append((b4[:, None, :] * a[None, :, :]).reshape(4 * SIDE, rank))
        flip = resid[:, g * 256 : (g + 1) * 256].T
        turned += [flip[q * SIDE : (q + 1) * SIDE] for q in range(4)]
    term_c = jnp.dot(
        jnp.concatenate(turned, axis=1),
        jnp.concatenate(pairs_ab, axis=0),
        preferred_element_type=F32,
    )
    low = lax.broadcasted_iota(jnp.int32, (SIDE // 2, 128), 1) < SIDE
    rows, pairs_ac = [], []
    for g in range(SIDE // 4):
        x = [cube[pl.ds(g * 4 + q, SIDE // 2, stride=PITCH), :] for q in range(4)]
        y = [pltpu.roll(v, SIDE, 1) for v in x]
        evens = [jnp.where(low, x[0], y[1]), jnp.where(low, x[2], y[3])]
        odds = [jnp.where(low, y[0], x[1]), jnp.where(low, y[2], x[3])]
        both = [jnp.concatenate(evens, axis=1), jnp.concatenate(odds, axis=1)]
        rows.append(jnp.concatenate(both, axis=0).astype(BF16))
        pairs_ac.append((a[g * 4 : g * 4 + 4][:, None, :] * c[None, :, :]).reshape(4 * SIDE, rank))
    mixed = jnp.dot(
        jnp.concatenate(rows, axis=1),
        jnp.concatenate(pairs_ac, axis=0),
        preferred_element_type=F32,
    )
    half = SIDE // 2
    for u in range(2):
        even[pl.ds(u, half, stride=2), :] = mixed[u * half : (u + 1) * half, :128]
        odd[pl.ds(u, half, stride=2), :] = mixed[u * half : (u + 1) * half, 128:]
    term_b = jnp.concatenate([even[...], odd[...]], axis=1)
    return term_b, term_c


def run_pick(blocks, ids, hours, own):
    rank = hours.shape[1]

    def kernel(ids, hours, own, out, same, sem, own_sem):
        copies = [pltpu.make_async_copy(own, same, own_sem)]
        copies[0].start()
        for t in range(blocks):
            at = pl.multiple_of(ids[8 + 4 * blocks + t] * SIDE, SIDE)
            copies.append(
                pltpu.make_async_copy(
                    hours.at[pl.ds(at, SIDE)], out.at[pl.ds(t * SIDE, SIDE)], sem.at[t]
                )
            )
            copies[-1].start()
        for copy in copies:
            copy.wait()

    grant = 4 * blocks * SIDE * rank + 4 * own.size + (2 << 20)
    return pl.pallas_call(
        kernel,
        in_specs=[SMEM, HBM, ANY],
        out_specs=[VMEM, VMEM],
        out_shape=[
            jax.ShapeDtypeStruct((blocks * SIDE, rank), BF16),
            jax.ShapeDtypeStruct(own.shape, BF16),
        ],
        scratch_shapes=[pltpu.SemaphoreType.DMA((blocks,)), pltpu.SemaphoreType.DMA],
        compiler_params=pltpu.CompilerParams(vmem_limit_bytes=grant),
        cost_estimate=pl.CostEstimate(flops=SLOW // 10, bytes_accessed=0, transcendentals=0),
        name="pick_hours",
    )(ids, hours, own)


def main_kernel(shape, ids, counts, hours, near, far, *refs):
    grps, devs, local, hour_rows = shape
    depth = devs // 2
    hd_acc, hd_send, b_rows, resids, *refs = refs
    ring, resid_0, resid_1, cube_0, cube_1, even, odd, ring_sem, resid_sem = refs
    stages = ((resid_0, cube_0), (resid_1, cube_1))
    blocks = counts.shape[0]
    hour_part = hour_rows // (2 * grps)
    hour_blocks = hour_part // SIDE
    dst_part = local // grps
    part = hour_part + depth * dst_part
    half = depth * local
    base = 8

    def fetch(t):
        slot = lax.rem(t, RING)
        return pltpu.make_async_copy(counts.at[t], ring.at[slot], ring_sem.at[slot])

    def put(t, way):
        return pltpu.make_async_copy(stages[way][0], resids.at[t], resid_sem.at[way])

    for t in range(min(RING, blocks)):
        fetch(t).start()
    hd_acc[...] = jnp.zeros_like(hd_acc)
    me, grp = ids[0], ids[1]
    core = me & 1

    def pick(at, other):
        at = pl.ds(pl.multiple_of(at, SIDE), SIDE)
        return jnp.where(other == 1, far[at, :], near[at, :])

    def dst_place(t):
        dst_from = ids[base + 2 * blocks + t] ^ me
        row = ids[base + 3 * blocks + t] * SIDE
        turn = (row // dst_part) ^ grp
        return dst_from & 1, turn, (dst_from >> 1) * dst_part + row % dst_part

    def rows_of(t):
        src_from = ids[base + t] ^ me
        a = pick((src_from >> 1) * local + ids[base + blocks + t] * SIDE, src_from & 1)
        other, turn, inner = dst_place(t)
        b = pick(half + turn * (depth * dst_part) + inner, other)
        return a, b, hours[pl.ds(pl.multiple_of(t * SIDE, SIDE), SIDE), :]

    def first(t, way):
        a, b, c = rows_of(t)
        b_rows[pl.ds(pl.multiple_of(t * SIDE, SIDE), SIDE), :] = b
        block_resid(ring.at[lax.rem(t, RING)], a, b, c, *stages[way])

    def second(t, way):
        a, b, c = rows_of(t)
        resid, cube = stages[way]
        term_b, term_c = block_terms(resid, a, b, c, cube, even, odd)
        other, turn, inner = dst_place(t)
        hour = ids[base + 4 * blocks + t]
        d_at = (other * grps + turn) * part + hour_part + inner
        home = hour // hour_blocks
        h_at = (((home // grps) ^ core) * grps + ((home % grps) ^ grp)) * part
        h_at = h_at + (hour % hour_blocks) * SIDE
        hd_acc[pl.ds(pl.multiple_of(d_at, SIDE), SIDE), :] += term_b
        hd_acc[pl.ds(pl.multiple_of(h_at, SIDE), SIDE), :] += term_c

    def step(t, way, guard):
        fetch(t).wait()

        if guard is None:
            put(t - 2, way).wait()
        else:

            @pl.when(guard)
            def _():
                put(t - 2, way).wait()

        first(t, way)
        second(t - 1, 1 - way)
        put(t, way).start()

        @pl.when(t - 1 + RING < blocks)
        def _():
            fetch(t - 1 + RING).start()

    def visit(i, carry):
        step(2 * i - 1, 1, i > 1)
        step(2 * i, 0, None)
        return carry

    last = blocks - 1
    fetch(0).wait()
    first(0, 0)
    put(0, 0).start()
    lax.fori_loop(1, blocks // 2, visit, 0)
    step(last, 1, None)
    second(last, 1)
    hd_half = grps * part
    hd_send[...] = hd_acc[pl.ds(hd_half, hd_half), :].astype(BF16)
    put(last - 1, 0).wait()
    put(last, 1).wait()


def src_kernel(shape, first, last, ids, resids, b_rows, hours, after, *refs):
    devs, local = shape
    depth = devs // 2
    fresh = first == 0
    blocks = resids.shape[0]
    refs = refs if fresh else refs[1:]
    s_acc, *sends, ring, sem = refs
    me, base = ids[0], 8

    def fetch(t):
        slot = lax.rem(t - first, RING)
        return pltpu.make_async_copy(resids.at[t], ring.at[slot], sem.at[slot])

    for t in range(first, min(first + RING, last)):
        fetch(t).start()
    if fresh:
        s_acc[...] = jnp.zeros_like(s_acc)

    def visit(t, carry):
        src_from = ids[base + t] ^ me
        src_slot = ids[base + blocks + t]
        z, order, steps = src_from >> 1, 0, depth // 2
        while steps:
            order = order + (z & 1) * steps
            z, steps = z >> 1, steps // 2
        s_at = ((src_from & 1) * depth + order) * local + src_slot * SIDE
        s_at = pl.multiple_of(s_at, SIDE)
        here = pl.ds(pl.multiple_of(t * SIDE, SIDE), SIDE)
        b, c = b_rows[here, :], hours[here, :]
        fetch(t).wait()
        resid = ring[lax.rem(t - first, RING)]
        pairs = [
            (b[g * 4 : g * 4 + 4][:, None, :] * c[None, :, :]).reshape(4 * SIDE, b.shape[1])
            for g in range(SIDE // 4)
        ]
        terms = []
        for at in range(0, b.shape[1], 128):
            columns = jnp.concatenate([p[:, at : at + 128] for p in pairs], axis=0)
            terms.append(jnp.dot(resid, columns, preferred_element_type=F32))
        s_acc[pl.ds(s_at, SIDE), :] += jnp.concatenate(terms, axis=1)

        @pl.when(t + RING < last)
        def _():
            fetch(t + RING).start()

        return carry

    lax.fori_loop(first, last, visit, 0)
    for send in sends:
        send[...] = s_acc[pl.ds(depth * local, depth * local), :].astype(BF16)


def size_of(shapes):
    return sum(jnp.dtype(t).itemsize * functools.reduce(lambda x, y: x * y, s) for s, t in shapes)


def run_main(shape, ids, counts, hours, near, far):
    grps, devs, local, hour_rows = shape
    rank = hours.shape[1]
    hd_rows = hour_rows + devs * local
    outs = [
        ((hd_rows, rank), F32),
        ((hd_rows // 2, rank), BF16),
        (hours.shape, BF16),
    ]
    scratch = [
        ((RING,) + counts.shape[1:], BF16),
        (counts.shape[1:], BF16),
        (counts.shape[1:], BF16),
        ((SIDE // 2 * PITCH, 128), F32),
        ((SIDE // 2 * PITCH, 128), F32),
        ((SIDE, 128), F32),
        ((SIDE, 128), F32),
    ]
    need = max(size_of(outs) + size_of(scratch) + (8 << 20), GRANT)
    return pl.pallas_call(
        functools.partial(main_kernel, shape),
        in_specs=[SMEM, HBM, VMEM, VMEM, VMEM],
        out_specs=[VMEM] * 3 + [HBM],
        out_shape=[jax.ShapeDtypeStruct(s, t) for s, t in outs]
        + [jax.ShapeDtypeStruct(counts.shape, BF16)],
        scratch_shapes=[pltpu.VMEM(s, t) for s, t in scratch]
        + [
            pltpu.SemaphoreType.DMA((RING,)),
            pltpu.SemaphoreType.DMA((2,)),
        ],
        compiler_params=pltpu.CompilerParams(vmem_limit_bytes=need),
        cost_estimate=pl.CostEstimate(
            flops=6 * counts.size * rank,
            bytes_accessed=counts.size * 4,
            transcendentals=counts.size,
        ),
        name="hour_dst_terms",
    )(ids, counts, hours, near, far)


def run_src(shape, first, last, ids, resids, b_rows, hours, after, s_acc=None):
    devs, local = shape
    rank = hours.shape[1]
    blocks, rows, columns = resids.shape
    more = [] if s_acc is None else [s_acc]
    outs = [((devs * local, rank), F32)]
    if last == blocks:
        outs.append(((devs * local // 2, rank), BF16))
    need = size_of(outs) + size_of([((RING, rows, columns), BF16)]) + (8 << 20)
    each = rows * columns
    return pl.pallas_call(
        functools.partial(src_kernel, shape, first, last),
        in_specs=[SMEM, HBM, VMEM, VMEM, ANY] + [VMEM] * len(more),
        out_specs=[VMEM] * len(outs),
        out_shape=[jax.ShapeDtypeStruct(s, t) for s, t in outs],
        scratch_shapes=[
            pltpu.VMEM((RING, rows, columns), BF16),
            pltpu.SemaphoreType.DMA((RING,)),
        ],
        input_output_aliases={5: 0} if more else {},
        compiler_params=pltpu.CompilerParams(vmem_limit_bytes=max(need, SRC_GRANT)),
        cost_estimate=pl.CostEstimate(
            flops=8 * (last - first) * each * rank,
            bytes_accessed=(last - first) * each * 2,
            transcendentals=0,
        ),
        name="src_terms",
    )(ids, resids, b_rows, hours, after, *more)


def call(kernel, name, ins, outs, specs=None, scratch=(), weight=0):
    shapes = [(x.shape, x.dtype) for x in ins] + list(outs) + list(scratch)
    return pl.pallas_call(
        kernel,
        in_specs=specs or [VMEM] * len(ins),
        out_specs=[VMEM] * len(outs),
        out_shape=[jax.ShapeDtypeStruct(s, t) for s, t in outs],
        scratch_shapes=[pltpu.VMEM(s, t) for s, t in scratch],
        compiler_params=pltpu.CompilerParams(vmem_limit_bytes=size_of(shapes) + (4 << 20)),
        cost_estimate=pl.CostEstimate(
            flops=weight, bytes_accessed=size_of(shapes), transcendentals=0
        ),
        name=name,
    )(*ins)


def shares(rows, rank, ways):
    return [((rows, rank), F32)] + [((rows, rank), BF16)] * (ways - 1)


def run_cut(ways, acc, got, after):
    rows, rank = got.shape[0] // ways, got.shape[1]

    def kernel(acc, got, after, *outs):
        for m in range(ways):
            at = pl.ds(m * rows, rows)
            outs[m][...] = (acc[at, :] + got[at, :].astype(F32)).astype(outs[m].dtype)
        outs[ways][...] = jnp.zeros_like(outs[ways])

    outs = shares(rows, rank, ways) + [((8, 128), F32)]
    return call(kernel, "core_hours_dst", (acc, got, after), outs, specs=[VMEM, VMEM, ANY])


def halve(keep, got, stay, send):
    rows = got.shape[0]
    half = rows // 2
    stay[...] = keep[pl.ds(0, half), :] + got[pl.ds(0, half), :].astype(F32)
    at = pl.ds(half, half)
    send[...] = (keep[at, :] + got[at, :].astype(F32)).astype(BF16)


def halves(got):
    rows, rank = got.shape
    return [((rows // 2, rank), F32), ((rows // 2, rank), BF16)]


def run_halve(keep, got):
    return call(halve, "src_half", (keep, got), halves(got))


def total(refs):
    acc = refs[0][...]
    for r in refs[1:]:
        acc = acc + r[...].astype(F32)
    return acc


def run_grp(hour_part, depth, ids, parts):
    rows, rank = parts[0].shape
    ways = len(parts)
    each, dst_rows = hour_part // depth, (rows - hour_part) // depth

    def kernel(ids, *refs):
        outs, acc = refs[ways:-1], refs[-1]
        z = ids[0] >> 1
        acc[...] = total(refs[:ways])
        for m in range(depth):
            kind = outs[m].dtype
            at = pl.multiple_of((z ^ m) * each, each)
            outs[m][pl.ds(0, each), :] = acc[pl.ds(at, each), :].astype(kind)
            at = hour_part + m * dst_rows
            outs[m][pl.ds(each, dst_rows), :] = acc[pl.ds(at, dst_rows), :].astype(kind)

    return call(
        kernel,
        "grp_sum",
        (ids, *parts),
        shares(each + dst_rows, rank, depth),
        specs=[SMEM] + [VMEM] * ways,
        scratch=[((rows, rank), F32)],
        weight=SLOW,
    )


def run_z(parts, hour_rows):
    rows, rank = parts[0].shape

    def kernel(*refs):
        hour, dst = refs[-2:]
        acc = total(refs[:-2]) * (1.0 / SIDE)
        hour[...] = acc[:hour_rows].astype(BF16)
        dst[...] = acc[hour_rows:].astype(BF16)

    outs = [((hour_rows, rank), BF16), ((rows - hour_rows, rank), BF16)]
    return call(kernel, "z_sum", parts, outs, weight=SLOW)


def run_join(parts, keep=None, got=None, passed=None):
    rows = [p.shape[0] for p in parts]
    outs = [((sum(rows), parts[0].shape[1]), BF16)]
    ins = tuple(parts)
    if got is not None:
        ins += (keep, got)
        outs += halves(got)
    if passed is not None:
        ins += (passed,)
        outs += [(passed.shape, BF16)]

    def kernel(*refs):
        if got is not None:
            halve(refs[len(parts)], refs[len(parts) + 1], refs[-2], refs[-1])
        if passed is not None:
            refs[-1][...] = refs[len(parts)][...]
        out, at = refs[len(ins)], 0
        for ref, n_rows in zip(refs, rows):
            out[at : at + n_rows, :] = ref[...]
            at += n_rows

    return call(kernel, "join", ins, outs)


def run_src_sum(keep, got, joined):
    def kernel(keep, got, joined, out, same):
        out[...] = (keep[...] + got[...].astype(F32)) * (1.0 / SIDE)
        same[...] = joined[...]

    outs = [(keep.shape, F32), (joined.shape, BF16)]
    return call(kernel, "src_sum", (keep, got, joined), outs)


def run_place(sizes, hour_rows, ids, parts, dst_rows):
    grps, devs = sizes
    depth = devs // 2
    arrays = [p for p, _, _ in parts]
    rank = arrays[0].shape[1]
    part = hour_rows // (2 * grps)
    rows = part // depth
    n = len(parts)

    def kernel(ids, *refs):
        ins, (hours, dst, stage, sem) = refs[:n], refs[n:]
        core, z, grp = ids[0] & 1, ids[0] >> 1, ids[1]
        copies = []
        for i, (_, far, m) in enumerate(parts):
            for k in range(depth):
                at = pl.multiple_of((z ^ k) * rows, rows)
                stage[i, pl.ds(at, rows), :] = ins[i][pl.ds(k * rows, rows), :].astype(F32)
            home = pl.multiple_of(((core ^ far) * grps + (grp ^ m)) * part, part)
            copies.append(
                pltpu.make_async_copy(stage.at[i], hours.at[pl.ds(home, part)], sem.at[i])
            )
            copies[-1].start()
            if not far:
                at = pl.multiple_of((grp ^ m) * dst_rows, dst_rows)
                dst[pl.ds(at, dst_rows), :] = ins[i][pl.ds(part, dst_rows), :].astype(F32)
        for copy in copies:
            copy.wait()

    outs = [((hour_rows, rank), F32), ((grps * dst_rows, rank), F32)]
    scratch = [((n, part, rank), F32)]
    need = size_of([(p.shape, p.dtype) for p in arrays] + outs[1:] + scratch) + (4 << 20)
    return pl.pallas_call(
        kernel,
        in_specs=[SMEM] + [VMEM] * n,
        out_specs=[HBM, VMEM],
        out_shape=[jax.ShapeDtypeStruct(s, t) for s, t in outs],
        scratch_shapes=[pltpu.VMEM(s, t) for s, t in scratch] + [pltpu.SemaphoreType.DMA((n,))],
        compiler_params=pltpu.CompilerParams(vmem_limit_bytes=need),
        name="place",
    )(ids, *arrays)


def per_device(
    sizes,
    counts,
    src_factor,
    dst_factor,
    hour_factor,
    src_owner,
    src_slot,
    dst_owner,
    dst_slot,
    hour_block,
):
    grps, devs = sizes
    depth = devs // 2
    local = src_factor.shape[0]
    hour_rows = hour_factor.shape[0]
    me = lax.axis_index("dev").astype(jnp.int32)
    grp = lax.axis_index("grp").astype(jnp.int32)
    place = jnp.stack([me, grp] + [me * 0] * 6)
    ids = jnp.concatenate(
        [place, src_owner[:, 0], src_slot, dst_owner[:, 0], dst_slot, hour_block]
    )
    dst_part = local // grps
    dst_own = lax.dynamic_slice_in_dim(dst_factor, grp * dst_part, dst_part, 0)
    dst_z = [dst_own] + [swap(dst_own, "dev", devs, 2 * m) for m in range(1, depth)]
    src_z = [src_factor] + [swap(src_factor, "dev", devs, 2 * m) for m in range(1, depth)]
    blocks = counts.shape[0]
    picked, src_same = run_pick(blocks, ids, hour_factor, src_factor)
    dst_here, src_z[1] = run_join(dst_z, passed=src_z[1])
    dsts = [dst_here] + [swap(dst_here, "grp", grps, m) for m in range(1, grps)]
    near = run_join([src_same] + src_z[1:] + dsts)[0]
    far = swap(near, "dev", devs, 1)
    shape = (grps, devs, local, hour_rows)
    hd_acc, hd_send, b_rows, resids = run_main(shape, ids, counts, picked, near, far)

    def exchange(parts, axis, size, step):
        return [parts[0]] + [swap(x, axis, size, step * m) for m, x in enumerate(parts) if m]

    hd_got = swap(hd_send, "dev", devs, 1)
    src = functools.partial(run_src, (devs, local))
    early = blocks // 6
    s_acc = src(0, early, ids, resids, b_rows, picked, hd_send)[0]
    *hd, cut_done = run_cut(grps, hd_acc, hd_got, s_acc)
    cut_done = swap(cut_done, "dev", devs, 1)
    s_acc, s_send = src(early, blocks, ids, resids, b_rows, picked, cut_done, s_acc)
    s_got = swap(s_send, "dev", devs, 1)
    hour_part = hour_rows // (2 * grps)
    hd = run_grp(hour_part, depth, ids, exchange(hd, "grp", grps, 1))
    hour_each = hour_part // depth
    s_keep, s_send = run_halve(s_acc, s_got)
    hour, dst = run_z(exchange(hd, "dev", devs, 2), hour_each)
    s_got = swap(s_send, "dev", devs, 2)
    back = [hour] + [swap(hour, "dev", devs, 2 * m) for m in range(1, depth)]
    joined, s_keep, s_send = run_join(back + [dst], s_keep, s_got)
    step = 4
    s_got = swap(s_send, "dev", devs, step)
    while 2 * step < devs:
        s_keep, s_send = run_halve(s_keep, s_got)
        step *= 2
        s_got = swap(s_send, "dev", devs, step)
    grad_src, same = run_src_sum(s_keep, s_got, joined)
    near = [joined] + [swap(joined, "grp", grps, m) for m in range(1, grps)]
    far = [swap(x, "dev", devs, 1) for x in [same] + near[1:]]
    parts = [(near[m], 0, m) for m in range(grps)] + [(far[m], 1, m) for m in range(grps)]
    grad_hour, grad_dst = run_place(sizes, hour_rows, ids, parts, dst_part)
    return grad_src, grad_dst, grad_hour


def solution(mesh):
    in_specs = (
        P(("grp", "dev"), None, None),
        P(("grp", "dev"), None),
        P("dev", None),
        P(),
        P(("grp", "dev"), None),
        P(("grp", "dev")),
        P(("grp", "dev"), None),
        P(("grp", "dev")),
        P(("grp", "dev")),
    )
    out_specs = (P(("grp", "dev"), None), P("dev", None), P())
    return jax.shard_map(
        functools.partial(per_device, mesh_sizes(mesh)),
        mesh=mesh,
        in_specs=in_specs,
        out_specs=out_specs,
        check_vma=False,
    )
```

```python
import functools

import jax
import jax.numpy as jnp
from jax import lax
from jax.experimental import pallas as pl
from jax.experimental.pallas import tpu as pltpu
from jax.sharding import PartitionSpec as P

F32 = jnp.float32
BF16 = jnp.bfloat16
SIDE = 64
RING = 8
PITCH = 72
GRANT = 36 << 20
SRC_GRANT = 44 << 20
SLOW = 10**11

VMEM = pl.BlockSpec(memory_space=pltpu.VMEM)
SMEM = pl.BlockSpec(memory_space=pltpu.SMEM)
ANY = pl.BlockSpec(memory_space=pl.ANY)
HBM = pl.BlockSpec(memory_space=pltpu.HBM)


def mesh_sizes(mesh):
    return mesh.shape["grp"], mesh.shape["dev"]


def swap(x, axis, size, mask):
    return lax.ppermute(x, axis, [(i, i ^ mask) for i in range(size)])


def block_resid(count, a, b, c, resid_out, cube):
    rank = a.shape[1]
    for g in range(SIDE // 4):
        b4 = b[g * 4 : g * 4 + 4]
        bc = (b4[:, None, :] * c[None, :, :]).reshape(4 * SIDE, rank)
        theta = lax.dot_general(a, bc, (((1,), (1,)), ((), ())), preferred_element_type=F32)
        wide = jnp.exp(theta) - count[:, g * 256 : (g + 1) * 256].astype(F32)
        for p in range(2):
            cube[pl.ds((g * 2 + p) * PITCH, SIDE), :] = wide[:, p * 128 : (p + 1) * 128]
        resid_out[:, g * 256 : (g + 1) * 256] = wide.astype(BF16)


def block_terms(resid, a, b, c, cube, even, odd):
    rank = a.shape[1]
    turned, pairs_ab = [], []
    for g in range(SIDE // 4):
        b4 = b[g * 4 : g * 4 + 4]
        pairs_ab.append((b4[:, None, :] * a[None, :, :]).reshape(4 * SIDE, rank))
        flip = resid[:, g * 256 : (g + 1) * 256].T
        turned += [flip[q * SIDE : (q + 1) * SIDE] for q in range(4)]
    term_c = jnp.dot(
        jnp.concatenate(turned, axis=1),
        jnp.concatenate(pairs_ab, axis=0),
        preferred_element_type=F32,
    )
    low = lax.broadcasted_iota(jnp.int32, (SIDE // 2, 128), 1) < SIDE
    rows, pairs_ac = [], []
    for g in range(SIDE // 4):
        x = [cube[pl.ds(g * 4 + q, SIDE // 2, stride=PITCH), :] for q in range(4)]
        y = [pltpu.roll(v, SIDE, 1) for v in x]
        evens = [jnp.where(low, x[0], y[1]), jnp.where(low, x[2], y[3])]
        odds = [jnp.where(low, y[0], x[1]), jnp.where(low, y[2], x[3])]
        both = [jnp.concatenate(evens, axis=1), jnp.concatenate(odds, axis=1)]
        rows.append(jnp.concatenate(both, axis=0).astype(BF16))
        pairs_ac.append((a[g * 4 : g * 4 + 4][:, None, :] * c[None, :, :]).reshape(4 * SIDE, rank))
    mixed = jnp.dot(
        jnp.concatenate(rows, axis=1),
        jnp.concatenate(pairs_ac, axis=0),
        preferred_element_type=F32,
    )
    half = SIDE // 2
    for u in range(2):
        even[pl.ds(u, half, stride=2), :] = mixed[u * half : (u + 1) * half, :128]
        odd[pl.ds(u, half, stride=2), :] = mixed[u * half : (u + 1) * half, 128:]
    term_b = jnp.concatenate([even[...], odd[...]], axis=1)
    return term_b, term_c


def run_pick(blocks, ids, hours, own):
    rank = hours.shape[1]

    def kernel(ids, hours, own, out, same, sem, own_sem):
        copies = [pltpu.make_async_copy(own, same, own_sem)]
        copies[0].start()
        for t in range(blocks):
            at = pl.multiple_of(ids[8 + 4 * blocks + t] * SIDE, SIDE)
            copies.append(
                pltpu.make_async_copy(
                    hours.at[pl.ds(at, SIDE)], out.at[pl.ds(t * SIDE, SIDE)], sem.at[t]
                )
            )
            copies[-1].start()
        for copy in copies:
            copy.wait()

    grant = 4 * blocks * SIDE * rank + 4 * own.size + (2 << 20)
    return pl.pallas_call(
        kernel,
        in_specs=[SMEM, HBM, ANY],
        out_specs=[VMEM, VMEM],
        out_shape=[
            jax.ShapeDtypeStruct((blocks * SIDE, rank), BF16),
            jax.ShapeDtypeStruct(own.shape, BF16),
        ],
        scratch_shapes=[pltpu.SemaphoreType.DMA((blocks,)), pltpu.SemaphoreType.DMA],
        compiler_params=pltpu.CompilerParams(vmem_limit_bytes=grant),
        cost_estimate=pl.CostEstimate(flops=SLOW // 10, bytes_accessed=0, transcendentals=0),
        name="pick_hours",
    )(ids, hours, own)


def main_kernel(shape, ids, counts, hours, near, far, *refs):
    grps, devs, local, hour_rows = shape
    depth = devs // 2
    hd_acc, hd_send, b_rows, resids, *refs = refs
    ring, resid_0, resid_1, cube_0, cube_1, even, odd, ring_sem, resid_sem = refs
    stages = ((resid_0, cube_0), (resid_1, cube_1))
    blocks = counts.shape[0]
    hour_part = hour_rows // (2 * grps)
    hour_blocks = hour_part // SIDE
    dst_part = local // grps
    part = hour_part + depth * dst_part
    half = depth * local
    base = 8

    def fetch(t):
        slot = lax.rem(t, RING)
        return pltpu.make_async_copy(counts.at[t], ring.at[slot], ring_sem.at[slot])

    def put(t, way):
        return pltpu.make_async_copy(stages[way][0], resids.at[t], resid_sem.at[way])

    for t in range(min(RING, blocks)):
        fetch(t).start()
    hd_acc[...] = jnp.zeros_like(hd_acc)
    me, grp = ids[0], ids[1]
    core = me & 1

    def pick(at, other):
        at = pl.ds(pl.multiple_of(at, SIDE), SIDE)
        return jnp.where(other == 1, far[at, :], near[at, :])

    def dst_place(t):
        dst_from = ids[base + 2 * blocks + t] ^ me
        row = ids[base + 3 * blocks + t] * SIDE
        turn = (row // dst_part) ^ grp
        return dst_from & 1, turn, (dst_from >> 1) * dst_part + row % dst_part

    def rows_of(t):
        src_from = ids[base + t] ^ me
        a = pick((src_from >> 1) * local + ids[base + blocks + t] * SIDE, src_from & 1)
        other, turn, inner = dst_place(t)
        b = pick(half + turn * (depth * dst_part) + inner, other)
        return a, b, hours[pl.ds(pl.multiple_of(t * SIDE, SIDE), SIDE), :]

    def first(t, way):
        a, b, c = rows_of(t)
        b_rows[pl.ds(pl.multiple_of(t * SIDE, SIDE), SIDE), :] = b
        block_resid(ring.at[lax.rem(t, RING)], a, b, c, *stages[way])

    def second(t, way):
        a, b, c = rows_of(t)
        resid, cube = stages[way]
        term_b, term_c = block_terms(resid, a, b, c, cube, even, odd)
        other, turn, inner = dst_place(t)
        hour = ids[base + 4 * blocks + t]
        d_at = (other * grps + turn) * part + hour_part + inner
        home = hour // hour_blocks
        h_at = (((home // grps) ^ core) * grps + ((home % grps) ^ grp)) * part
        h_at = h_at + (hour % hour_blocks) * SIDE
        hd_acc[pl.ds(pl.multiple_of(d_at, SIDE), SIDE), :] += term_b
        hd_acc[pl.ds(pl.multiple_of(h_at, SIDE), SIDE), :] += term_c

    def step(t, way, guard):
        fetch(t).wait()

        if guard is None:
            put(t - 2, way).wait()
        else:

            @pl.when(guard)
            def _():
                put(t - 2, way).wait()

        first(t, way)
        second(t - 1, 1 - way)
        put(t, way).start()

        @pl.when(t - 1 + RING < blocks)
        def _():
            fetch(t - 1 + RING).start()

    def visit(i, carry):
        step(2 * i - 1, 1, i > 1)
        step(2 * i, 0, None)
        return carry

    last = blocks - 1
    fetch(0).wait()
    first(0, 0)
    put(0, 0).start()
    lax.fori_loop(1, blocks // 2, visit, 0)
    step(last, 1, None)
    second(last, 1)
    hd_half = grps * part
    hd_send[...] = hd_acc[pl.ds(hd_half, hd_half), :].astype(BF16)
    put(last - 1, 0).wait()
    put(last, 1).wait()


def src_kernel(shape, first, last, ids, resids, b_rows, hours, after, *refs):
    devs, local = shape
    depth = devs // 2
    fresh = first == 0
    blocks = resids.shape[0]
    refs = refs if fresh else refs[1:]
    s_acc, *sends, ring, sem = refs
    me, base = ids[0], 8

    def fetch(t):
        slot = lax.rem(t - first, RING)
        return pltpu.make_async_copy(resids.at[t], ring.at[slot], sem.at[slot])

    for t in range(first, min(first + RING, last)):
        fetch(t).start()
    if fresh:
        s_acc[...] = jnp.zeros_like(s_acc)

    def visit(t, carry):
        src_from = ids[base + t] ^ me
        src_slot = ids[base + blocks + t]
        z, order, steps = src_from >> 1, 0, depth // 2
        while steps:
            order = order + (z & 1) * steps
            z, steps = z >> 1, steps // 2
        s_at = ((src_from & 1) * depth + order) * local + src_slot * SIDE
        s_at = pl.multiple_of(s_at, SIDE)
        here = pl.ds(pl.multiple_of(t * SIDE, SIDE), SIDE)
        b, c = b_rows[here, :], hours[here, :]
        fetch(t).wait()
        resid = ring[lax.rem(t - first, RING)]
        pairs = [
            (b[g * 4 : g * 4 + 4][:, None, :] * c[None, :, :]).reshape(4 * SIDE, b.shape[1])
            for g in range(SIDE // 4)
        ]
        terms = []
        for at in range(0, b.shape[1], 128):
            columns = jnp.concatenate([p[:, at : at + 128] for p in pairs], axis=0)
            terms.append(jnp.dot(resid, columns, preferred_element_type=F32))
        s_acc[pl.ds(s_at, SIDE), :] += jnp.concatenate(terms, axis=1)

        @pl.when(t + RING < last)
        def _():
            fetch(t + RING).start()

        return carry

    lax.fori_loop(first, last, visit, 0)
    for send in sends:
        send[...] = s_acc[pl.ds(depth * local, depth * local), :].astype(BF16)


def size_of(shapes):
    return sum(jnp.dtype(t).itemsize * functools.reduce(lambda x, y: x * y, s) for s, t in shapes)


def run_main(shape, ids, counts, hours, near, far):
    grps, devs, local, hour_rows = shape
    rank = hours.shape[1]
    hd_rows = hour_rows + devs * local
    outs = [
        ((hd_rows, rank), F32),
        ((hd_rows // 2, rank), BF16),
        (hours.shape, BF16),
    ]
    scratch = [
        ((RING,) + counts.shape[1:], BF16),
        (counts.shape[1:], BF16),
        (counts.shape[1:], BF16),
        ((SIDE // 2 * PITCH, 128), F32),
        ((SIDE // 2 * PITCH, 128), F32),
        ((SIDE, 128), F32),
        ((SIDE, 128), F32),
    ]
    need = max(size_of(outs) + size_of(scratch) + (8 << 20), GRANT)
    return pl.pallas_call(
        functools.partial(main_kernel, shape),
        in_specs=[SMEM, HBM, VMEM, VMEM, VMEM],
        out_specs=[VMEM] * 3 + [HBM],
        out_shape=[jax.ShapeDtypeStruct(s, t) for s, t in outs]
        + [jax.ShapeDtypeStruct(counts.shape, BF16)],
        scratch_shapes=[pltpu.VMEM(s, t) for s, t in scratch]
        + [
            pltpu.SemaphoreType.DMA((RING,)),
            pltpu.SemaphoreType.DMA((2,)),
        ],
        compiler_params=pltpu.CompilerParams(vmem_limit_bytes=need),
        cost_estimate=pl.CostEstimate(
            flops=6 * counts.size * rank,
            bytes_accessed=counts.size * 4,
            transcendentals=counts.size,
        ),
        name="hour_dst_terms",
    )(ids, counts, hours, near, far)


def run_src(shape, first, last, ids, resids, b_rows, hours, after, s_acc=None):
    devs, local = shape
    rank = hours.shape[1]
    blocks, rows, columns = resids.shape
    more = [] if s_acc is None else [s_acc]
    outs = [((devs * local, rank), F32)]
    if last == blocks:
        outs.append(((devs * local // 2, rank), BF16))
    need = size_of(outs) + size_of([((RING, rows, columns), BF16)]) + (8 << 20)
    each = rows * columns
    return pl.pallas_call(
        functools.partial(src_kernel, shape, first, last),
        in_specs=[SMEM, HBM, VMEM, VMEM, ANY] + [VMEM] * len(more),
        out_specs=[VMEM] * len(outs),
        out_shape=[jax.ShapeDtypeStruct(s, t) for s, t in outs],
        scratch_shapes=[
            pltpu.VMEM((RING, rows, columns), BF16),
            pltpu.SemaphoreType.DMA((RING,)),
        ],
        input_output_aliases={5: 0} if more else {},
        compiler_params=pltpu.CompilerParams(vmem_limit_bytes=max(need, SRC_GRANT)),
        cost_estimate=pl.CostEstimate(
            flops=8 * (last - first) * each * rank,
            bytes_accessed=(last - first) * each * 2,
            transcendentals=0,
        ),
        name="src_terms",
    )(ids, resids, b_rows, hours, after, *more)


def call(kernel, name, ins, outs, specs=None, scratch=(), weight=0):
    shapes = [(x.shape, x.dtype) for x in ins] + list(outs) + list(scratch)
    return pl.pallas_call(
        kernel,
        in_specs=specs or [VMEM] * len(ins),
        out_specs=[VMEM] * len(outs),
        out_shape=[jax.ShapeDtypeStruct(s, t) for s, t in outs],
        scratch_shapes=[pltpu.VMEM(s, t) for s, t in scratch],
        compiler_params=pltpu.CompilerParams(vmem_limit_bytes=size_of(shapes) + (4 << 20)),
        cost_estimate=pl.CostEstimate(
            flops=weight, bytes_accessed=size_of(shapes), transcendentals=0
        ),
        name=name,
    )(*ins)


def shares(rows, rank, ways):
    return [((rows, rank), F32)] + [((rows, rank), BF16)] * (ways - 1)


def run_cut(ways, acc, got, after):
    rows, rank = got.shape[0] // ways, got.shape[1]

    def kernel(acc, got, after, *outs):
        for m in range(ways):
            at = pl.ds(m * rows, rows)
            outs[m][...] = (acc[at, :] + got[at, :].astype(F32)).astype(outs[m].dtype)
        outs[ways][...] = jnp.zeros_like(outs[ways])

    outs = shares(rows, rank, ways) + [((8, 128), F32)]
    return call(kernel, "core_hours_dst", (acc, got, after), outs, specs=[VMEM, VMEM, ANY])


def halve(keep, got, stay, send):
    rows = got.shape[0]
    half = rows // 2
    stay[...] = keep[pl.ds(0, half), :] + got[pl.ds(0, half), :].astype(F32)
    at = pl.ds(half, half)
    send[...] = (keep[at, :] + got[at, :].astype(F32)).astype(BF16)


def halves(got):
    rows, rank = got.shape
    return [((rows // 2, rank), F32), ((rows // 2, rank), BF16)]


def run_halve(keep, got):
    return call(halve, "src_half", (keep, got), halves(got))


def total(refs):
    acc = refs[0][...]
    for r in refs[1:]:
        acc = acc + r[...].astype(F32)
    return acc


def run_grp(hour_part, depth, parts):
    rows, rank = parts[0].shape
    ways = len(parts)
    each, dst_rows = hour_part // depth, (rows - hour_part) // depth

    def kernel(*refs):
        outs, acc = refs[ways:-1], refs[-1]
        z = lax.axis_index("dev") >> 1
        acc[...] = total(refs[:ways])
        for m in range(depth):
            kind = outs[m].dtype
            at = pl.multiple_of((z ^ m) * each, each)
            outs[m][pl.ds(0, each), :] = acc[pl.ds(at, each), :].astype(kind)
            at = hour_part + m * dst_rows
            outs[m][pl.ds(each, dst_rows), :] = acc[pl.ds(at, dst_rows), :].astype(kind)

    return call(
        kernel,
        "grp_sum",
        parts,
        shares(each + dst_rows, rank, depth),
        scratch=[((rows, rank), F32)],
        weight=SLOW,
    )


def run_z(parts, hour_rows):
    rows, rank = parts[0].shape

    def kernel(*refs):
        hour, dst = refs[-2:]
        acc = total(refs[:-2]) * (1.0 / SIDE)
        hour[...] = acc[:hour_rows].astype(BF16)
        dst[...] = acc[hour_rows:].astype(BF16)

    outs = [((hour_rows, rank), BF16), ((rows - hour_rows, rank), BF16)]
    return call(kernel, "z_sum", parts, outs, weight=SLOW)


def run_join(parts, keep=None, got=None, passed=None):
    rows = [p.shape[0] for p in parts]
    outs = [((sum(rows), parts[0].shape[1]), BF16)]
    ins = tuple(parts)
    if got is not None:
        ins += (keep, got)
        outs += halves(got)
    if passed is not None:
        ins += (passed,)
        outs += [(passed.shape, BF16)]

    def kernel(*refs):
        if got is not None:
            halve(refs[len(parts)], refs[len(parts) + 1], refs[-2], refs[-1])
        if passed is not None:
            refs[-1][...] = refs[len(parts)][...]
        out, at = refs[len(ins)], 0
        for ref, n_rows in zip(refs, rows):
            out[at : at + n_rows, :] = ref[...]
            at += n_rows

    return call(kernel, "join", ins, outs)


def run_src_sum(keep, got, joined):
    def kernel(keep, got, joined, out, same):
        out[...] = (keep[...] + got[...].astype(F32)) * (1.0 / SIDE)
        same[...] = joined[...]

    outs = [(keep.shape, F32), (joined.shape, BF16)]
    return call(kernel, "src_sum", (keep, got, joined), outs)


def run_place(sizes, hour_rows, parts, dst_rows):
    grps, devs = sizes
    depth = devs // 2
    arrays = [p for p, _, _ in parts]
    rank = arrays[0].shape[1]
    part = hour_rows // (2 * grps)
    rows = part // depth
    n = len(parts)

    def kernel(*refs):
        ins, (hours, dst, stage, dst_stage, sem) = refs[:n], refs[n:]
        dev, grp = lax.axis_index("dev"), lax.axis_index("grp")
        core, z = dev & 1, dev >> 1
        copies = []
        for i, (_, far, m) in enumerate(parts):
            for k in range(depth):
                at = pl.multiple_of((z ^ k) * rows, rows)
                stage[i, pl.ds(at, rows), :] = ins[i][pl.ds(k * rows, rows), :].astype(F32)
            home = pl.multiple_of(((core ^ far) * grps + (grp ^ m)) * part, part)
            copies.append(
                pltpu.make_async_copy(stage.at[i], hours.at[pl.ds(home, part)], sem.at[i])
            )
            copies[-1].start()
            if not far:
                at = pl.multiple_of((grp ^ m) * dst_rows, dst_rows)
                new = ins[i][pl.ds(part, dst_rows), :].astype(F32)
                dst_stage[pl.ds(at, dst_rows), :] = new
            if i == grps - 1:
                copies.append(pltpu.make_async_copy(dst_stage, dst, sem.at[n]))
                copies[-1].start()
        for copy in copies:
            copy.wait()

    outs = [((hour_rows, rank), F32), ((grps * dst_rows, rank), F32)]
    scratch = [((n, part, rank), F32), outs[1]]
    need = size_of([(p.shape, p.dtype) for p in arrays] + scratch) + (4 << 20)
    return pl.pallas_call(
        kernel,
        in_specs=[VMEM] * n,
        out_specs=[HBM, HBM],
        out_shape=[jax.ShapeDtypeStruct(s, t) for s, t in outs],
        scratch_shapes=[pltpu.VMEM(s, t) for s, t in scratch]
        + [pltpu.SemaphoreType.DMA((n + 1,))],
        compiler_params=pltpu.CompilerParams(vmem_limit_bytes=need),
        name="place",
    )(*arrays)


def per_device(
    sizes,
    counts,
    src_factor,
    dst_factor,
    hour_factor,
    src_owner,
    src_slot,
    dst_owner,
    dst_slot,
    hour_block,
):
    grps, devs = sizes
    depth = devs // 2
    local = src_factor.shape[0]
    hour_rows = hour_factor.shape[0]
    me = lax.axis_index("dev").astype(jnp.int32)
    grp = lax.axis_index("grp").astype(jnp.int32)
    place = jnp.stack([me, grp] + [me * 0] * 6)
    ids = jnp.concatenate(
        [place, src_owner[:, 0], src_slot, dst_owner[:, 0], dst_slot, hour_block]
    )
    dst_part = local // grps
    dst_own = lax.dynamic_slice_in_dim(dst_factor, grp * dst_part, dst_part, 0)
    dst_z = [dst_own] + [swap(dst_own, "dev", devs, 2 * m) for m in range(1, depth)]
    src_z = [src_factor] + [swap(src_factor, "dev", devs, 2 * m) for m in range(1, depth)]
    blocks = counts.shape[0]
    picked, src_same = run_pick(blocks, ids, hour_factor, src_factor)
    dst_here, src_z[1] = run_join(dst_z, passed=src_z[1])
    dsts = [dst_here] + [swap(dst_here, "grp", grps, m) for m in range(1, grps)]
    near = run_join([src_same] + src_z[1:] + dsts)[0]
    far = swap(near, "dev", devs, 1)
    shape = (grps, devs, local, hour_rows)
    hd_acc, hd_send, b_rows, resids = run_main(shape, ids, counts, picked, near, far)

    def exchange(parts, axis, size, step):
        return [parts[0]] + [swap(x, axis, size, step * m) for m, x in enumerate(parts) if m]

    hd_got = swap(hd_send, "dev", devs, 1)
    src = functools.partial(run_src, (devs, local))
    early = blocks // 8
    s_acc = src(0, early, ids, resids, b_rows, picked, hd_send)[0]
    *hd, cut_done = run_cut(grps, hd_acc, hd_got, s_acc)
    cut_done = swap(cut_done, "dev", devs, 1)
    s_acc, s_send = src(early, blocks, ids, resids, b_rows, picked, cut_done, s_acc)
    s_got = swap(s_send, "dev", devs, 1)
    hour_part = hour_rows // (2 * grps)
    hd = run_grp(hour_part, depth, exchange(hd, "grp", grps, 1))
    hour_each = hour_part // depth
    s_keep, s_send = run_halve(s_acc, s_got)
    hour, dst = run_z(exchange(hd, "dev", devs, 2), hour_each)
    s_got = swap(s_send, "dev", devs, 2)
    back = [hour] + [swap(hour, "dev", devs, 2 * m) for m in range(1, depth)]
    joined, s_keep, s_send = run_join(back + [dst], s_keep, s_got)
    step = 4
    s_got = swap(s_send, "dev", devs, step)
    while 2 * step < devs:
        s_keep, s_send = run_halve(s_keep, s_got)
        step *= 2
        s_got = swap(s_send, "dev", devs, step)
    grad_src, same = run_src_sum(s_keep, s_got, joined)
    near = [joined] + [swap(joined, "grp", grps, m) for m in range(1, grps)]
    far = [swap(x, "dev", devs, 1) for x in [same] + near[1:]]
    parts = [(near[m], 0, m) for m in range(grps)] + [(far[m], 1, m) for m in range(grps)]
    grad_hour, grad_dst = run_place(sizes, hour_rows, parts, dst_part)
    return grad_src, grad_dst, grad_hour


def solution(mesh):
    in_specs = (
        P(("grp", "dev"), None, None),
        P(("grp", "dev"), None),
        P("dev", None),
        P(),
        P(("grp", "dev"), None),
        P(("grp", "dev")),
        P(("grp", "dev"), None),
        P(("grp", "dev")),
        P(("grp", "dev")),
    )
    out_specs = (P(("grp", "dev"), None), P("dev", None), P())
    return jax.shard_map(
        functools.partial(per_device, mesh_sizes(mesh)),
        mesh=mesh,
        in_specs=in_specs,
        out_specs=out_specs,
        check_vma=False,
    )
```

```python
import functools

import jax
import jax.numpy as jnp
from jax import lax
from jax.experimental import pallas as pl
from jax.experimental.pallas import tpu as pltpu
from jax.sharding import PartitionSpec as P

F32 = jnp.float32
BF16 = jnp.bfloat16
SIDE = 64
RING = 8
PITCH = 72
GRANT = 36 << 20
SRC_GRANT = 44 << 20
SLOW = 10**11

VMEM = pl.BlockSpec(memory_space=pltpu.VMEM)
SMEM = pl.BlockSpec(memory_space=pltpu.SMEM)
ANY = pl.BlockSpec(memory_space=pl.ANY)
HBM = pl.BlockSpec(memory_space=pltpu.HBM)


def mesh_sizes(mesh):
    return mesh.shape["grp"], mesh.shape["dev"]


def swap(x, axis, size, mask):
    return lax.ppermute(x, axis, [(i, i ^ mask) for i in range(size)])


def block_resid(count, a, b, c, resid_out, cube):
    rank = a.shape[1]
    for g in range(SIDE // 4):
        b4 = b[g * 4 : g * 4 + 4]
        bc = (b4[:, None, :] * c[None, :, :]).reshape(4 * SIDE, rank)
        theta = lax.dot_general(a, bc, (((1,), (1,)), ((), ())), preferred_element_type=F32)
        wide = jnp.exp(theta) - count[:, g * 256 : (g + 1) * 256].astype(F32)
        for p in range(2):
            cube[pl.ds((g * 2 + p) * PITCH, SIDE), :] = wide[:, p * 128 : (p + 1) * 128]
        resid_out[:, g * 256 : (g + 1) * 256] = wide.astype(BF16)


def block_terms(resid, a, b, c, cube, even, odd):
    rank = a.shape[1]
    turned, pairs_ab = [], []
    for g in range(SIDE // 4):
        b4 = b[g * 4 : g * 4 + 4]
        pairs_ab.append((b4[:, None, :] * a[None, :, :]).reshape(4 * SIDE, rank))
        flip = resid[:, g * 256 : (g + 1) * 256].T
        turned += [flip[q * SIDE : (q + 1) * SIDE] for q in range(4)]
    term_c = jnp.dot(
        jnp.concatenate(turned, axis=1),
        jnp.concatenate(pairs_ab, axis=0),
        preferred_element_type=F32,
    )
    low = lax.broadcasted_iota(jnp.int32, (SIDE // 2, 128), 1) < SIDE
    rows, pairs_ac = [], []
    for g in range(SIDE // 4):
        x = [cube[pl.ds(g * 4 + q, SIDE // 2, stride=PITCH), :] for q in range(4)]
        y = [pltpu.roll(v, SIDE, 1) for v in x]
        evens = [jnp.where(low, x[0], y[1]), jnp.where(low, x[2], y[3])]
        odds = [jnp.where(low, y[0], x[1]), jnp.where(low, y[2], x[3])]
        both = [jnp.concatenate(evens, axis=1), jnp.concatenate(odds, axis=1)]
        rows.append(jnp.concatenate(both, axis=0).astype(BF16))
        pairs_ac.append((a[g * 4 : g * 4 + 4][:, None, :] * c[None, :, :]).reshape(4 * SIDE, rank))
    mixed = jnp.dot(
        jnp.concatenate(rows, axis=1),
        jnp.concatenate(pairs_ac, axis=0),
        preferred_element_type=F32,
    )
    half = SIDE // 2
    for u in range(2):
        even[pl.ds(u, half, stride=2), :] = mixed[u * half : (u + 1) * half, :128]
        odd[pl.ds(u, half, stride=2), :] = mixed[u * half : (u + 1) * half, 128:]
    term_b = jnp.concatenate([even[...], odd[...]], axis=1)
    return term_b, term_c


def run_pick(blocks, ids, hours, own):
    rank = hours.shape[1]

    def kernel(ids, hours, own, out, same, sem, own_sem):
        copies = [pltpu.make_async_copy(own, same, own_sem)]
        copies[0].start()
        for t in range(blocks):
            at = pl.multiple_of(ids[8 + 4 * blocks + t] * SIDE, SIDE)
            copies.append(
                pltpu.make_async_copy(
                    hours.at[pl.ds(at, SIDE)], out.at[pl.ds(t * SIDE, SIDE)], sem.at[t]
                )
            )
            copies[-1].start()
        for copy in copies:
            copy.wait()

    grant = 4 * blocks * SIDE * rank + 4 * own.size + (2 << 20)
    return pl.pallas_call(
        kernel,
        in_specs=[SMEM, HBM, ANY],
        out_specs=[VMEM, VMEM],
        out_shape=[
            jax.ShapeDtypeStruct((blocks * SIDE, rank), BF16),
            jax.ShapeDtypeStruct(own.shape, BF16),
        ],
        scratch_shapes=[pltpu.SemaphoreType.DMA((blocks,)), pltpu.SemaphoreType.DMA],
        compiler_params=pltpu.CompilerParams(vmem_limit_bytes=grant),
        cost_estimate=pl.CostEstimate(flops=SLOW // 10, bytes_accessed=0, transcendentals=0),
        name="pick_hours",
    )(ids, hours, own)


def main_kernel(shape, ids, counts, hours, near, far, *refs):
    grps, devs, local, hour_rows = shape
    depth = devs // 2
    hd_acc, hd_send, b_rows, resids, *refs = refs
    ring, resid_0, resid_1, cube_0, cube_1, even, odd, ring_sem, resid_sem = refs
    stages = ((resid_0, cube_0), (resid_1, cube_1))
    blocks = counts.shape[0]
    hour_part = hour_rows // (2 * grps)
    hour_blocks = hour_part // SIDE
    dst_part = local // grps
    part = hour_part + depth * dst_part
    half = depth * local
    base = 8

    def fetch(t):
        slot = lax.rem(t, RING)
        return pltpu.make_async_copy(counts.at[t], ring.at[slot], ring_sem.at[slot])

    def put(t, way):
        return pltpu.make_async_copy(stages[way][0], resids.at[t], resid_sem.at[way])

    ahead = 2
    for t in range(ahead):
        fetch(t).start()
    hd_acc[...] = jnp.zeros_like(hd_acc)
    for t in range(ahead, min(RING, blocks)):
        fetch(t).start()
    me, grp = ids[0], ids[1]
    core = me & 1

    def pick(at, other):
        at = pl.ds(pl.multiple_of(at, SIDE), SIDE)
        return jnp.where(other == 1, far[at, :], near[at, :])

    def dst_place(t):
        dst_from = ids[base + 2 * blocks + t] ^ me
        row = ids[base + 3 * blocks + t] * SIDE
        turn = (row // dst_part) ^ grp
        return dst_from & 1, turn, (dst_from >> 1) * dst_part + row % dst_part

    def rows_of(t):
        src_from = ids[base + t] ^ me
        a = pick((src_from >> 1) * local + ids[base + blocks + t] * SIDE, src_from & 1)
        other, turn, inner = dst_place(t)
        b = pick(half + turn * (depth * dst_part) + inner, other)
        return a, b, hours[pl.ds(pl.multiple_of(t * SIDE, SIDE), SIDE), :]

    def first(t, way):
        a, b, c = rows_of(t)
        b_rows[pl.ds(pl.multiple_of(t * SIDE, SIDE), SIDE), :] = b
        block_resid(ring.at[lax.rem(t, RING)], a, b, c, *stages[way])

    def second(t, way):
        a, b, c = rows_of(t)
        resid, cube = stages[way]
        term_b, term_c = block_terms(resid, a, b, c, cube, even, odd)
        other, turn, inner = dst_place(t)
        hour = ids[base + 4 * blocks + t]
        d_at = (other * grps + turn) * part + hour_part + inner
        home = hour // hour_blocks
        h_at = (((home // grps) ^ core) * grps + ((home % grps) ^ grp)) * part
        h_at = h_at + (hour % hour_blocks) * SIDE
        hd_acc[pl.ds(pl.multiple_of(d_at, SIDE), SIDE), :] += term_b
        hd_acc[pl.ds(pl.multiple_of(h_at, SIDE), SIDE), :] += term_c

    def step(t, way, guard):
        fetch(t).wait()

        if guard is None:
            put(t - 2, way).wait()
        else:

            @pl.when(guard)
            def _():
                put(t - 2, way).wait()

        first(t, way)
        second(t - 1, 1 - way)
        put(t, way).start()

        @pl.when(t - 1 + RING < blocks)
        def _():
            fetch(t - 1 + RING).start()

    def visit(i, carry):
        step(2 * i - 1, 1, i > 1)
        step(2 * i, 0, None)
        return carry

    last = blocks - 1
    fetch(0).wait()
    first(0, 0)
    put(0, 0).start()
    lax.fori_loop(1, blocks // 2, visit, 0)
    step(last, 1, None)
    second(last, 1)
    hd_half = grps * part
    hd_send[...] = hd_acc[pl.ds(hd_half, hd_half), :].astype(BF16)
    put(last - 1, 0).wait()
    put(last, 1).wait()


def src_kernel(shape, first, last, ids, resids, b_rows, hours, after, *refs):
    devs, local = shape
    depth = devs // 2
    fresh = first == 0
    blocks = resids.shape[0]
    refs = refs if fresh else refs[1:]
    s_acc, *sends, ring, sem = refs
    me, base = ids[0], 8

    def fetch(t):
        slot = lax.rem(t - first, RING)
        return pltpu.make_async_copy(resids.at[t], ring.at[slot], sem.at[slot])

    for t in range(first, min(first + RING, last)):
        fetch(t).start()
    if fresh:
        s_acc[...] = jnp.zeros_like(s_acc)

    def visit(t, carry):
        src_from = ids[base + t] ^ me
        src_slot = ids[base + blocks + t]
        z, order, steps = src_from >> 1, 0, depth // 2
        while steps:
            order = order + (z & 1) * steps
            z, steps = z >> 1, steps // 2
        s_at = ((src_from & 1) * depth + order) * local + src_slot * SIDE
        s_at = pl.multiple_of(s_at, SIDE)
        here = pl.ds(pl.multiple_of(t * SIDE, SIDE), SIDE)
        b, c = b_rows[here, :], hours[here, :]
        fetch(t).wait()
        resid = ring[lax.rem(t - first, RING)]
        pairs = [
            (b[g * 4 : g * 4 + 4][:, None, :] * c[None, :, :]).reshape(4 * SIDE, b.shape[1])
            for g in range(SIDE // 4)
        ]
        terms = []
        for at in range(0, b.shape[1], 128):
            columns = jnp.concatenate([p[:, at : at + 128] for p in pairs], axis=0)
            terms.append(jnp.dot(resid, columns, preferred_element_type=F32))
        s_acc[pl.ds(s_at, SIDE), :] += jnp.concatenate(terms, axis=1)

        @pl.when(t + RING < last)
        def _():
            fetch(t + RING).start()

        return carry

    lax.fori_loop(first, last, visit, 0)
    for send in sends:
        send[...] = s_acc[pl.ds(depth * local, depth * local), :].astype(BF16)


def size_of(shapes):
    return sum(jnp.dtype(t).itemsize * functools.reduce(lambda x, y: x * y, s) for s, t in shapes)


def run_main(shape, ids, counts, hours, near, far):
    grps, devs, local, hour_rows = shape
    rank = hours.shape[1]
    hd_rows = hour_rows + devs * local
    outs = [
        ((hd_rows, rank), F32),
        ((hd_rows // 2, rank), BF16),
        (hours.shape, BF16),
    ]
    scratch = [
        ((RING,) + counts.shape[1:], BF16),
        (counts.shape[1:], BF16),
        (counts.shape[1:], BF16),
        ((SIDE // 2 * PITCH, 128), F32),
        ((SIDE // 2 * PITCH, 128), F32),
        ((SIDE, 128), F32),
        ((SIDE, 128), F32),
    ]
    need = max(size_of(outs) + size_of(scratch) + (8 << 20), GRANT)
    return pl.pallas_call(
        functools.partial(main_kernel, shape),
        in_specs=[SMEM, HBM, VMEM, VMEM, VMEM],
        out_specs=[VMEM] * 3 + [HBM],
        out_shape=[jax.ShapeDtypeStruct(s, t) for s, t in outs]
        + [jax.ShapeDtypeStruct(counts.shape, BF16)],
        scratch_shapes=[pltpu.VMEM(s, t) for s, t in scratch]
        + [
            pltpu.SemaphoreType.DMA((RING,)),
            pltpu.SemaphoreType.DMA((2,)),
        ],
        compiler_params=pltpu.CompilerParams(vmem_limit_bytes=need),
        cost_estimate=pl.CostEstimate(
            flops=6 * counts.size * rank,
            bytes_accessed=counts.size * 4,
            transcendentals=counts.size,
        ),
        name="hour_dst_terms",
    )(ids, counts, hours, near, far)


def run_src(shape, first, last, ids, resids, b_rows, hours, after, s_acc=None):
    devs, local = shape
    rank = hours.shape[1]
    blocks, rows, columns = resids.shape
    more = [] if s_acc is None else [s_acc]
    outs = [((devs * local, rank), F32)]
    if last == blocks:
        outs.append(((devs * local // 2, rank), BF16))
    need = size_of(outs) + size_of([((RING, rows, columns), BF16)]) + (8 << 20)
    each = rows * columns
    return pl.pallas_call(
        functools.partial(src_kernel, shape, first, last),
        in_specs=[SMEM, HBM, VMEM, VMEM, ANY] + [VMEM] * len(more),
        out_specs=[VMEM] * len(outs),
        out_shape=[jax.ShapeDtypeStruct(s, t) for s, t in outs],
        scratch_shapes=[
            pltpu.VMEM((RING, rows, columns), BF16),
            pltpu.SemaphoreType.DMA((RING,)),
        ],
        input_output_aliases={5: 0} if more else {},
        compiler_params=pltpu.CompilerParams(vmem_limit_bytes=max(need, SRC_GRANT)),
        cost_estimate=pl.CostEstimate(
            flops=8 * (last - first) * each * rank,
            bytes_accessed=(last - first) * each * 2,
            transcendentals=0,
        ),
        name="src_terms",
    )(ids, resids, b_rows, hours, after, *more)


def call(kernel, name, ins, outs, specs=None, scratch=(), weight=0):
    shapes = [(x.shape, x.dtype) for x in ins] + list(outs) + list(scratch)
    return pl.pallas_call(
        kernel,
        in_specs=specs or [VMEM] * len(ins),
        out_specs=[VMEM] * len(outs),
        out_shape=[jax.ShapeDtypeStruct(s, t) for s, t in outs],
        scratch_shapes=[pltpu.VMEM(s, t) for s, t in scratch],
        compiler_params=pltpu.CompilerParams(vmem_limit_bytes=size_of(shapes) + (4 << 20)),
        cost_estimate=pl.CostEstimate(
            flops=weight, bytes_accessed=size_of(shapes), transcendentals=0
        ),
        name=name,
    )(*ins)


def shares(rows, rank, ways):
    return [((rows, rank), F32)] + [((rows, rank), BF16)] * (ways - 1)


def run_cut(ways, acc, got, after):
    rows, rank = got.shape[0] // ways, got.shape[1]

    def kernel(acc, got, after, *outs):
        for m in range(ways):
            at = pl.ds(m * rows, rows)
            outs[m][...] = (acc[at, :] + got[at, :].astype(F32)).astype(outs[m].dtype)
        outs[ways][...] = jnp.zeros_like(outs[ways])

    outs = shares(rows, rank, ways) + [((8, 128), F32)]
    return call(kernel, "core_hours_dst", (acc, got, after), outs, specs=[VMEM, VMEM, ANY])


def halve(keep, got, stay, send):
    rows = got.shape[0]
    half = rows // 2
    stay[...] = keep[pl.ds(0, half), :] + got[pl.ds(0, half), :].astype(F32)
    at = pl.ds(half, half)
    send[...] = (keep[at, :] + got[at, :].astype(F32)).astype(BF16)


def halves(got):
    rows, rank = got.shape
    return [((rows // 2, rank), F32), ((rows // 2, rank), BF16)]


def run_halve(keep, got):
    return call(halve, "src_half", (keep, got), halves(got))


def total(refs):
    acc = refs[0][...]
    for r in refs[1:]:
        acc = acc + r[...].astype(F32)
    return acc


def run_grp(hour_part, depth, parts):
    rows, rank = parts[0].shape
    ways = len(parts)
    each, dst_rows = hour_part // depth, (rows - hour_part) // depth

    def kernel(*refs):
        outs, acc = refs[ways:-1], refs[-1]
        z = lax.axis_index("dev") >> 1
        acc[...] = total(refs[:ways])
        for m in range(depth):
            kind = outs[m].dtype
            at = pl.multiple_of((z ^ m) * each, each)
            outs[m][pl.ds(0, each), :] = acc[pl.ds(at, each), :].astype(kind)
            at = hour_part + m * dst_rows
            outs[m][pl.ds(each, dst_rows), :] = acc[pl.ds(at, dst_rows), :].astype(kind)

    return call(
        kernel,
        "grp_sum",
        parts,
        shares(each + dst_rows, rank, depth),
        scratch=[((rows, rank), F32)],
        weight=SLOW,
    )


def run_z(parts, hour_rows):
    rows, rank = parts[0].shape

    def kernel(*refs):
        hour, dst = refs[-2:]
        acc = total(refs[:-2]) * (1.0 / SIDE)
        hour[...] = acc[:hour_rows].astype(BF16)
        dst[...] = acc[hour_rows:].astype(BF16)

    outs = [((hour_rows, rank), BF16), ((rows - hour_rows, rank), BF16)]
    return call(kernel, "z_sum", parts, outs, weight=SLOW)


def run_join(parts, keep=None, got=None, passed=None):
    rows = [p.shape[0] for p in parts]
    outs = [((sum(rows), parts[0].shape[1]), BF16)]
    ins = tuple(parts)
    if got is not None:
        ins += (keep, got)
        outs += halves(got)
    if passed is not None:
        ins += (passed,)
        outs += [(passed.shape, BF16)]

    def kernel(*refs):
        if got is not None:
            halve(refs[len(parts)], refs[len(parts) + 1], refs[-2], refs[-1])
        if passed is not None:
            refs[-1][...] = refs[len(parts)][...]
        out, at = refs[len(ins)], 0
        for ref, n_rows in zip(refs, rows):
            out[at : at + n_rows, :] = ref[...]
            at += n_rows

    return call(kernel, "join", ins, outs)


def run_src_sum(keep, got, joined):
    def kernel(keep, got, joined, out, same):
        out[...] = (keep[...] + got[...].astype(F32)) * (1.0 / SIDE)
        same[...] = joined[...]

    outs = [(keep.shape, F32), (joined.shape, BF16)]
    return call(kernel, "src_sum", (keep, got, joined), outs)


def run_place(sizes, hour_rows, parts, other, dst_rows, so_far=None):
    grps, devs = sizes
    depth = devs // 2
    rank = parts[0].shape[1]
    part = hour_rows // (2 * grps)
    rows = part // depth
    near = so_far is None

    def kernel(*refs):
        ins = refs[:grps]
        if near:
            hours, dst, stage, sem, dst_stage = refs[grps:]
        else:
            hours, stage, sem = refs[grps + 1 :]
        dev, grp = lax.axis_index("dev"), lax.axis_index("grp")
        core, z = dev & 1, dev >> 1
        copies = []
        if near:
            for m in range(grps):
                at = pl.multiple_of((grp ^ m) * dst_rows, dst_rows)
                new = ins[m][pl.ds(part, dst_rows), :].astype(F32)
                dst_stage[pl.ds(at, dst_rows), :] = new
            copies.append(pltpu.make_async_copy(dst_stage, dst, sem.at[grps]))
            copies[-1].start()
        for m in range(grps):
            for k in range(depth):
                at = pl.multiple_of((z ^ k) * rows, rows)
                stage[m, pl.ds(at, rows), :] = ins[m][pl.ds(k * rows, rows), :].astype(F32)
            home = pl.multiple_of(((core ^ other) * grps + (grp ^ m)) * part, part)
            copies.append(
                pltpu.make_async_copy(stage.at[m], hours.at[pl.ds(home, part)], sem.at[m])
            )
            copies[-1].start()
        for copy in copies:
            copy.wait()

    outs = [((hour_rows, rank), F32)]
    scratch = [((grps, part, rank), F32)]
    extra = [((grps * dst_rows, rank), F32)] if near else []
    need = size_of([(p.shape, p.dtype) for p in parts] + scratch + extra) + (4 << 20)
    return pl.pallas_call(
        kernel,
        in_specs=[VMEM] * grps + [HBM] * (not near),
        out_specs=[HBM] * len(outs + extra),
        out_shape=[jax.ShapeDtypeStruct(s, t) for s, t in outs + extra],
        scratch_shapes=[pltpu.VMEM(s, t) for s, t in scratch]
        + [pltpu.SemaphoreType.DMA((grps + 1,))]
        + [pltpu.VMEM(s, t) for s, t in extra],
        input_output_aliases={} if near else {grps: 0},
        compiler_params=pltpu.CompilerParams(vmem_limit_bytes=need),
        cost_estimate=pl.CostEstimate(
            flops=SLOW // 10 if near else 0, bytes_accessed=0, transcendentals=0
        ),
        name="place",
    )(*parts, *([] if near else [so_far]))


def per_device(
    sizes,
    counts,
    src_factor,
    dst_factor,
    hour_factor,
    src_owner,
    src_slot,
    dst_owner,
    dst_slot,
    hour_block,
):
    grps, devs = sizes
    depth = devs // 2
    local = src_factor.shape[0]
    hour_rows = hour_factor.shape[0]
    me = lax.axis_index("dev").astype(jnp.int32)
    grp = lax.axis_index("grp").astype(jnp.int32)
    place = jnp.stack([me, grp] + [me * 0] * 6)
    ids = jnp.concatenate(
        [place, src_owner[:, 0], src_slot, dst_owner[:, 0], dst_slot, hour_block]
    )
    dst_part = local // grps
    dst_own = lax.dynamic_slice_in_dim(dst_factor, grp * dst_part, dst_part, 0)
    dst_z = [dst_own] + [swap(dst_own, "dev", devs, 2 * m) for m in range(1, depth)]
    src_z = [src_factor] + [swap(src_factor, "dev", devs, 2 * m) for m in range(1, depth)]
    blocks = counts.shape[0]
    picked, src_same = run_pick(blocks, ids, hour_factor, src_factor)
    dst_here, src_z[1] = run_join(dst_z, passed=src_z[1])
    dsts = [dst_here] + [swap(dst_here, "grp", grps, m) for m in range(1, grps)]
    near = run_join([src_same] + src_z[1:] + dsts)[0]
    far = swap(near, "dev", devs, 1)
    shape = (grps, devs, local, hour_rows)
    hd_acc, hd_send, b_rows, resids = run_main(shape, ids, counts, picked, near, far)

    def exchange(parts, axis, size, step):
        return [parts[0]] + [swap(x, axis, size, step * m) for m, x in enumerate(parts) if m]

    hd_got = swap(hd_send, "dev", devs, 1)
    src = functools.partial(run_src, (devs, local))
    early = blocks // 8
    s_acc = src(0, early, ids, resids, b_rows, picked, hd_send)[0]
    *hd, cut_done = run_cut(grps, hd_acc, hd_got, s_acc)
    cut_done = swap(cut_done, "dev", devs, 1)
    s_acc, s_send = src(early, blocks, ids, resids, b_rows, picked, cut_done, s_acc)
    s_got = swap(s_send, "dev", devs, 1)
    hour_part = hour_rows // (2 * grps)
    hd = run_grp(hour_part, depth, exchange(hd, "grp", grps, 1))
    hour_each = hour_part // depth
    s_keep, s_send = run_halve(s_acc, s_got)
    hour, dst = run_z(exchange(hd, "dev", devs, 2), hour_each)
    s_got = swap(s_send, "dev", devs, 2)
    back = [hour] + [swap(hour, "dev", devs, 2 * m) for m in range(1, depth)]
    joined, s_keep, s_send = run_join(back + [dst], s_keep, s_got)
    step = 4
    s_got = swap(s_send, "dev", devs, step)
    while 2 * step < devs:
        s_keep, s_send = run_halve(s_keep, s_got)
        step *= 2
        s_got = swap(s_send, "dev", devs, step)
    grad_src, same = run_src_sum(s_keep, s_got, joined)
    near = [joined] + [swap(joined, "grp", grps, m) for m in range(1, grps)]
    far = [swap(x, "dev", devs, 1) for x in [same] + near[1:]]
    grad_hour, grad_dst = run_place(sizes, hour_rows, near, 0, dst_part)
    grad_hour = run_place(sizes, hour_rows, far, 1, dst_part, grad_hour)[0]
    return grad_src, grad_dst, grad_hour


def solution(mesh):
    in_specs = (
        P(("grp", "dev"), None, None),
        P(("grp", "dev"), None),
        P("dev", None),
        P(),
        P(("grp", "dev"), None),
        P(("grp", "dev")),
        P(("grp", "dev"), None),
        P(("grp", "dev")),
        P(("grp", "dev")),
    )
    out_specs = (P(("grp", "dev"), None), P("dev", None), P())
    return jax.shard_map(
        functools.partial(per_device, mesh_sizes(mesh)),
        mesh=mesh,
        in_specs=in_specs,
        out_specs=out_specs,
        check_vma=False,
    )
```

```python
import functools

import jax
import jax.numpy as jnp
from jax import lax
from jax.experimental import pallas as pl
from jax.experimental.pallas import tpu as pltpu
from jax.sharding import PartitionSpec as P

F32 = jnp.float32
BF16 = jnp.bfloat16
SIDE = 64
RING = 8
PITCH = 72
GRANT = 36 << 20
SRC_GRANT = 44 << 20
SLOW = 10**11

VMEM = pl.BlockSpec(memory_space=pltpu.VMEM)
SMEM = pl.BlockSpec(memory_space=pltpu.SMEM)
ANY = pl.BlockSpec(memory_space=pl.ANY)
HBM = pl.BlockSpec(memory_space=pltpu.HBM)


def mesh_sizes(mesh):
    return mesh.shape["grp"], mesh.shape["dev"]


def swap(x, axis, size, mask):
    return lax.ppermute(x, axis, [(i, i ^ mask) for i in range(size)])


def block_resid(count, a, b, c, resid_out, cube):
    rank = a.shape[1]
    for g in range(SIDE // 4):
        b4 = b[g * 4 : g * 4 + 4]
        bc = (b4[:, None, :] * c[None, :, :]).reshape(4 * SIDE, rank)
        theta = lax.dot_general(a, bc, (((1,), (1,)), ((), ())), preferred_element_type=F32)
        wide = jnp.exp(theta) - count[:, g * 256 : (g + 1) * 256].astype(F32)
        for p in range(2):
            cube[pl.ds((g * 2 + p) * PITCH, SIDE), :] = wide[:, p * 128 : (p + 1) * 128]
        resid_out[:, g * 256 : (g + 1) * 256] = wide.astype(BF16)


def block_terms(resid, a, b, c, cube, even, odd):
    rank = a.shape[1]
    turned, pairs_ab = [], []
    for g in range(SIDE // 4):
        b4 = b[g * 4 : g * 4 + 4]
        pairs_ab.append((b4[:, None, :] * a[None, :, :]).reshape(4 * SIDE, rank))
        flip = resid[:, g * 256 : (g + 1) * 256].T
        turned += [flip[q * SIDE : (q + 1) * SIDE] for q in range(4)]
    term_c = jnp.dot(
        jnp.concatenate(turned, axis=1),
        jnp.concatenate(pairs_ab, axis=0),
        preferred_element_type=F32,
    )
    low = lax.broadcasted_iota(jnp.int32, (SIDE // 2, 128), 1) < SIDE
    rows, pairs_ac = [], []
    for g in range(SIDE // 4):
        x = [cube[pl.ds(g * 4 + q, SIDE // 2, stride=PITCH), :] for q in range(4)]
        y = [pltpu.roll(v, SIDE, 1) for v in x]
        evens = [jnp.where(low, x[0], y[1]), jnp.where(low, x[2], y[3])]
        odds = [jnp.where(low, y[0], x[1]), jnp.where(low, y[2], x[3])]
        both = [jnp.concatenate(evens, axis=1), jnp.concatenate(odds, axis=1)]
        rows.append(jnp.concatenate(both, axis=0).astype(BF16))
        pairs_ac.append((a[g * 4 : g * 4 + 4][:, None, :] * c[None, :, :]).reshape(4 * SIDE, rank))
    mixed = jnp.dot(
        jnp.concatenate(rows, axis=1),
        jnp.concatenate(pairs_ac, axis=0),
        preferred_element_type=F32,
    )
    half = SIDE // 2
    for u in range(2):
        even[pl.ds(u, half, stride=2), :] = mixed[u * half : (u + 1) * half, :128]
        odd[pl.ds(u, half, stride=2), :] = mixed[u * half : (u + 1) * half, 128:]
    term_b = jnp.concatenate([even[...], odd[...]], axis=1)
    return term_b, term_c


def run_pick(blocks, ids, hours, own):
    rank = hours.shape[1]

    def kernel(ids, hours, own, out, same, sem, own_sem):
        copies = [pltpu.make_async_copy(own, same, own_sem)]
        copies[0].start()
        for t in range(blocks):
            at = pl.multiple_of(ids[8 + 4 * blocks + t] * SIDE, SIDE)
            copies.append(
                pltpu.make_async_copy(
                    hours.at[pl.ds(at, SIDE)], out.at[pl.ds(t * SIDE, SIDE)], sem.at[t]
                )
            )
            copies[-1].start()
        for copy in copies:
            copy.wait()

    grant = 4 * blocks * SIDE * rank + 4 * own.size + (2 << 20)
    return pl.pallas_call(
        kernel,
        in_specs=[SMEM, HBM, ANY],
        out_specs=[VMEM, VMEM],
        out_shape=[
            jax.ShapeDtypeStruct((blocks * SIDE, rank), BF16),
            jax.ShapeDtypeStruct(own.shape, BF16),
        ],
        scratch_shapes=[pltpu.SemaphoreType.DMA((blocks,)), pltpu.SemaphoreType.DMA],
        compiler_params=pltpu.CompilerParams(vmem_limit_bytes=grant),
        cost_estimate=pl.CostEstimate(flops=SLOW // 10, bytes_accessed=0, transcendentals=0),
        name="pick_hours",
    )(ids, hours, own)


def main_kernel(shape, ids, counts, hours, near, far, *refs):
    grps, devs, local, hour_rows = shape
    depth = devs // 2
    hd_acc, hd_send, b_rows, resids, *refs = refs
    ring, resid_0, resid_1, cube_0, cube_1, even, odd, ring_sem, resid_sem = refs
    stages = ((resid_0, cube_0), (resid_1, cube_1))
    blocks = counts.shape[0]
    hour_part = hour_rows // (2 * grps)
    hour_blocks = hour_part // SIDE
    dst_part = local // grps
    part = hour_part + depth * dst_part
    half = depth * local
    base = 8

    def fetch(t):
        slot = lax.rem(t, RING)
        return pltpu.make_async_copy(counts.at[t], ring.at[slot], ring_sem.at[slot])

    def put(t, way):
        return pltpu.make_async_copy(stages[way][0], resids.at[t], resid_sem.at[way])

    ahead = 2
    for t in range(ahead):
        fetch(t).start()
    hd_acc[...] = jnp.zeros_like(hd_acc)
    for t in range(ahead, min(RING, blocks)):
        fetch(t).start()
    me, grp = ids[0], ids[1]
    core = me & 1

    def pick(at, other):
        at = pl.ds(pl.multiple_of(at, SIDE), SIDE)
        return jnp.where(other == 1, far[at, :], near[at, :])

    def dst_place(t):
        dst_from = ids[base + 2 * blocks + t] ^ me
        row = ids[base + 3 * blocks + t] * SIDE
        turn = (row // dst_part) ^ grp
        return dst_from & 1, turn, (dst_from >> 1) * dst_part + row % dst_part

    def rows_of(t):
        src_from = ids[base + t] ^ me
        a = pick((src_from >> 1) * local + ids[base + blocks + t] * SIDE, src_from & 1)
        other, turn, inner = dst_place(t)
        b = pick(half + turn * (depth * dst_part) + inner, other)
        return a, b, hours[pl.ds(pl.multiple_of(t * SIDE, SIDE), SIDE), :]

    def first(t, way):
        a, b, c = rows_of(t)
        b_rows[pl.ds(pl.multiple_of(t * SIDE, SIDE), SIDE), :] = b
        block_resid(ring.at[lax.rem(t, RING)], a, b, c, *stages[way])

    def second(t, way):
        a, b, c = rows_of(t)
        resid, cube = stages[way]
        term_b, term_c = block_terms(resid, a, b, c, cube, even, odd)
        other, turn, inner = dst_place(t)
        hour = ids[base + 4 * blocks + t]
        d_at = (other * grps + turn) * part + hour_part + inner
        home = hour // hour_blocks
        h_at = (((home // grps) ^ core) * grps + ((home % grps) ^ grp)) * part
        h_at = h_at + (hour % hour_blocks) * SIDE
        hd_acc[pl.ds(pl.multiple_of(d_at, SIDE), SIDE), :] += term_b
        hd_acc[pl.ds(pl.multiple_of(h_at, SIDE), SIDE), :] += term_c

    def step(t, way, guard):
        fetch(t).wait()

        if guard is None:
            put(t - 2, way).wait()
        else:

            @pl.when(guard)
            def _():
                put(t - 2, way).wait()

        first(t, way)
        second(t - 1, 1 - way)
        put(t, way).start()

        @pl.when(t - 1 + RING < blocks)
        def _():
            fetch(t - 1 + RING).start()

    def visit(i, carry):
        step(2 * i - 1, 1, i > 1)
        step(2 * i, 0, None)
        return carry

    last = blocks - 1
    fetch(0).wait()
    first(0, 0)
    put(0, 0).start()
    lax.fori_loop(1, blocks // 2, visit, 0)
    step(last, 1, None)
    second(last, 1)
    hd_half = grps * part
    hd_send[...] = hd_acc[pl.ds(hd_half, hd_half), :].astype(BF16)
    put(last - 1, 0).wait()
    put(last, 1).wait()


def src_kernel(shape, first, last, ids, resids, b_rows, hours, after, *refs):
    devs, local = shape
    depth = devs // 2
    fresh = first == 0
    blocks = resids.shape[0]
    refs = refs if fresh else refs[1:]
    s_acc, *sends, ring, sem = refs
    me, base = ids[0], 8

    def fetch(t):
        slot = lax.rem(t - first, RING)
        return pltpu.make_async_copy(resids.at[t], ring.at[slot], sem.at[slot])

    for t in range(first, min(first + RING, last)):
        fetch(t).start()
    if fresh:
        s_acc[...] = jnp.zeros_like(s_acc)

    def visit(t, carry):
        src_from = ids[base + t] ^ me
        src_slot = ids[base + blocks + t]
        z, order, steps = src_from >> 1, 0, depth // 2
        while steps:
            order = order + (z & 1) * steps
            z, steps = z >> 1, steps // 2
        s_at = ((src_from & 1) * depth + order) * local + src_slot * SIDE
        s_at = pl.multiple_of(s_at, SIDE)
        here = pl.ds(pl.multiple_of(t * SIDE, SIDE), SIDE)
        b, c = b_rows[here, :], hours[here, :]
        fetch(t).wait()
        resid = ring[lax.rem(t - first, RING)]
        pairs = [
            (b[g * 4 : g * 4 + 4][:, None, :] * c[None, :, :]).reshape(4 * SIDE, b.shape[1])
            for g in range(SIDE // 4)
        ]
        terms = []
        for at in range(0, b.shape[1], 128):
            columns = jnp.concatenate([p[:, at : at + 128] for p in pairs], axis=0)
            terms.append(jnp.dot(resid, columns, preferred_element_type=F32))
        s_acc[pl.ds(s_at, SIDE), :] += jnp.concatenate(terms, axis=1)

        @pl.when(t + RING < last)
        def _():
            fetch(t + RING).start()

        return carry

    lax.fori_loop(first, last, visit, 0)
    at = depth * local
    for send in sends:
        rows = send.shape[0]
        send[...] = s_acc[pl.ds(at, rows), :].astype(BF16)
        at += rows


def size_of(shapes):
    return sum(jnp.dtype(t).itemsize * functools.reduce(lambda x, y: x * y, s) for s, t in shapes)


def run_main(shape, ids, counts, hours, near, far):
    grps, devs, local, hour_rows = shape
    rank = hours.shape[1]
    hd_rows = hour_rows + devs * local
    outs = [
        ((hd_rows, rank), F32),
        ((hd_rows // 2, rank), BF16),
        (hours.shape, BF16),
    ]
    scratch = [
        ((RING,) + counts.shape[1:], BF16),
        (counts.shape[1:], BF16),
        (counts.shape[1:], BF16),
        ((SIDE // 2 * PITCH, 128), F32),
        ((SIDE // 2 * PITCH, 128), F32),
        ((SIDE, 128), F32),
        ((SIDE, 128), F32),
    ]
    need = max(size_of(outs) + size_of(scratch) + (8 << 20), GRANT)
    return pl.pallas_call(
        functools.partial(main_kernel, shape),
        in_specs=[SMEM, HBM, VMEM, VMEM, VMEM],
        out_specs=[VMEM] * 3 + [HBM],
        out_shape=[jax.ShapeDtypeStruct(s, t) for s, t in outs]
        + [jax.ShapeDtypeStruct(counts.shape, BF16)],
        scratch_shapes=[pltpu.VMEM(s, t) for s, t in scratch]
        + [
            pltpu.SemaphoreType.DMA((RING,)),
            pltpu.SemaphoreType.DMA((2,)),
        ],
        compiler_params=pltpu.CompilerParams(vmem_limit_bytes=need),
        cost_estimate=pl.CostEstimate(
            flops=6 * counts.size * rank,
            bytes_accessed=counts.size * 4,
            transcendentals=counts.size,
        ),
        name="hour_dst_terms",
    )(ids, counts, hours, near, far)


def run_src(shape, first, last, ids, resids, b_rows, hours, after, s_acc=None):
    devs, local = shape
    rank = hours.shape[1]
    blocks, rows, columns = resids.shape
    more = [] if s_acc is None else [s_acc]
    outs = [((devs * local, rank), F32)]
    if last == blocks:
        outs += [((devs * local // 4, rank), BF16)] * 2
    need = size_of(outs) + size_of([((RING, rows, columns), BF16)]) + (8 << 20)
    each = rows * columns
    return pl.pallas_call(
        functools.partial(src_kernel, shape, first, last),
        in_specs=[SMEM, HBM, VMEM, VMEM, ANY] + [VMEM] * len(more),
        out_specs=[VMEM] * len(outs),
        out_shape=[jax.ShapeDtypeStruct(s, t) for s, t in outs],
        scratch_shapes=[
            pltpu.VMEM((RING, rows, columns), BF16),
            pltpu.SemaphoreType.DMA((RING,)),
        ],
        input_output_aliases={5: 0} if more else {},
        compiler_params=pltpu.CompilerParams(vmem_limit_bytes=max(need, SRC_GRANT)),
        cost_estimate=pl.CostEstimate(
            flops=8 * (last - first) * each * rank,
            bytes_accessed=(last - first) * each * 2,
            transcendentals=0,
        ),
        name="src_terms",
    )(ids, resids, b_rows, hours, after, *more)


def call(kernel, name, ins, outs, specs=None, scratch=(), weight=0):
    shapes = [(x.shape, x.dtype) for x in ins] + list(outs) + list(scratch)
    return pl.pallas_call(
        kernel,
        in_specs=specs or [VMEM] * len(ins),
        out_specs=[VMEM] * len(outs),
        out_shape=[jax.ShapeDtypeStruct(s, t) for s, t in outs],
        scratch_shapes=[pltpu.VMEM(s, t) for s, t in scratch],
        compiler_params=pltpu.CompilerParams(vmem_limit_bytes=size_of(shapes) + (4 << 20)),
        cost_estimate=pl.CostEstimate(
            flops=weight, bytes_accessed=size_of(shapes), transcendentals=0
        ),
        name=name,
    )(*ins)


def shares(rows, rank, ways):
    return [((rows, rank), F32)] + [((rows, rank), BF16)] * (ways - 1)


def run_cut(ways, acc, got, after):
    rows, rank = got.shape[0] // ways, got.shape[1]

    def kernel(acc, got, after, *outs):
        for m in range(ways):
            at = pl.ds(m * rows, rows)
            outs[m][...] = (acc[at, :] + got[at, :].astype(F32)).astype(outs[m].dtype)
        outs[ways][...] = jnp.zeros_like(outs[ways])

    outs = shares(rows, rank, ways) + [((8, 128), F32)]
    return call(kernel, "core_hours_dst", (acc, got, after), outs, specs=[VMEM, VMEM, ANY])


def halve(keep, got, stay, send):
    rows = got.shape[0]
    half = rows // 2
    stay[...] = keep[pl.ds(0, half), :] + got[pl.ds(0, half), :].astype(F32)
    at = pl.ds(half, half)
    send[...] = (keep[at, :] + got[at, :].astype(F32)).astype(BF16)


def halves(got):
    rows, rank = got.shape
    return [((rows // 2, rank), F32), ((rows // 2, rank), BF16)]


def run_first_halve(keep, low, high):
    half, rank = low.shape

    def kernel(keep, low, high, stay, send):
        stay[...] = keep[pl.ds(0, half), :] + low[...].astype(F32)
        send[...] = (keep[pl.ds(half, half), :] + high[...].astype(F32)).astype(BF16)

    return call(
        kernel,
        "src_half",
        (keep, low, high),
        [((half, rank), F32), ((half, rank), BF16)],
    )


def run_halve(keep, got):
    return call(halve, "src_half", (keep, got), halves(got))


def total(refs):
    acc = refs[0][...]
    for r in refs[1:]:
        acc = acc + r[...].astype(F32)
    return acc


def run_grp(hour_part, depth, parts, after):
    rows, rank = parts[0].shape
    ways = len(parts)
    each, dst_rows = hour_part // depth, (rows - hour_part) // depth

    def kernel(*refs):
        outs, acc = refs[ways + 1 : -1], refs[-1]
        z = lax.axis_index("dev") >> 1
        acc[...] = total(refs[:ways])
        for m in range(depth):
            kind = outs[m].dtype
            at = pl.multiple_of((z ^ m) * each, each)
            outs[m][pl.ds(0, each), :] = acc[pl.ds(at, each), :].astype(kind)
            at = hour_part + m * dst_rows
            outs[m][pl.ds(each, dst_rows), :] = acc[pl.ds(at, dst_rows), :].astype(kind)

    return call(
        kernel,
        "grp_sum",
        (*parts, after),
        shares(each + dst_rows, rank, depth),
        specs=[VMEM] * ways + [ANY],
        scratch=[((rows, rank), F32)],
        weight=SLOW,
    )


def run_z(parts, hour_rows, keep, got):
    n = len(parts)
    rows, rank = parts[0].shape

    def kernel(*refs):
        keep, got, hour, dst, stay, send = refs[n:]
        halve(keep, got, stay, send)
        acc = total(refs[:n]) * (1.0 / SIDE)
        hour[...] = acc[:hour_rows].astype(BF16)
        dst[...] = acc[hour_rows:].astype(BF16)

    outs = [((hour_rows, rank), BF16), ((rows - hour_rows, rank), BF16)] + halves(got)
    return call(kernel, "z_sum", (*parts, keep, got), outs, weight=SLOW)


def run_join(parts, passed=None):
    rows = [p.shape[0] for p in parts]
    outs = [((sum(rows), parts[0].shape[1]), BF16)]
    ins = tuple(parts)
    if passed is not None:
        ins += (passed,)
        outs += [(passed.shape, BF16)]

    def kernel(*refs):
        if passed is not None:
            refs[-1][...] = refs[len(parts)][...]
        out, at = refs[len(ins)], 0
        for ref, n_rows in zip(refs, rows):
            out[at : at + n_rows, :] = ref[...]
            at += n_rows

    return call(kernel, "join", ins, outs)


def run_src_sum(keep, got, joined):
    def kernel(keep, got, joined, out, same):
        out[...] = (keep[...] + got[...].astype(F32)) * (1.0 / SIDE)
        same[...] = joined[...]

    outs = [(keep.shape, F32), (joined.shape, BF16)]
    return call(kernel, "src_sum", (keep, got, joined), outs)


def run_place(sizes, hour_rows, parts, other, dst_rows, so_far=None):
    grps, devs = sizes
    depth = devs // 2
    rank = parts[0].shape[1]
    part = hour_rows // (2 * grps)
    rows = part // depth
    near = so_far is None

    def kernel(*refs):
        ins = refs[:grps]
        if near:
            hours, dst, stage, sem, dst_stage = refs[grps:]
        else:
            hours, stage, sem = refs[grps + 1 :]
        dev, grp = lax.axis_index("dev"), lax.axis_index("grp")
        core, z = dev & 1, dev >> 1
        copies = []
        if near:
            for m in range(grps):
                at = pl.multiple_of((grp ^ m) * dst_rows, dst_rows)
                new = ins[m][pl.ds(part, dst_rows), :].astype(F32)
                dst_stage[pl.ds(at, dst_rows), :] = new
            copies.append(pltpu.make_async_copy(dst_stage, dst, sem.at[grps]))
            copies[-1].start()
        for m in range(grps):
            for k in range(depth):
                at = pl.multiple_of((z ^ k) * rows, rows)
                stage[m, pl.ds(at, rows), :] = ins[m][pl.ds(k * rows, rows), :].astype(F32)
            home = pl.multiple_of(((core ^ other) * grps + (grp ^ m)) * part, part)
            copies.append(
                pltpu.make_async_copy(stage.at[m], hours.at[pl.ds(home, part)], sem.at[m])
            )
            copies[-1].start()
        for copy in copies:
            copy.wait()

    outs = [((hour_rows, rank), F32)]
    scratch = [((grps, part, rank), F32)]
    extra = [((grps * dst_rows, rank), F32)] if near else []
    need = size_of([(p.shape, p.dtype) for p in parts] + scratch + extra) + (4 << 20)
    return pl.pallas_call(
        kernel,
        in_specs=[VMEM] * grps + [HBM] * (not near),
        out_specs=[HBM] * len(outs + extra),
        out_shape=[jax.ShapeDtypeStruct(s, t) for s, t in outs + extra],
        scratch_shapes=[pltpu.VMEM(s, t) for s, t in scratch]
        + [pltpu.SemaphoreType.DMA((grps + 1,))]
        + [pltpu.VMEM(s, t) for s, t in extra],
        input_output_aliases={} if near else {grps: 0},
        compiler_params=pltpu.CompilerParams(vmem_limit_bytes=need),
        cost_estimate=pl.CostEstimate(
            flops=SLOW // 10 if near else 0, bytes_accessed=0, transcendentals=0
        ),
        name="place",
    )(*parts, *([] if near else [so_far]))


def per_device(
    sizes,
    counts,
    src_factor,
    dst_factor,
    hour_factor,
    src_owner,
    src_slot,
    dst_owner,
    dst_slot,
    hour_block,
):
    grps, devs = sizes
    depth = devs // 2
    local = src_factor.shape[0]
    hour_rows = hour_factor.shape[0]
    me = lax.axis_index("dev").astype(jnp.int32)
    grp = lax.axis_index("grp").astype(jnp.int32)
    place = jnp.stack([me, grp] + [me * 0] * 6)
    ids = jnp.concatenate(
        [place, src_owner[:, 0], src_slot, dst_owner[:, 0], dst_slot, hour_block]
    )
    dst_part = local // grps
    dst_own = lax.dynamic_slice_in_dim(dst_factor, grp * dst_part, dst_part, 0)
    dst_z = [dst_own] + [swap(dst_own, "dev", devs, 2 * m) for m in range(1, depth)]
    src_z = [src_factor] + [swap(src_factor, "dev", devs, 2 * m) for m in range(1, depth)]
    blocks = counts.shape[0]
    picked, src_same = run_pick(blocks, ids, hour_factor, src_factor)
    dst_here, src_z[1] = run_join(dst_z, passed=src_z[1])
    dsts = [dst_here] + [swap(dst_here, "grp", grps, m) for m in range(1, grps)]
    near = run_join([src_same] + src_z[1:] + dsts)[0]
    far = swap(near, "dev", devs, 1)
    shape = (grps, devs, local, hour_rows)
    hd_acc, hd_send, b_rows, resids = run_main(shape, ids, counts, picked, near, far)

    def exchange(parts, axis, size, step):
        return [parts[0]] + [swap(x, axis, size, step * m) for m, x in enumerate(parts) if m]

    hd_got = swap(hd_send, "dev", devs, 1)
    src = functools.partial(run_src, (devs, local))
    early = blocks // 8
    s_acc = src(0, early, ids, resids, b_rows, picked, hd_send)[0]
    *hd, cut_done = run_cut(grps, hd_acc, hd_got, s_acc)
    cut_done = swap(cut_done, "dev", devs, 1)
    s_acc, *s_sends = src(early, blocks, ids, resids, b_rows, picked, cut_done, s_acc)
    s_got = [swap(x, "dev", devs, 1) for x in s_sends]
    hour_part = hour_rows // (2 * grps)
    s_keep, s_send = run_first_halve(s_acc, *s_got)
    hd = run_grp(hour_part, depth, exchange(hd, "grp", grps, 1), s_keep)
    hour_each = hour_part // depth
    s_got = swap(s_send, "dev", devs, 2)
    hd = exchange(hd, "dev", devs, 2)
    hour, dst, s_keep, s_send = run_z(hd, hour_each, s_keep, s_got)
    back = [hour] + [swap(hour, "dev", devs, 2 * m) for m in range(1, depth)]
    joined = run_join(back + [dst])[0]
    step = 4
    s_got = swap(s_send, "dev", devs, step)
    while 2 * step < devs:
        s_keep, s_send = run_halve(s_keep, s_got)
        step *= 2
        s_got = swap(s_send, "dev", devs, step)
    grad_src, same = run_src_sum(s_keep, s_got, joined)
    near = [joined] + [swap(joined, "grp", grps, m) for m in range(1, grps)]
    far = [swap(x, "dev", devs, 1) for x in [same] + near[1:]]
    grad_hour, grad_dst = run_place(sizes, hour_rows, near, 0, dst_part)
    grad_hour = run_place(sizes, hour_rows, far, 1, dst_part, grad_hour)[0]
    return grad_src, grad_dst, grad_hour


def solution(mesh):
    in_specs = (
        P(("grp", "dev"), None, None),
        P(("grp", "dev"), None),
        P("dev", None),
        P(),
        P(("grp", "dev"), None),
        P(("grp", "dev")),
        P(("grp", "dev"), None),
        P(("grp", "dev")),
        P(("grp", "dev")),
    )
    out_specs = (P(("grp", "dev"), None), P("dev", None), P())
    return jax.shard_map(
        functools.partial(per_device, mesh_sizes(mesh)),
        mesh=mesh,
        in_specs=in_specs,
        out_specs=out_specs,
        check_vma=False,
    )
```
